32 devices in a mesh: section: 4 (over x, core), dp: 8 (over z, y).
Axes of the slice: x: 2, y: 2, z: 4, core: 2. Of those that a mesh axis runs over, the one named last changes fastest.
Arguments:
- token_ids: int32 [2, 1024], P(None, 'dp'), may hold values from 0 to 31999
- noise: bfloat16 [2, 1024, 256], P(None, 'dp'), may hold values from -6 to 6
- noised: int32 [2, 1024], P(None, 'dp'), may hold values 0 or 1
- lengths: int32 [2, 8, 8], P(None, 'dp'), may hold values from 0 to 128, as said below
- step_index: int32 [2, 8, 8], P(None, 'dp'), may hold values from 0 to 199
- table: bfloat16 [32000, 256], P(('section', 'dp')), may hold values from -6 to 6
- in_proj: bfloat16 [256, 1024], replicated, may hold values from -0.375 to 0.375
- in_bias: bfloat16 [1024], replicated, may hold values from -3 to 3
- ln1_gain: bfloat16 [4, 1024], P('section'), may hold values from 0.5 to 1.5
- ln1_bias: bfloat16 [4, 1024], P('section'), may hold values from -1 to 1
- w_qkv: bfloat16 [4, 1024, 3072], P('section'), may hold values from -0.1875 to 0.1875
- w_out: bfloat16 [4, 1024, 1024], P('section'), may hold values from -0.75 to 0.75
- ln2_gain: bfloat16 [4, 1024], P('section'), may hold values from 0.5 to 1.5
- ln2_bias: bfloat16 [4, 1024], P('section'), may hold values from -1 to 1
- w_up: bfloat16 [4, 1024, 4096], P('section'), may hold values from -0.1875 to 0.1875
- w_down: bfloat16 [4, 4096, 1024], P('section'), may hold values from -0.09375 to 0.09375
- w_time: bfloat16 [4, 256, 1024], P('section'), may hold values from -0.375 to 0.375
- final_gain: bfloat16 [1024], replicated, may hold values from 0.5 to 1.5
- final_bias: bfloat16 [1024], replicated, may hold values from -1 to 1
- out_proj: bfloat16 [1024, 256], replicated, may hold values from -0.5 to 0.5
Outputs:
- loss: float32 [2, 8, 128], P(None, 'dp', 'section')
- grad_table: float32 [32000, 256], P(('section', 'dp'))
- grad_in_proj: float32 [256, 1024], P('section')
- grad_in_bias: float32 [1024], P('section')
- grad_ln1_gain: float32 [4, 1024], P('section', 'dp')
- grad_ln1_bias: float32 [4, 1024], P('section', 'dp')
- grad_w_qkv: float32 [4, 1024, 3072], P('section', 'dp')
- grad_w_out: float32 [4, 1024, 1024], P('section', 'dp')
- grad_ln2_gain: float32 [4, 1024], P('section', 'dp')
- grad_ln2_bias: float32 [4, 1024], P('section', 'dp')
- grad_w_up: float32 [4, 1024, 4096], P('section', 'dp')
- grad_w_down: float32 [4, 4096, 1024], P('section', 'dp')
- grad_w_time: float32 [4, 256, 1024], P('section', 'dp')
- grad_final_gain: float32 [1024], P('section')
- grad_final_bias: float32 [1024], P('section')
- grad_out_proj: float32 [1024, 256], P('section')
The draws below stay inside these ranges and needn't reach their ends.
Inputs may be any that keep to these rules, and one draw needn't show every extreme that they name: In each bucket the lengths sum to at most 128; slots after the last sequence are padding. In every micro-batch one bucket holds a single sequence of 128 tokens.
All inputs are finite; a program needn't handle non-finite values. No bound on the sum of `noised` on one device may be relied on, other than what follows from the above.
Results may differ from the reference program's by a relative error of at most 0.017.
Values may be sent and summed in bfloat16 or wider, within the bound.
A program may use at most 1 GiB of HBM per device.

```python
import math
import jax
import jax.numpy as jnp
import numpy as np
from jax import lax

D = 1024
HEADS = 16
FF = 4096
E = 256
V = 32000
TOK_DEV = 128
SEQS = 8
MICRO = 2
NOISE_STEPS = 200
HEAD_DIM = 64
LAYERS = 4
TOKENS_MB = 1024
N_DP = 8


def draw_lengths(key, part):
    key = jax.random.fold_in(key, 17)
    key_scale, key_drawn, key_whole = jax.random.split(key, 3)
    shape = (MICRO, N_DP, SEQS)
    power = jax.random.randint(key_scale, shape, 0, 9)
    ceiling = jnp.maximum(1, TOK_DEV * jnp.left_shift(jnp.ones(shape, jnp.int32), power) // 256)
    drawn = jax.random.randint(key_drawn, shape, 1, ceiling + 1)
    running = jnp.minimum(jnp.cumsum(drawn, axis=-1), TOK_DEV)
    before = jnp.concatenate([jnp.zeros((MICRO, N_DP, 1), jnp.int32), running[..., :-1]], axis=-1)
    spans = running - before
    chosen = jax.random.randint(key_whole, (MICRO,), 0, N_DP)
    whole = (jnp.arange(N_DP)[None, :] == chosen[:, None])[..., None]
    single = jnp.where(jnp.arange(SEQS) == 0, TOK_DEV, 0)
    return jnp.where(whole, single[None, None, :], spans).astype(jnp.int32)


def set_ends(values, own_key, low, high):
    longest = values.shape.index(max(values.shape))
    spots = []
    for shift in (0, 1):
        where = [jax.random.randint(jax.random.fold_in(own_key, axis), (), 0, length) for axis, length in enumerate(values.shape)]
        where[longest] = (where[longest] + shift) % values.shape[longest]
        spots.append(tuple(where))
    return values.at[spots[0]].set(low).at[spots[1]].set(high)


def block_scale(key, dims, pieces, low, high):
    level = 1.0
    for axis_at, shards_of in pieces:
        steps = jax.random.uniform(jax.random.fold_in(jax.random.fold_in(key, 6), axis_at), (shards_of,), jnp.float32, low / len(pieces), high / len(pieces))
        level = level * jnp.repeat(jnp.exp(steps), dims[axis_at] // shards_of).reshape((-1,) + (1,) * (len(dims) - 1 - axis_at))
    return level


def rank_bounds(count, lean):
    loads = [(1 << 20) // math.isqrt(standing ** lean) + 1 for standing in range(1, count + 1)]
    deviation = 1 + sum(loads) // (1 << 30)
    return np.cumsum(np.array([max(1, weight // deviation) for weight in loads]))


def ranked_ids(stream_key, extent, count, skew):
    table = rank_bounds(count, skew)
    lot = jax.random.randint(jax.random.fold_in(stream_key, 1), extent, 0, int(table[count - 1]))
    grade = jnp.searchsorted(jnp.asarray(table, jnp.int32), lot, side="right")
    return jax.random.permutation(jax.random.fold_in(stream_key, 2), count)[grade].astype(jnp.int32)


def centred(rng, shape, width, limit, cuts=(), held_as=jnp.bfloat16):
    level = block_scale(rng, shape, cuts, -0.22, 0.18) if cuts else 1.0
    result = jax.random.normal(rng, shape, jnp.float32) * width * level
    return jnp.minimum(jnp.maximum(result, -limit), limit).astype(held_as)


def setup_inputs(seed: int = 0) -> dict:
    streams_of = jax.random.split(jax.random.key(seed), 21)
    return {
        "token_ids": set_ends(ranked_ids(streams_of[0], (MICRO, TOKENS_MB), V, 2), jax.random.fold_in(streams_of[0], 3), 0, V - 1).astype(jnp.int32),
        "noise": centred(streams_of[1], (MICRO, TOKENS_MB, E), 1.0, 6.0, ((1, 8),)),
        "noised": set_ends((jax.random.randint(streams_of[2], (MICRO, TOKENS_MB), 0, 4) < 3).astype(jnp.int32), jax.random.fold_in(streams_of[2], 1), 0, 1),
        "lengths": draw_lengths(jax.random.fold_in(streams_of[20], 71), 0),
        "step_index": set_ends(jax.random.randint(streams_of[4], (MICRO, N_DP, SEQS), 0, NOISE_STEPS), jax.random.fold_in(streams_of[4], 1), 0, NOISE_STEPS - 1).astype(jnp.int32),
        "table": centred(streams_of[5], (V, E), 1.0, 6.0, ((0, 32),)),
        "in_proj": centred(streams_of[6], (E, D), E ** -0.5, 0.375),
        "in_bias": centred(streams_of[7], (D,), 0.5, 3.0),
        "ln1_gain": jnp.clip(1.0 + 0.1 * jax.random.normal(streams_of[8], (LAYERS, D), jnp.float32), 0.5, 1.5).astype(jnp.bfloat16),
        "ln1_bias": centred(streams_of[9], (LAYERS, D), 0.2, 1.0, ((0, 4),)),
        "w_qkv": centred(streams_of[10], (LAYERS, D, 3 * D), D ** -0.5, 0.1875, ((0, 4),)),
        "w_out": centred(streams_of[11], (LAYERS, D, D), (D // 16) ** -0.5, 0.75, ((0, 4),)),
        "ln2_gain": jnp.clip(1.0 + 0.1 * jax.random.normal(streams_of[12], (LAYERS, D), jnp.float32), 0.5, 1.5).astype(jnp.bfloat16),
        "ln2_bias": centred(streams_of[13], (LAYERS, D), 0.2, 1.0, ((0, 4),)),
        "w_up": centred(streams_of[14], (LAYERS, D, FF), D ** -0.5, 0.1875, ((0, 4),)),
        "w_down": centred(streams_of[15], (LAYERS, FF, D), FF ** -0.5, 0.09375, ((0, 4),)),
        "w_time": centred(streams_of[16], (LAYERS, E, D), E ** -0.5, 0.375, ((0, 4),)),
        "final_gain": jnp.clip(1.0 + 0.1 * jax.random.normal(streams_of[17], (D,), jnp.float32), 0.5, 1.5).astype(jnp.bfloat16),
        "final_bias": centred(streams_of[18], (D,), 0.2, 1.0),
        "out_proj": centred(streams_of[19], (D, E), (D // 8) ** -0.5, 0.5),
    }


norm_eps = 1e-05
mask_fill = -1e+30
sigma_low = 1.0
sigma_high = 300.0
rope_base = 10000.0

@jax.custom_vjp
def low(v):
    return lax.optimization_barrier(v.astype(jnp.bfloat16)).astype(jnp.float32)

@jax.custom_vjp
def low_back(v):
    return v

def low_keep(v):
    return (low(v), None)

def low_pass(kept, grad):
    return (grad,)

def back_keep(v):
    return (v, None)

def back_low(kept, grad):
    return (low(grad),)
low.defvjp(low_keep, low_pass)
low_back.defvjp(back_keep, back_low)

def dot_high(left, right):
    return jnp.dot(left, right, precision=lax.Precision.HIGHEST)

def layer_norm(values, gain, bias):
    center = values - lax.optimization_barrier(jnp.mean(values, axis=-1, keepdims=True))
    spread = lax.optimization_barrier(jnp.mean(center * center, axis=-1, keepdims=True))
    return center * lax.rsqrt(spread + norm_eps) * gain + bias

def rotate(vectors, cosine, sine):
    half = vectors.shape[-1] // 2
    first = vectors[..., :half]
    second = vectors[..., half:]
    cos_part = cosine[:, None, :]
    sin_part = sine[:, None, :]
    return jnp.concatenate([first * cos_part - second * sin_part, second * cos_part + first * sin_part], axis=-1)

def bucket_layout(lens, steps, tokens, embed, head_size, noise_steps):
    ends = jnp.cumsum(lens)
    starts = ends - lens
    place = jnp.arange(tokens, dtype=jnp.int32)
    member = (place[:, None] >= starts[None, :]) & (place[:, None] < ends[None, :])
    member_int = member.astype(jnp.int32)
    slots = lens.shape[0]
    inside = lax.optimization_barrier(jnp.sum(member_int, axis=1))
    segment = lax.optimization_barrier(jnp.sum(member_int * jnp.arange(slots, dtype=jnp.int32)[None, :], axis=1)) + (1 - inside) * slots
    offset = lax.optimization_barrier(jnp.sum(member_int * starts[None, :], axis=1)) + (1 - inside) * ends[-1]
    within = (place - offset).astype(jnp.float32)
    membership = member.astype(jnp.float32)
    sigma = sigma_low * (sigma_high / sigma_low) ** (steps.astype(jnp.float32) / (noise_steps - 1))
    level = lax.optimization_barrier(jnp.sum(membership * sigma[None, :], axis=1))
    half = embed // 2
    rates = 100.0 ** (jnp.arange(half).astype(jnp.float32) / half)
    phase = (jnp.log(sigma) * 0.25)[:, None] * rates[None, :]
    features = jnp.concatenate([jnp.cos(phase), jnp.sin(phase)], axis=1)
    quarter = head_size // 2
    inverse = rope_base ** (-(jnp.arange(quarter).astype(jnp.float32) * 2.0) / head_size)
    angles = within[:, None] * inverse[None, :]
    same_seq = segment[:, None] == segment[None, :]
    return (membership, same_seq, jnp.cos(angles), jnp.sin(angles), features, level, inside.astype(jnp.float32))

def bucket_loss(params, token_row, noise_row, noised_row, lens, steps):
    table, in_proj, in_bias, gain_one, bias_one, w_qkv, w_out, gain_two, bias_two, w_up, w_down, w_time, final_gain, final_bias, out_proj = params
    membership, same_seq, cosine, sine, features, level, inside = bucket_layout(lens, steps, TOK_DEV, E, HEAD_DIM, NOISE_STEPS)
    amount = noised_row.astype(jnp.float32) * level
    shrink = lax.rsqrt(1.0 + amount * amount)
    mixed = low((table[token_row] + amount[:, None] * noise_row) * shrink[:, None])
    hidden = low_back(dot_high(mixed, in_proj)) + in_bias
    time_low = low(features)
    scale = HEAD_DIM ** (-0.5)
    for layer in range(LAYERS):
        per_seq = low_back(dot_high(time_low, w_time[layer]))
        current = hidden + dot_high(membership, per_seq)
        normed = low(layer_norm(current, gain_one[layer], bias_one[layer]))
        packed = low_back(dot_high(normed, w_qkv[layer])).reshape(TOK_DEV, 3, HEADS, HEAD_DIM)
        queries = low(rotate(packed[:, 0], cosine, sine))
        keys = low(rotate(packed[:, 1], cosine, sine))
        values = low(packed[:, 2])
        scores = low_back(jnp.einsum('thd,shd->hts', queries, keys, precision=lax.Precision.HIGHEST) * scale)
        scores = jnp.where(same_seq[None], scores, mask_fill)
        probs = low(jax.nn.softmax(scores, axis=-1))
        attended = jnp.einsum('hts,shd->thd', probs, values, precision=lax.Precision.HIGHEST).reshape(TOK_DEV, D)
        attended = low(low_back(attended))
        after_attn = current + low_back(dot_high(attended, w_out[layer]))
        normed_mlp = low(layer_norm(after_attn, gain_two[layer], bias_two[layer]))
        pre_act = low_back(dot_high(normed_mlp, w_up[layer]))
        activated = low(jax.nn.gelu(pre_act, approximate=False))
        hidden = after_attn + low_back(dot_high(activated, w_down[layer]))
    final = low(layer_norm(hidden, final_gain, final_bias))
    latent = low(low_back(dot_high(final, out_proj)))
    logits = low_back(dot_high(latent, table.T) * E ** (-0.5))
    total = jax.nn.logsumexp(logits, axis=1)
    picked = jnp.take_along_axis(logits, token_row[:, None], axis=1)[:, 0]
    weight = noised_row.astype(jnp.float32) * inside / (MICRO * TOK_DEV)
    return weight * (total - picked)

def reference(token_ids, noise, noised, lengths, step_index, table, in_proj, in_bias, ln1_gain, ln1_bias, w_qkv, w_out, ln2_gain, ln2_bias, w_up, w_down, w_time, final_gain, final_bias, out_proj):
    params = tuple((item.astype(jnp.float32) for item in (table, in_proj, in_bias, ln1_gain, ln1_bias, w_qkv, w_out, ln2_gain, ln2_bias, w_up, w_down, w_time, final_gain, final_bias, out_proj)))
    buckets = MICRO * N_DP
    token_rows = token_ids.reshape(buckets, TOK_DEV)
    noise_rows = noise.astype(jnp.float32).reshape(buckets, TOK_DEV, E)
    noised_rows = noised.reshape(buckets, TOK_DEV)
    lens_rows = lengths.reshape(buckets, SEQS)
    step_rows = step_index.reshape(buckets, SEQS)

    def one_bucket(grad_sum, data):
        value, back = jax.vjp(lambda weights: bucket_loss(weights, *data), params)
        grads = back(jnp.ones_like(value))[0]
        return (jax.tree.map(jnp.add, grad_sum, grads), value)
    grads, losses = lax.scan(one_bucket, jax.tree.map(jnp.zeros_like, params), (token_rows, noise_rows, noised_rows, lens_rows, step_rows))
    loss = losses.reshape(MICRO, N_DP, TOK_DEV)
    return (loss, grads[0], grads[1], grads[2], grads[3], grads[4], grads[5], grads[6], grads[7], grads[8], grads[9], grads[10], grads[11], grads[12], grads[13], grads[14])
```

```python
from functools import partial
from typing import Any, NamedTuple

import jax
import jax.numpy as jnp
from jax import lax
from jax.experimental import pallas as pl
from jax.experimental.pallas import tpu as pltpu
from jax.sharding import PartitionSpec as P

HEADS = 16
NOISE_STEPS = 200
SECTION = "section"
DP = "dp"
MESH = pl.DeviceIdType.MESH
VMEM_BYTES = 62 * 1024 * 1024
FF_CHUNK = 512
PACK_CHUNK = 512
ROW_CHUNK = 1024
LANES = 128
ACROSS = 2

norm_eps = 1e-05
mask_fill = -1e30
sigma_low = 1.0
sigma_high = 300.0
rope_base = 10000.0


def layer_norm(values, gain, bias):
    center = values - jnp.mean(values, axis=-1, keepdims=True)
    spread = jnp.mean(center * center, axis=-1, keepdims=True)
    return center * lax.rsqrt(spread + norm_eps) * gain + bias


def gelu_exact(values):
    return jax.nn.gelu(values, approximate=False)


def rotate(vectors, cosine, sine):
    half = vectors.shape[-1] // 2
    first = vectors[..., :half]
    second = vectors[..., half:]
    cos_part = cosine[:, None, :]
    sin_part = sine[:, None, :]
    return jnp.concatenate(
        [first * cos_part - second * sin_part, second * cos_part + first * sin_part], axis=-1
    )


def rotate_back(grads, cosine, sine):
    half = grads.shape[-1] // 2
    first = grads[..., :half]
    second = grads[..., half:]
    cos_part = cosine[:, None, :]
    sin_part = sine[:, None, :]
    return jnp.concatenate(
        [first * cos_part + second * sin_part, second * cos_part - first * sin_part], axis=-1
    )


def bucket_layout(lens, steps, tokens, embed, head_size, noise_steps):
    ends = jnp.cumsum(lens)
    starts = ends - lens
    place = jnp.arange(tokens, dtype=jnp.int32)
    member = (place[:, None] >= starts[None, :]) & (place[:, None] < ends[None, :])
    member_int = member.astype(jnp.int32)
    slots = lens.shape[0]
    inside = jnp.sum(member_int, axis=1)
    segment = (
        jnp.sum(member_int * jnp.arange(slots, dtype=jnp.int32)[None, :], axis=1)
        + (1 - inside) * slots
    )
    offset = jnp.sum(member_int * starts[None, :], axis=1) + (1 - inside) * ends[-1]
    within = (place - offset).astype(jnp.float32)
    membership = member.astype(jnp.float32)
    sigma = sigma_low * (sigma_high / sigma_low) ** (steps.astype(jnp.float32) / (noise_steps - 1))
    level = jnp.sum(membership * sigma[None, :], axis=1)
    half = embed // 2
    rates = 100.0 ** (jnp.arange(half).astype(jnp.float32) / half)
    phase = (jnp.log(sigma) * 0.25)[:, None] * rates[None, :]
    features = jnp.concatenate([jnp.cos(phase), jnp.sin(phase)], axis=1)
    quarter = head_size // 2
    inverse = rope_base ** (-(jnp.arange(quarter).astype(jnp.float32) * 2.0) / head_size)
    angles = within[:, None] * inverse[None, :]
    same_seq = segment[:, None] == segment[None, :]
    return (
        membership,
        same_seq,
        jnp.cos(angles),
        jnp.sin(angles),
        features,
        level,
        inside.astype(jnp.float32),
    )


def embed_input(full_table, token_row, noise_row, noised_row, level):
    rows = full_table[token_row].astype(jnp.float32)
    amount = noised_row.astype(jnp.float32) * level
    shrink = lax.rsqrt(1.0 + amount * amount)
    mixed = (rows + amount[:, None] * noise_row.astype(jnp.float32)) * shrink[:, None]
    return (mixed.astype(jnp.bfloat16), shrink)


def normal(values):
    center = values - jnp.mean(values, axis=-1, keepdims=True)
    spread = jnp.mean(center * center, axis=-1, keepdims=True)
    inverse = lax.rsqrt(spread + norm_eps)
    return (center * inverse, inverse)


def normal_back(grads, gain, unit, inverse):
    scaled = grads * gain
    first = jnp.mean(scaled, axis=-1, keepdims=True)
    second = jnp.mean(scaled * unit, axis=-1, keepdims=True)
    return inverse * (scaled - first - unit * second)


def dot(left, right):
    return lax.dot_general(
        left, right, (((1,), (0,)), ((), ())), preferred_element_type=jnp.float32
    )


def dot_right(left, right):
    return lax.dot_general(
        left, right, (((1,), (1,)), ((), ())), preferred_element_type=jnp.float32
    )


def dot_left(left, right):
    return lax.dot_general(
        left, right, (((0,), (0,)), ((), ())), preferred_element_type=jnp.float32
    )


def halves_swapped(values, head_size, lane):
    half = head_size // 2
    size = values.shape[-1]
    ahead = pltpu.roll(values, size - half, 1)
    behind = pltpu.roll(values, half, 1)
    return jnp.where(lane % head_size < half, ahead, behind)


def apart(pair, lane, head_size):
    zero = jnp.zeros_like(pair)
    return jnp.concatenate(
        [jnp.where(lane < head_size, pair, zero), jnp.where(lane < head_size, zero, pair)], axis=0
    )


NORMED, MLP, BRANCH, ATTN, LATENT, LOG_TOTAL, MIXED_GRAD, NORM_ROWS, SEQ_ROWS, FEATURES = range(10)
WIDE, PER_SLOT, BLOCKS = 4, 7, 10


class Sources(NamedTuple):
    table: Any
    qkv: Any
    out: Any
    up: Any
    down: Any


class Given(NamedTuple):
    ints: Any
    noise: Any
    amount: Any
    norms: Any
    timed: Any
    cosine: Any
    sine: Any
    mask: Any
    member: Any
    features: Any
    padding: Any
    out_proj: Any
    in_proj: Any
    weight: Any
    shrink: Any


class Kept(NamedTuple):
    table: Any
    qkv: Any
    out: Any
    up: Any
    down: Any
    part: Any
    ints: Any
    rows_parts: Any
    rows: Any
    mixed: Any
    other: Any
    mine: Any
    mine_stats: Any
    arrived: Any
    final: Any
    final_low: Any
    raw: Any
    narrow: Any
    grad_packed: Any
    current: Any
    after: Any
    packed: Any
    probs: Any
    slope: Any
    leaving: Any
    returned: Any
    upstream: Any
    stats: Any
    pulled: Any
    grad_latent: Any
    seq: Any
    end_rows: Any
    end_parts: Any
    end_own: Any
    start_row: Any
    start_parts: Any
    start_own: Any


class Signals(NamedTuple):
    load: Any
    keep: Any
    out: Any
    line: Any
    beside: Any
    pair: Any
    relay: Any
    ints_send: Any
    ints_recv: Any
    rows_send: Any
    rows_recv: Any
    parts_send: Any
    parts_recv: Any
    table_send: Any
    table_recv: Any
    other_send: Any
    other_recv: Any
    log_send: Any
    log_recv: Any
    on_send: Any
    on_recv: Any
    back_send: Any
    back_recv: Any
    latent_send: Any
    latent_recv: Any
    stats_send: Any
    stats_recv: Any
    pulled_send: Any
    pulled_recv: Any
    end_send: Any
    end_recv: Any
    start_send: Any
    start_recv: Any
    mixed_send: Any
    mixed_recv: Any
    ends: Any


def chain_kernel(sections, groups, heights, *refs):
    refs = iter(refs)
    sources, given = (kind(*(next(refs) for _ in kind._fields)) for kind in (Sources, Given))
    boards = [next(refs) for _ in range(BLOCKS)]
    end_out, start_out, ints_out, loss_out, branch_out, attn_out = (next(refs) for _ in range(6))
    own = [next(refs) for _ in range(BLOCKS)]
    r, sems = (kind(*(next(refs) for _ in kind._fields)) for kind in (Kept, Signals))
    section = lax.axis_index(SECTION)
    group = lax.axis_index(DP)
    last = sections - 1
    along, beside, line = groups // ACROSS, lax.rem(group, ACROSS), group // ACROSS
    partner = line * ACROSS + (1 - beside)
    micro, tokens, width = r.arrived.shape
    inner = r.up.shape[1]
    embed = r.part.shape[2]
    slots = given.member.shape[1]
    height, padded = heights
    head_size = width // HEADS
    scale = head_size ** (-0.5)
    logit_scale = embed ** (-0.5)
    pair = 2 * head_size
    lane = lax.broadcasted_iota(jnp.int32, (tokens, pair), 1)
    low = jnp.bfloat16

    loads = [
        pltpu.make_async_copy(source, target, sems.load.at[index])
        for index, (source, target) in enumerate(
            zip(sources, (r.table, r.qkv, r.out, r.up, r.down))
        )
    ]
    load_table, load_qkv, load_out, load_up, load_down = loads
    for load in (load_table, load_qkv, load_out):
        load.start()

    def section_peer(step):
        return lax.rem(section + step, sections)

    def line_peer(step):
        return lax.rem(line + step, along)

    def group_peer(step):
        return lax.rem(group + step, groups)

    barrier = pltpu.get_barrier_semaphore()
    for step in range(1, sections):
        pl.semaphore_signal(
            barrier, inc=1, device_id={SECTION: section_peer(step)}, device_id_type=MESH
        )
    for step in range(1, groups):
        pl.semaphore_signal(
            barrier, inc=1, device_id={DP: group_peer(step)}, device_id_type=MESH
        )
    for step in range(1, sections):
        pl.semaphore_signal(
            barrier,
            inc=1,
            device_id={SECTION: section_peer(step), DP: partner},
            device_id_type=MESH,
        )
    pl.semaphore_wait(barrier, 2 * sections + groups - 3)

    def sent(source, target, to, send_sem, recv_sem, axis=SECTION):
        return pltpu.make_async_remote_copy(
            src_ref=source,
            dst_ref=target,
            send_sem=send_sem,
            recv_sem=recv_sem,
            device_id={axis: to},
            device_id_type=MESH,
        )

    def place(name, slot):
        board = boards[name]
        if name < PER_SLOT:
            index, mine = name * micro + slot, own[name].at[slot]
        else:
            index, mine = PER_SLOT * micro + name - PER_SLOT, own[name]
        if name < WIDE:
            return index, mine, lambda at: board.at[at, slot]
        if name < PER_SLOT:
            return index, mine, lambda at: board.at[at, beside, slot]
        return index, mine, lambda at: board.at[at, beside]

    relayed = along == 4
    count = PER_SLOT * micro + BLOCKS - PER_SLOT
    early = section < sections // 2
    at_end = (line == 0) | (line == along - 1)

    def slots_of(name):
        if name in (BRANCH, ATTN):
            return micro - 1
        return micro if name < PER_SLOT else 1

    def spread(name, slot=0):
        index, mine, at = place(name, slot)
        here = at(line)
        pltpu.make_async_copy(mine, here, sems.keep.at[index]).start()
        for step in range(1, along):
            peer = line_peer(step)
            to = peer * ACROSS + beside
            if name < WIDE and relayed:
                far = (at_end & (jnp.abs(line - peer) == 2)).astype(jnp.int32)

                @pl.when(jnp.abs(line - peer) < 3)
                def _():
                    arrival = sems.line.at[far * count + index]
                    sent(mine, here, to, sems.out.at[index], arrival, DP).start()

            else:
                sent(mine, here, to, sems.out.at[index], sems.line.at[index], DP).start()
        if name >= WIDE:
            sent(mine, here, partner, sems.out.at[index], sems.pair.at[index], DP).start()

    def relay_copy(name, slot):
        index, mine, at = place(name, slot)
        there = at(jnp.where(line == 1, along - 1, 0))
        to = jnp.where(line == 1, 0, along - 1) * ACROSS + beside
        return sent(there, there, to, sems.relay.at[index], sems.line.at[index], DP)

    def relay(name, slot):
        if relayed:
            index, mine, at = place(name, slot)

            @pl.when(jnp.logical_not(at_end))
            def _():
                wait_blocks(at(pl.ds(0, 1)), sems.line.at[count + index])
                relay_copy(name, slot).start()

    def wait_blocks(ref, sem):
        pltpu.make_async_copy(ref, ref, sem).wait()

    def forward(name, slot=0):
        index, mine, at = place(name, slot)
        wait_blocks(at(pl.ds(0, along - 1)), sems.line.at[index])
        for step in range(1, along):
            there = at(line_peer(step))
            sent(there, there, partner, sems.beside.at[index], sems.pair.at[index], DP).start()

    def settle(name, slot=0):
        index, mine, at = place(name, slot)
        pltpu.make_async_copy(mine, at(line), sems.keep.at[index]).wait()
        if name < WIDE and relayed:

            @pl.when(at_end)
            def _():
                wait_blocks(at(pl.ds(0, 2)), sems.out.at[index])
                wait_blocks(at(pl.ds(0, 3)), sems.line.at[index])

            @pl.when(jnp.logical_not(at_end))
            def _():
                wait_blocks(at(pl.ds(0, 3)), sems.out.at[index])
                wait_blocks(at(pl.ds(0, 2)), sems.line.at[index])
                relay_copy(name, slot).wait_send()

        elif name < WIDE:
            wait_blocks(at(pl.ds(0, along - 1)), sems.out.at[index])
            wait_blocks(at(pl.ds(0, along - 1)), sems.line.at[index])
        else:
            wait_blocks(at(pl.ds(0, along)), sems.out.at[index])
            wait_blocks(at(pl.ds(0, along - 1)), sems.beside.at[index])
            wait_blocks(at(pl.ds(0, along)), sems.pair.at[index])

    def passed_on(slot):
        to = jnp.minimum(section + 1, last)
        return sent(
            r.final.at[slot],
            r.arrived.at[slot],
            to,
            sems.on_send.at[slot],
            sems.on_recv.at[slot],
        )

    def passed_back(slot):
        to = jnp.maximum(section - 1, 0)
        return sent(
            r.leaving.at[slot],
            r.returned.at[slot],
            to,
            sems.back_send.at[slot],
            sems.back_recv.at[slot],
        )

    def to_head(source, target, section_to, group_to, send_sem, recv_sem):
        return pltpu.make_async_remote_copy(
            src_ref=source,
            dst_ref=target,
            send_sem=send_sem,
            recv_sem=recv_sem,
            device_id={SECTION: section_to, DP: group_to},
            device_id_type=MESH,
        )

    me = section * ACROSS + beside

    def latent_to(slot, step):
        ref = own[LATENT].at[slot]
        sem = sems.latent_send.at[slot * sections + step]
        return sent(ref, ref, section_peer(step), sem, sems.latent_recv.at[slot])

    def latent_over(slot, step):
        sem = sems.other_send.at[slot * sections + step]
        return to_head(
            own[LATENT].at[slot],
            r.other.at[slot],
            section_peer(step),
            partner,
            sem,
            sems.other_recv.at[slot],
        )

    def shares_to(slot, side):
        to = partner if side else group
        sem = slot * ACROSS + side
        return (
            to_head(
                r.mine.at[side, slot],
                r.pulled.at[me, slot],
                last,
                to,
                sems.pulled_send.at[sem],
                sems.pulled_recv.at[slot * ACROSS * sections + me],
            ),
            to_head(
                r.mine_stats.at[side, slot],
                r.stats.at[me, slot],
                last,
                to,
                sems.stats_send.at[sem],
                sems.stats_recv.at[slot * ACROSS * sections + me],
            ),
        )

    def shares_from(slot, source):
        sem = slot * ACROSS * sections + source
        return tuple(
            to_head(store.at[source, slot], store.at[source, slot], last, partner, send, recv)
            for store, send, recv in (
                (r.pulled, sems.pulled_send.at[slot], sems.pulled_recv.at[sem]),
                (r.stats, sems.stats_send.at[slot], sems.stats_recv.at[sem]),
            )
        )

    def log_to(slot, step):
        ref = own[LOG_TOTAL].at[slot]
        sem = sems.log_send.at[slot * sections + step]
        return sent(ref, ref, section_peer(step), sem, sems.log_recv.at[slot])

    def end_to(step):
        to = section_peer(step)
        return sent(
            r.end_parts.at[to], r.end_own, to, sems.end_send.at[step], sems.end_recv
        )

    def start_to(step):
        to = section_peer(step)
        return sent(
            r.start_parts.at[to], r.start_own, to, sems.start_send.at[step], sems.start_recv
        )

    def mixed_to(slot, step):
        ref = own[MIXED_GRAD].at[slot]
        return sent(
            ref,
            ref,
            section_peer(step),
            sems.mixed_send.at[slot * sections + step],
            sems.mixed_recv.at[slot],
        )

    def ints_to(step):
        ref = r.ints.at[group]
        return sent(
            ref, ref, group_peer(step), sems.ints_send.at[step], sems.ints_recv.at[group], DP
        )

    def ints_from(step):
        source = group_peer(step)
        ref = r.ints.at[source]
        return sent(ref, ref, source, sems.ints_send.at[step], sems.ints_recv.at[source], DP)

    def leaving_rows(peer, stage):
        at = stage * along + peer
        high = r.up.shape[0] // (micro * tokens)
        first = pl.multiple_of(lax.rem(at, high) * (micro * tokens), micro * tokens)
        column = pl.multiple_of(at // high * embed, embed)
        return r.up.at[pl.ds(first, micro * tokens), pl.ds(column, embed)]

    def arriving_rows(peer, stage):
        at = stage * along + peer
        wide = r.down.shape[1] // embed
        first = pl.multiple_of(at // wide * (micro * tokens), micro * tokens)
        column = pl.multiple_of(lax.rem(at, wide) * embed, embed)
        return r.down.at[pl.ds(first, micro * tokens), pl.ds(column, embed)]

    def rows_across(step):
        peer = line_peer(step)
        return sent(
            leaving_rows(peer, 0),
            arriving_rows(peer, 0),
            partner,
            sems.rows_send.at[step],
            sems.rows_recv.at[peer],
            DP,
        )

    def rows_along(step):
        peer = line_peer(step)
        return sent(
            leaving_rows(peer, 1),
            arriving_rows(line, 1),
            peer * ACROSS + beside,
            sems.rows_send.at[along + step],
            sems.rows_recv.at[along + line],
            DP,
        )

    def rows_from(step):
        source = line_peer(step)
        ref = arriving_rows(source, 1)
        sem = along + source
        return sent(ref, ref, partner, sems.rows_send.at[sem], sems.rows_recv.at[sem], DP)

    def parts_to(step):
        ref = r.rows_parts.at[section]
        return sent(
            ref, ref, section_peer(step), sems.parts_send.at[step], sems.parts_recv.at[section]
        )

    def parts_from(step):
        source = section_peer(step)
        ref = r.rows_parts.at[source]
        return sent(ref, ref, source, sems.parts_send.at[step], sems.parts_recv.at[source])

    def table_to(step):
        to = line_peer(step) * ACROSS + beside
        return sent(
            r.table, r.part.at[line], to, sems.table_send.at[step], sems.table_recv.at[line], DP
        )

    def table_settle():
        for step in range(1, along):
            peer = line_peer(step)
            ref = r.part.at[peer]
            sent(
                ref, ref, partner, sems.table_send.at[step], sems.table_recv.at[peer], DP
            ).wait_recv()

    def looked_up(owner):
        ids = r.ints[owner]
        base = (section * groups + group) * height
        column = lax.broadcasted_iota(jnp.int32, (micro * tokens, padded), 1)
        spots = []
        for slot in range(micro):
            wide = jnp.broadcast_to(ids[slot : slot + 1, :tokens], (tokens, tokens))
            spots.append(jnp.transpose(wide.astype(jnp.float32))[:, 0:1])
        at = jnp.concatenate(spots, axis=0).astype(jnp.int32) - base
        at = jnp.where(at < height, at, -1)
        hit = (column == at).astype(jnp.float32).astype(low)
        return dot(hit, r.table[...]).astype(low)

    def front():
        r.ints[group] = given.ints[...]
        for step in range(1, groups):
            ints_to(step).start()
        load_table.wait()
        steps = [*range(1, along), 0]
        for step in range(1, groups):
            ints_from(step).wait_recv()
        for step in steps:
            peer = line_peer(step)
            leaving_rows(peer, 0)[...] = looked_up(peer * ACROSS + (1 - beside))
            rows_across(step).start()
            leaving_rows(peer, 1)[...] = looked_up(peer * ACROSS + beside)
        for step in steps:
            peer = line_peer(step)
            rows_across(step).wait_recv()
            both = leaving_rows(peer, 1)[...].astype(jnp.float32)
            both = both + arriving_rows(peer, 0)[...].astype(jnp.float32)
            if step:
                leaving_rows(peer, 1)[...] = both.astype(low)
                rows_along(step).start()
        total = both
        for step in range(1, along):
            rows_from(step).wait_recv()
            total = total + arriving_rows(line_peer(step), 1)[...].astype(jnp.float32)
        load_down.start()
        r.rows_parts[section] = total.astype(low)
        for step in range(1, sections):
            parts_to(step).start()
        for step in steps:
            rows_across(step).wait_send()
            if step:
                rows_along(step).wait_send()
        load_up.start()
        for step in range(1, along):
            table_to(step).start()
        r.part[line] = r.table[...]
        for step in range(1, sections):
            parts_from(step).wait_recv()
            total = total + r.rows_parts[section_peer(step)].astype(jnp.float32)
        r.rows[...] = total.astype(low).reshape(micro, tokens, embed)

        @pl.when(section == 0)
        def _():
            for slot in range(micro):
                rows = r.rows[slot].astype(jnp.float32)
                mixed = rows + given.amount[slot] * given.noise[slot].astype(jnp.float32)
                mixed = (mixed * given.shrink[slot]).astype(low)
                r.mixed[slot] = mixed
                r.arrived[slot] = dot(mixed, given.in_proj[...]) + given.norms[6:7]

    def layer_on(slot):
        @pl.when(section > 0)
        def _():
            passed_on(slot).wait_recv()

        current = r.arrived[slot] + given.timed[slot]
        r.current[slot] = current
        normed = (normal(current)[0] * given.norms[0:1] + given.norms[1:2]).astype(low)
        own[NORMED][slot] = normed
        if slot == 0:
            load_qkv.wait()
        for at in range(0, 3 * width, PACK_CHUNK):
            r.raw[:, at : at + PACK_CHUNK] = dot(normed, r.qkv[:, at : at + PACK_CHUNK])

        @pl.when(jnp.logical_not(early))
        def _():
            spread(NORMED, slot)

        for at in range(0, width, pair):
            turned = []
            for kind in range(2):
                raw = r.raw[:, kind * width + at : kind * width + at + pair]
                raw = raw * given.cosine[slot] + halves_swapped(raw, head_size, lane) * given.sine[slot]
                raw = raw.astype(low)
                r.packed[slot, :, kind * width + at : kind * width + at + pair] = raw
                turned.append(raw)
            values = r.raw[:, 2 * width + at : 2 * width + at + pair].astype(low)
            r.packed[slot, :, 2 * width + at : 2 * width + at + pair] = values
            scores = dot_right(turned[0], apart(turned[1], lane, head_size)) * scale
            sides = []
            for side in range(2):
                part = scores[:, side * tokens : (side + 1) * tokens] + given.mask[slot]
                raised = jnp.exp(part - jnp.max(part, axis=-1, keepdims=True))
                sides.append(raised / jnp.sum(raised, axis=-1, keepdims=True))
            probs = jnp.concatenate(sides, axis=1)
            r.probs[slot, at // pair] = probs
            r.narrow[:, at : at + pair] = dot(
                probs.astype(low), apart(values, lane, head_size)
            ).astype(low)
        if slot == 0:
            load_out.wait()
        after = current + dot(r.narrow[...], r.out[...])
        r.after[slot] = after
        normed_mlp = (normal(after)[0] * given.norms[2:3] + given.norms[3:4]).astype(low)
        own[MLP][slot] = normed_mlp

        @pl.when(jnp.logical_not(early))
        def _():
            spread(MLP, slot)

        if slot == 0:
            load_up.wait()
            load_down.wait()
        total = after
        for at in range(0, inner, FF_CHUNK):
            pre_act = dot(normed_mlp, r.up[:, at : at + FF_CHUNK])
            below = 0.5 + 0.5 * lax.erf(pre_act * 0.5**0.5)
            bell = jnp.exp(-0.5 * pre_act * pre_act) * (0.5 / jnp.pi) ** 0.5
            r.slope[slot, :, at : at + FF_CHUNK] = below + pre_act * bell
            activated = (pre_act * below).astype(low)
            total = total + dot(activated, r.down[at : at + FF_CHUNK, :])
        r.final[slot] = total

        @pl.when(section < last)
        def _():
            passed_on(slot).start()

        @pl.when(section == last)
        def _():
            final = (normal(total)[0] * given.norms[4:5] + given.norms[5:6]).astype(low)
            r.final_low[slot] = final
            own[LATENT][slot] = dot(final, given.out_proj[...]).astype(low)
            for step in range(sections):
                if step:
                    latent_to(slot, step).start()
                latent_over(slot, step).start()

    def vocabulary(slot):
        @pl.when(section < last)
        def _():
            latent_to(slot, 1).wait_recv()

        latent_over(slot, 1).wait_recv()
        both = jnp.concatenate([own[LATENT][slot], r.other[slot]], axis=0)
        top = jnp.full((ACROSS * tokens, 1), mask_fill, jnp.float32)
        mass = jnp.zeros((ACROSS * tokens, 1), jnp.float32)
        pulled = jnp.zeros((ACROSS * tokens, embed), jnp.float32)
        shards = ROW_CHUNK // padded
        for at in range(0, along, shards):
            rows = r.part[at : at + shards].reshape(ROW_CHUNK, embed)
            logits = dot_right(both, rows) * logit_scale + given.padding[0:1]
            best = jnp.maximum(top, jnp.max(logits, axis=-1, keepdims=True))
            raised = jnp.exp(logits - best)
            fade = jnp.exp(top - best)
            mass = mass * fade + jnp.sum(raised, axis=-1, keepdims=True)
            pulled = pulled * fade + dot(raised.astype(low), rows)
            top = best
        for side in range(ACROSS):
            rows = slice(side * tokens, (side + 1) * tokens)
            r.mine[side, slot] = pulled[rows].astype(low)
            r.mine_stats[side, slot] = jnp.where(lane < LANES // 2, top[rows], mass[rows])
        for copy in shares_to(slot, 1):
            copy.start()

        @pl.when(section < last)
        def _():
            for copy in shares_to(slot, 0):
                copy.start()

    def combine(slot):
        @pl.when(section == last)
        def _():
            sources = [lax.rem(me + step, ACROSS * sections) for step in range(1, ACROSS * sections)]
            for source in sources:
                for copy in shares_from(slot, source):
                    copy.wait_recv()
            stats = [r.mine_stats[0, slot]] + [r.stats[source, slot] for source in sources]
            best = stats[0][:, 0:1]
            for item in stats[1:]:
                best = jnp.maximum(best, item[:, 0:1])
            shares = [jnp.exp(item[:, 0:1] - best) for item in stats]
            total = sum(
                share * item[:, LANES // 2 : LANES // 2 + 1] for share, item in zip(shares, stats)
            )
            pulled = [r.mine[0, slot]] + [r.pulled[source, slot] for source in sources]
            mean = sum(
                share / total * item.astype(jnp.float32) for share, item in zip(shares, pulled)
            )
            row = r.rows[slot].astype(jnp.float32)
            grad_latent = ((mean - row) * (logit_scale * given.weight[slot])).astype(low)
            r.grad_latent[slot] = grad_latent
            grads = dot_right(grad_latent, given.out_proj[...])
            unit, inverse = normal(r.final[slot])
            r.upstream[...] = normal_back(grads, given.norms[4:5], unit, inverse)
            gain = jnp.sum(grads * unit, axis=0, keepdims=True)
            bias = jnp.sum(grads, axis=0, keepdims=True)
            if slot == 0:
                r.end_rows[0:1] = gain
                r.end_rows[1:2] = bias
            else:
                r.end_rows[0:1] += gain
                r.end_rows[1:2] += bias
            log_total = best + jnp.log(total)
            picked = own[LATENT][slot].astype(jnp.float32) * row
            picked = jnp.sum(picked, axis=-1, keepdims=True) * logit_scale
            loss = given.weight[slot] * (log_total - picked)
            turned = jnp.transpose(jnp.where(lane < LANES // 2, log_total, loss))
            own[LOG_TOTAL][slot, 0:4] = turned[0:4]
            own[LOG_TOTAL][slot, 4:8] = turned[LANES // 2 : LANES // 2 + 4]
            for step in range(1, sections):
                log_to(slot, step).start()

        @pl.when(section < last)
        def _():
            passed_back(slot).wait_recv()
            r.upstream[...] = r.returned[slot].astype(jnp.float32)

    def together(rows):
        return jnp.where(lane < head_size, rows[:tokens], rows[tokens:])

    def turned_back(grads, slot):
        return grads * given.cosine[slot] - halves_swapped(grads, head_size, lane) * given.sine[slot]

    def layer_back(slot):
        upstream = r.upstream[...]
        branch = upstream.astype(low)
        own[BRANCH][slot] = branch
        if slot < micro - 1:
            spread(BRANCH, slot)
        grads = jnp.zeros((tokens, width), jnp.float32)
        for at in range(0, inner, FF_CHUNK):
            grad_act = dot_right(branch, r.down[at : at + FF_CHUNK, :])
            grad_pre = (r.slope[slot, :, at : at + FF_CHUNK] * grad_act).astype(low)
            grads = grads + dot_right(grad_pre, r.up[:, at : at + FF_CHUNK])
        unit, inverse = normal(r.after[slot])
        gain_two = jnp.sum(grads * unit, axis=0, keepdims=True)
        bias_two = jnp.sum(grads, axis=0, keepdims=True)
        grad_after = upstream + normal_back(grads, given.norms[2:3], unit, inverse)
        attn_branch = grad_after.astype(low)
        own[ATTN][slot] = attn_branch
        if slot < micro - 1:
            spread(ATTN, slot)
        r.narrow[...] = dot_right(attn_branch, r.out[...]).astype(low)
        for at in range(0, width, pair):
            queries = r.packed[slot, :, at : at + pair]
            keys = r.packed[slot, :, width + at : width + at + pair]
            values = r.packed[slot, :, 2 * width + at : 2 * width + at + pair]
            grad_here = r.narrow[:, at : at + pair]
            probs = r.probs[slot, at // pair]
            grad_prob = dot_right(grad_here, apart(values, lane, head_size))
            sides = []
            for side in range(2):
                here = probs[:, side * tokens : (side + 1) * tokens]
                there = grad_prob[:, side * tokens : (side + 1) * tokens]
                mean = jnp.sum(here * there, axis=-1, keepdims=True)
                sides.append(here * (there - mean))
            grad_score = jnp.concatenate(sides, axis=1).astype(low)
            grad_query = dot(grad_score, apart(keys, lane, head_size)) * scale
            grad_key = together(dot_left(grad_score, queries)) * scale
            grad_value = together(dot_left(probs.astype(low), grad_here))
            for kind, grad in enumerate(
                (turned_back(grad_query, slot), turned_back(grad_key, slot), grad_value)
            ):
                r.grad_packed[:, kind * width + at : kind * width + at + pair] = grad.astype(low)
        grads = jnp.zeros((tokens, width), jnp.float32)
        for at in range(0, 3 * width, PACK_CHUNK):
            grads = grads + dot_right(
                r.grad_packed[:, at : at + PACK_CHUNK], r.qkv[:, at : at + PACK_CHUNK]
            )
        unit, inverse = normal(r.current[slot])
        gain_one = jnp.sum(grads * unit, axis=0, keepdims=True)
        bias_one = jnp.sum(grads, axis=0, keepdims=True)
        grad_current = grad_after + normal_back(grads, given.norms[0:1], unit, inverse)
        leaving = grad_current.astype(low)
        r.leaving[slot] = leaving

        @pl.when(section > 0)
        def _():
            passed_back(slot).start()

        r.seq[slot * slots : (slot + 1) * slots] = lax.dot_general(
            given.member[slot],
            grad_current,
            (((1,), (0,)), ((), ())),
            precision=lax.Precision.HIGHEST,
            preferred_element_type=jnp.float32,
        )
        for index, row in enumerate((gain_one, bias_one, gain_two, bias_two)):
            if slot == 0:
                own[NORM_ROWS][index : index + 1] = row
            else:
                own[NORM_ROWS][index : index + 1] += row

        @pl.when(section == 0)
        def _():
            moved = dot_right(leaving, given.in_proj[...]) * given.shrink[slot]
            own[MIXED_GRAD][slot] = moved.astype(low)
            for step in range(1, sections):
                mixed_to(slot, step).start()
            column = jnp.sum(grad_current, axis=0, keepdims=True)
            if slot == 0:
                r.start_row[...] = column
            else:
                r.start_row[...] += column

    own[NORM_ROWS][...] = jnp.zeros_like(own[NORM_ROWS])
    r.seq[...] = jnp.zeros_like(r.seq)
    r.end_rows[...] = jnp.zeros_like(r.end_rows)
    own[FEATURES][...] = given.features[...]
    front()
    spread(FEATURES)

    layer_on(0)
    for slot in range(1, micro):
        layer_on(slot)

    def spread_all(*names):
        for name in names:
            for slot in range(slots_of(name)):
                spread(name, slot)

    def relay_all(*names):
        for name in names:
            for slot in range(slots_of(name)):
                relay(name, slot)

    @pl.when(early)
    def _():
        spread_all(NORMED, MLP)

    table_settle()
    vocabulary(0)

    @pl.when(section < last)
    def _():
        for slot in range(1, micro):
            vocabulary(slot)

    @pl.when(early)
    def _():
        relay_all(NORMED)

    for slot in range(micro):
        if slot > 0:

            @pl.when(section == last)
            def _():
                vocabulary(slot)

        combine(slot)
        spread(LATENT, slot)
        layer_back(slot)

        @pl.when(section < last)
        def _():
            log_to(slot, 1).wait_recv()

        spread(LOG_TOTAL, slot)
        if slot == 0:

            @pl.when(early)
            def _():
                relay_all(MLP)

    @pl.when(jnp.logical_not(early))
    def _():
        relay_all(NORMED, MLP)

    @pl.when(section == last)
    def _():
        grads = sum(dot_left(r.final_low[slot], r.grad_latent[slot]) for slot in range(micro))
        tall = width // sections
        r.end_parts[...] = jnp.zeros_like(r.end_parts)
        for to in range(sections):
            r.end_parts[to, :tall, :] = grads[to * tall : (to + 1) * tall].astype(low)
            rows = r.end_rows[:, to * tall : (to + 1) * tall]
            r.end_parts[to, tall : tall + 8, :embed] = rows[:, :embed].astype(low)
        for step in range(1, sections):
            end_to(step).start()
        r.end_own[...] = r.end_parts[last]

    @pl.when(section == 0)
    def _():
        grads = sum(dot_left(r.mixed[slot], r.leaving[slot]) for slot in range(micro))
        tall = embed // sections
        r.start_parts[...] = jnp.zeros_like(r.start_parts)
        for to in range(sections):
            r.start_parts[to, :tall, :] = grads[to * tall : (to + 1) * tall].astype(low)
            r.start_parts[to, tall : tall + 8, :] = jnp.broadcast_to(
                r.start_row[...], (8, width)
            ).astype(low)
        for step in range(1, sections):
            start_to(step).start()
        r.start_own[...] = r.start_parts[0]

    own[SEQ_ROWS][...] = r.seq[...].astype(low)
    spread(NORM_ROWS)
    spread(SEQ_ROWS)
    for slot in range(micro):
        forward(LATENT, slot)
        forward(LOG_TOTAL, slot)
    forward(FEATURES)
    forward(NORM_ROWS)
    forward(SEQ_ROWS)

    relay_all(BRANCH, ATTN)

    @pl.when(section < last)
    def _():
        end_to(1).wait_recv()

    for slot in range(micro):

        @pl.when(section > 0)
        def _():
            mixed_to(slot, 1).wait_recv()

        spread(MIXED_GRAD, slot)

    @pl.when(section > 0)
    def _():
        start_to(1).wait_recv()

    keeps = (
        pltpu.make_async_copy(r.end_own, end_out, sems.ends.at[0]),
        pltpu.make_async_copy(r.start_own, start_out, sems.ends.at[1]),
        pltpu.make_async_copy(r.ints, ints_out, sems.ends.at[2]),
        pltpu.make_async_copy(own[LOG_TOTAL], loss_out, sems.ends.at[3]),
        pltpu.make_async_copy(own[BRANCH].at[micro - 1], branch_out, sems.ends.at[4]),
        pltpu.make_async_copy(own[ATTN].at[micro - 1], attn_out, sems.ends.at[5]),
    )
    for keep in keeps:
        keep.start()
    for slot in range(micro):
        forward(MIXED_GRAD, slot)
    for name in range(BLOCKS):
        for slot in range(slots_of(name)):
            settle(name, slot)
    for keep in keeps:
        keep.wait()

    for step in range(1, groups):
        ints_to(step).wait_send()
    for step in range(1, along):
        table_to(step).wait_send()
    for step in range(1, sections):
        parts_to(step).wait_send()
    for slot in range(micro):
        for copy in shares_to(slot, 1):
            copy.wait_send()

        @pl.when(section < last)
        def _():
            passed_on(slot).wait_send()
            for copy in shares_to(slot, 0):
                copy.wait_send()

        @pl.when(section > 0)
        def _():
            passed_back(slot).wait_send()

        @pl.when(section == last)
        def _():
            for step in range(sections):
                if step:
                    latent_to(slot, step).wait_send()
                    log_to(slot, step).wait_send()
                latent_over(slot, step).wait_send()

    @pl.when(section == last)
    def _():
        for step in range(1, sections):
            end_to(step).wait_send()

    @pl.when(section == 0)
    def _():
        for step in range(1, sections):
            for slot in range(micro):
                mixed_to(slot, step).wait_send()
            start_to(step).wait_send()


def run_chain(sources, given, sections, groups, heights):
    f32, low = jnp.float32, jnp.bfloat16
    micro, tokens, width = given.timed.shape
    inner = sources.up.shape[1]
    padded = heights[1]
    embed = given.out_proj.shape[1]
    slots = given.member.shape[1]
    lines = groups // ACROSS
    vmem = pl.BlockSpec(memory_space=pltpu.VMEM)
    anywhere = pl.BlockSpec(memory_space=pl.ANY)
    seq = -(-micro * slots // 16) * 16
    shape = jax.ShapeDtypeStruct
    blocks = (
        shape((micro, tokens, width), low),
        shape((micro, tokens, width), low),
        shape((micro, tokens, width), low),
        shape((micro, tokens, width), low),
        shape((micro, tokens, embed), low),
        shape((micro, 8, LANES), f32),
        shape((micro, tokens, embed), low),
        shape((8, width), f32),
        shape((seq, width), low),
        shape(given.features.shape, low),
    )
    end = shape((width // sections + 16, embed), low)
    start = shape((embed // sections + 16, width), low)
    dma = pltpu.SemaphoreType.DMA
    count = PER_SLOT * micro + BLOCKS - PER_SLOT
    pairs = micro * sections
    kept = Kept(
        *(pltpu.VMEM(source.shape, low) for source in sources),
        part=pltpu.VMEM((lines, padded, embed), low),
        ints=pltpu.VMEM((groups, *given.ints.shape), jnp.int32),
        rows_parts=pltpu.VMEM((sections, micro * tokens, embed), low),
        rows=pltpu.VMEM((micro, tokens, embed), low),
        mixed=pltpu.VMEM((micro, tokens, embed), low),
        other=pltpu.VMEM((micro, tokens, embed), low),
        mine=pltpu.VMEM((ACROSS, micro, tokens, embed), low),
        mine_stats=pltpu.VMEM((ACROSS, micro, tokens, LANES), f32),
        arrived=pltpu.VMEM((micro, tokens, width), f32),
        final=pltpu.VMEM((micro, tokens, width), f32),
        final_low=pltpu.VMEM((micro, tokens, width), low),
        raw=pltpu.VMEM((tokens, 3 * width), f32),
        narrow=pltpu.VMEM((tokens, width), low),
        grad_packed=pltpu.VMEM((tokens, 3 * width), low),
        current=pltpu.VMEM((micro, tokens, width), f32),
        after=pltpu.VMEM((micro, tokens, width), f32),
        packed=pltpu.VMEM((micro, tokens, 3 * width), low),
        probs=pltpu.VMEM((micro, HEADS // 2, tokens, 2 * tokens), f32),
        slope=pltpu.VMEM((micro, tokens, inner), f32),
        leaving=pltpu.VMEM((micro, tokens, width), low),
        returned=pltpu.VMEM((micro, tokens, width), low),
        upstream=pltpu.VMEM((tokens, width), f32),
        stats=pltpu.VMEM((ACROSS * sections, micro, tokens, LANES), f32),
        pulled=pltpu.VMEM((ACROSS * sections, micro, tokens, embed), low),
        grad_latent=pltpu.VMEM((micro, tokens, embed), low),
        seq=pltpu.VMEM((seq, width), f32),
        end_rows=pltpu.VMEM((8, width), f32),
        end_parts=pltpu.VMEM((sections, *end.shape), low),
        end_own=pltpu.VMEM(end.shape, low),
        start_row=pltpu.VMEM((1, width), f32),
        start_parts=pltpu.VMEM((sections, *start.shape), low),
        start_own=pltpu.VMEM(start.shape, low),
    )
    signals = Signals(
        load=dma((len(sources),)),
        keep=dma((count,)),
        out=dma((count,)),
        line=dma((2 * count,)),
        beside=dma((count,)),
        pair=dma((count,)),
        relay=dma((count,)),
        ints_send=dma((groups,)),
        ints_recv=dma((groups,)),
        rows_send=dma((groups,)),
        rows_recv=dma((groups,)),
        parts_send=dma((sections,)),
        parts_recv=dma((sections,)),
        table_send=dma((lines,)),
        table_recv=dma((lines,)),
        other_send=dma((pairs,)),
        other_recv=dma((micro,)),
        log_send=dma((pairs,)),
        log_recv=dma((micro,)),
        on_send=dma((micro,)),
        on_recv=dma((micro,)),
        back_send=dma((micro,)),
        back_recv=dma((micro,)),
        latent_send=dma((pairs,)),
        latent_recv=dma((micro,)),
        stats_send=dma((micro * ACROSS,)),
        stats_recv=dma((pairs * ACROSS,)),
        pulled_send=dma((micro * ACROSS,)),
        pulled_recv=dma((pairs * ACROSS,)),
        end_send=dma((sections,)),
        end_recv=dma,
        start_send=dma((sections,)),
        start_recv=dma,
        mixed_send=dma((pairs,)),
        mixed_recv=dma((micro,)),
        ends=dma((6,)),
    )
    boards = tuple(
        shape(
            (
                lines,
                *((ACROSS,) if at >= WIDE else ()),
                *((micro - 1, tokens, width) if at in (BRANCH, ATTN) else block.shape),
            ),
            block.dtype,
        )
        for at, block in enumerate(blocks)
    )
    outs = pl.pallas_call(
        partial(chain_kernel, sections, groups, heights),
        out_shape=(
            *boards,
            end,
            start,
            shape((groups, *given.ints.shape), jnp.int32),
            shape((micro, 8, LANES), f32),
            shape((tokens, width), low),
            shape((tokens, width), low),
        ),
        in_specs=[anywhere] * len(sources) + [vmem] * len(given),
        out_specs=(anywhere,) * (BLOCKS + 6),
        scratch_shapes=(
            *(pltpu.VMEM(block.shape, block.dtype) for block in blocks),
            *kept,
            *signals,
        ),
        compiler_params=pltpu.CompilerParams(
            collective_id=1, has_side_effects=True, vmem_limit_bytes=VMEM_BYTES
        ),
        cost_estimate=pl.CostEstimate(
            flops=10**11, bytes_accessed=6 * 10**8, transcendentals=10**7
        ),
        name="chain",
    )(*sources, *given)
    return outs[:BLOCKS], outs[BLOCKS:]


class Given2(NamedTuple):
    ints: Any
    log_total: Any
    turns: Any
    end: Any
    start: Any
    features: Any
    seq_rows: Any
    norm_rows: Any


class Results(NamedTuple):
    qkv: Any
    out: Any
    up: Any
    down: Any
    table: Any
    end: Any
    start: Any
    time: Any
    norms: Any


class Parts(NamedTuple):
    normed: Any
    mlp: Any
    branch: Any
    attn: Any
    qkv: Any
    out: Any
    up: Any
    down: Any
    raw: Any
    grad_att: Any
    attended: Any
    grad_packed: Any
    up_sum: Any
    down_sum: Any
    qkv_sum: Any
    out_sum: Any
    up_send: Any
    up_recv: Any
    down_send: Any
    down_recv: Any
    qkv_send: Any
    qkv_recv: Any
    out_send: Any
    out_recv: Any
    up_leave: Any
    up_arrive: Any
    qkv_leave: Any
    qkv_arrive: Any
    table: Any
    latent: Any
    mixed: Any
    end_recv: Any
    start_recv: Any
    end_line: Any
    start_line: Any
    time: Any


class Flags(NamedTuple):
    load: Any
    keep: Any
    late_send: Any
    late_recv: Any
    relay: Any
    pair_send: Any
    pair_recv: Any
    up_send: Any
    up_recv: Any
    qkv_send: Any
    qkv_recv: Any
    ends_send: Any
    end_recv: Any
    start_recv: Any


HBM_INPUTS = 13


def segments(lengths, slots):
    at = lax.broadcasted_iota(jnp.int32, lengths.shape, 1)
    end = lengths[:, 0:1]
    sequence = jnp.zeros_like(at)
    first = jnp.zeros_like(at)
    for slot in range(slots):
        passed = at >= end
        sequence = sequence + passed.astype(jnp.int32)
        first = jnp.where(passed, end, first)
        if slot < slots - 1:
            end = end + lengths[:, slot + 1 : slot + 2]
    return sequence, at - first, (at < end).astype(jnp.float32)


def grads_kernel(groups, slots, *refs):
    refs = iter(refs)
    hbm = [next(refs) for _ in range(HBM_INPUTS)]
    given, results, r, sems = (
        kind(*(next(refs) for _ in kind._fields)) for kind in (Given2, Results, Parts, Flags)
    )
    boards, lates, weights, (latent, mixed, table) = hbm[:4], hbm[4:6], hbm[6:10], hbm[10:]
    group = lax.axis_index(DP)
    along, beside, line = groups // ACROSS, lax.rem(group, ACROSS), group // ACROSS
    partner = line * ACROSS + (1 - beside)
    theirs = 1 - beside
    low = jnp.bfloat16
    micro, _, tokens, width = r.normed.shape
    last = micro - 1
    half = along * tokens
    quarter = r.up.shape[1]
    cols = r.out.shape[0]
    head_size = width // HEADS
    scale = head_size ** (-0.5)
    pair = 2 * head_size
    lane = lax.broadcasted_iota(jnp.int32, (tokens, pair), 1)

    def part_of(size):
        return pl.ds(pl.multiple_of(line * size, size), size)

    moves = [
        (weights[2].at[:, part_of(quarter)], r.up),
        (weights[3].at[part_of(quarter), :], r.down),
    ]
    for slot in range(last):
        moves.append((boards[1].at[:, slot], r.mlp.at[slot]))
        moves.append((boards[2].at[:, slot], r.branch.at[slot]))
    ready = len(moves)
    moves.append((weights[1].at[part_of(cols), :], r.out))
    for kind in range(3):
        from_col = pl.multiple_of(kind * width + line * cols, cols)
        moves.append((weights[0].at[:, pl.ds(from_col, cols)], r.qkv.at[:, pl.ds(kind * cols, cols)]))
    for slot in range(micro):
        moves.append((boards[0].at[:, slot], r.normed.at[slot]))
    for slot in range(last):
        moves.append((boards[3].at[:, slot], r.attn.at[slot]))
    moves.append((boards[1].at[:, last], r.mlp.at[last]))
    moves += [(latent, r.latent), (mixed, r.mixed), (table, r.table)]
    loads = [
        pltpu.make_async_copy(source, target, sems.load.at[index])
        for index, (source, target) in enumerate(moves)
    ]
    for load in loads:
        load.start()

    def line_peer(step):
        return lax.rem(line + step, along)

    barrier = pltpu.get_barrier_semaphore()
    for step in range(1, along):
        to = line_peer(step) * ACROSS + beside
        pl.semaphore_signal(barrier, inc=1, device_id={DP: to}, device_id_type=MESH)
    pl.semaphore_signal(barrier, inc=1, device_id={DP: partner}, device_id_type=MESH)
    pl.semaphore_wait(barrier, along)

    def sent(source, target, to, send_sem, recv_sem):
        return pltpu.make_async_remote_copy(
            src_ref=source,
            dst_ref=target,
            send_sem=send_sem,
            recv_sem=recv_sem,
            device_id={DP: to},
            device_id_type=MESH,
        )

    relayed = along == 4
    at_end = (line == 0) | (line == along - 1)
    late = (r.branch.at[last], r.attn.at[last])

    def keep(index):
        return pltpu.make_async_copy(lates[index], late[index].at[line], sems.keep.at[index])

    def push(index):
        keep(index).start()
        for step in range(1, along):
            peer = line_peer(step)
            far = 0
            if relayed:
                far = (at_end & (jnp.abs(line - peer) == 2)).astype(jnp.int32)
            copy = sent(
                lates[index],
                late[index].at[line],
                peer * ACROSS + beside,
                sems.late_send.at[index],
                sems.late_recv.at[far * 2 + index],
            )
            if relayed:
                pl.when(jnp.abs(line - peer) < 3)(copy.start)
            else:
                copy.start()

    def wait_blocks(index, count, sem):
        ref = late[index].at[pl.ds(0, count)]
        pltpu.make_async_copy(ref, ref, sem).wait()

    def relay_copy(index):
        there = late[index].at[jnp.where(line == 1, along - 1, 0)]
        to = jnp.where(line == 1, 0, along - 1) * ACROSS + beside
        return sent(there, there, to, sems.relay.at[index], sems.late_recv.at[index])

    def relay(index):
        if relayed:

            @pl.when(jnp.logical_not(at_end))
            def _():
                wait_blocks(index, 1, sems.late_recv.at[2 + index])
                relay_copy(index).start()

    def arrived(index):
        keep(index).wait()
        if relayed:

            @pl.when(at_end)
            def _():
                wait_blocks(index, 3, sems.late_recv.at[index])

            @pl.when(jnp.logical_not(at_end))
            def _():
                wait_blocks(index, 2, sems.late_recv.at[index])

        else:
            wait_blocks(index, along - 1, sems.late_recv.at[index])

    def pushed(index):
        if relayed:

            @pl.when(at_end)
            def _():
                wait_blocks(index, 2, sems.late_send.at[index])

            @pl.when(jnp.logical_not(at_end))
            def _():
                wait_blocks(index, 3, sems.late_send.at[index])
                relay_copy(index).wait_send()

        else:
            wait_blocks(index, along - 1, sems.late_send.at[index])

    push(0)

    swaps = [
        sent(source, target, partner, sems.pair_send.at[index], sems.pair_recv.at[index])
        for index, (source, target) in enumerate(
            (
                (r.up_send, r.up_recv),
                (r.down_send, r.down_recv),
                (r.qkv_send, r.qkv_recv),
                (r.out_send, r.out_recv),
                (given.end, r.end_recv),
                (given.start, r.start_recv),
            )
        )
    ]
    swaps[4].start()
    swaps[5].start()

    def along_line(step, board, send, recv):
        ref = board.at[line]
        to = line_peer(step) * ACROSS + beside
        return sent(ref, ref, to, sems.ends_send.at[send * along + step], recv.at[line])

    def scatter(step, leave, arrive, send, recv):
        to = line_peer(step)
        return sent(leave.at[to], arrive.at[line], to * ACROSS + beside, send.at[step], recv.at[line])

    def gathered(source, arrive, recv):
        ref = arrive.at[source]
        return sent(ref, ref, partner, recv.at[source], recv.at[source])

    chunk = quarter // ACROSS

    def feed_forward(slot):
        normed_mlp = r.mlp[slot].reshape(half, width)
        branch = r.branch[slot].reshape(half, width)
        for side in range(ACROSS):
            at = side * chunk
            pre_act = dot(normed_mlp, r.up[:, at : at + chunk])
            below = 0.5 + 0.5 * lax.erf(pre_act * 0.5**0.5)
            bell = jnp.exp(-0.5 * pre_act * pre_act) * (0.5 / jnp.pi) ** 0.5
            activated = (pre_act * below).astype(low)
            grad_act = dot_right(branch, r.down[at : at + chunk, :])
            grad_pre = ((below + pre_act * bell) * grad_act).astype(low)
            grad_up = dot_left(normed_mlp, grad_pre).reshape(*r.up_sum.shape[:3], chunk)
            grad_down = dot_left(activated, branch)
            if slot == 0:
                r.up_sum[:, :, :, at : at + chunk] = grad_up
                r.down_sum[side] = grad_down
            else:
                r.up_sum[:, :, :, at : at + chunk] += grad_up
                r.down_sum[side] += grad_down

    def turned(values, turns, sign):
        swapped = halves_swapped(values, head_size, lane) * turns[1]
        return values * turns[0] + (swapped if sign > 0 else -swapped)

    def together(rows):
        return jnp.where(lane < head_size, rows[:tokens], rows[tokens:])

    def bucket_turns(slot, owner):
        lengths = given.ints[owner, 2 * micro + slot : 2 * micro + slot + 1, :]
        sequence, inside, _ = segments(lengths, slots)
        both = jnp.broadcast_to(sequence * LANES + inside, (tokens, LANES)).astype(jnp.float32)
        column = jnp.transpose(both).astype(jnp.int32)
        mask = jnp.where(column // LANES == sequence, 0.0, mask_fill)
        hit = (column % LANES == lane).astype(jnp.float32).astype(low)
        found = dot(hit, given.turns[...])
        wide = 2 * pair
        found = found[:, :wide] + found[:, wide : 2 * wide] + found[:, 2 * wide :]
        return (found[:, :pair], found[:, pair:]), mask

    def attention(slot):
        normed = r.normed[slot].reshape(half, width)
        for at in range(0, 3 * cols, cols):
            r.raw[:, at : at + cols] = dot(normed, r.qkv[:, at : at + cols])
        r.grad_att[...] = dot_right(r.attn[slot].reshape(half, width), r.out[...]).astype(low)

        def one_bucket(peer, carry):
            turns, mask = bucket_turns(slot, peer * ACROSS + beside)
            rows = pl.ds(pl.multiple_of(peer * tokens, tokens), tokens)
            to = pl.ds(pl.multiple_of((slot * along + peer) * tokens, tokens), tokens)
            for at in range(0, cols, pair):
                queries = turned(r.raw[rows, at : at + pair], turns, 1).astype(low)
                keys = turned(r.raw[rows, cols + at : cols + at + pair], turns, 1).astype(low)
                values = r.raw[rows, 2 * cols + at : 2 * cols + at + pair].astype(low)
                grad_here = r.grad_att[rows, at : at + pair]
                keys_apart = apart(keys, lane, head_size)
                values_apart = apart(values, lane, head_size)
                scores = dot_right(queries, keys_apart) * scale
                grad_prob = dot_right(grad_here, values_apart)
                probs, grad_score = [], []
                for side in range(2):
                    part = scores[:, side * tokens : (side + 1) * tokens] + mask
                    raised = jnp.exp(part - jnp.max(part, axis=-1, keepdims=True))
                    here = raised / jnp.sum(raised, axis=-1, keepdims=True)
                    there = grad_prob[:, side * tokens : (side + 1) * tokens]
                    mean = jnp.sum(here * there, axis=-1, keepdims=True)
                    probs.append(here.astype(low))
                    grad_score.append((here * (there - mean)).astype(low))
                probs = jnp.concatenate(probs, axis=1)
                grad_score = jnp.concatenate(grad_score, axis=1)
                r.attended[to, at : at + pair] = dot(probs, values_apart).astype(low)
                grad_query = turned(dot(grad_score, keys_apart) * scale, turns, -1)
                grad_key = turned(together(dot_left(grad_score, queries)) * scale, turns, -1)
                grad_value = together(dot_left(probs, grad_here))
                for kind, grad in enumerate((grad_query, grad_key, grad_value)):
                    r.grad_packed[to, kind * cols + at : kind * cols + at + pair] = grad.astype(low)
            return carry

        lax.fori_loop(0, along, one_bucket, 0)

    for load in loads[:ready]:
        load.wait()
    for slot in range(last):
        feed_forward(slot)
    relay(0)
    push(1)
    for load in loads[ready:]:
        load.wait()
    arrived(0)
    feed_forward(last)
    r.up_send[...] = r.up_sum[:, theirs].astype(low)
    swaps[0].start()
    r.down_send[...] = r.down_sum[theirs].astype(low)
    swaps[1].start()
    for slot in range(last):
        attention(slot)
    relay(1)

    ends = ((0, r.end_line, sems.end_recv), (1, r.start_line, sems.start_recv))
    for swap, mine, other, board in (
        (swaps[4], given.end, r.end_recv, r.end_line),
        (swaps[5], given.start, r.start_recv, r.start_line),
    ):
        swap.wait_recv()
        board[line] = (mine[...].astype(jnp.float32) + other[...].astype(jnp.float32)).astype(low)
    for send, board, recv in ends:
        for step in range(1, along):
            along_line(step, board, send, recv).start()

    height, embed = results.table.shape
    group_tokens = r.latent.shape[0] // groups
    logit_scale = embed ** (-0.5)
    base = (lax.axis_index(SECTION) * groups + group) * height
    row = lax.broadcasted_iota(jnp.int32, (r.table.shape[0], group_tokens), 0)

    def one_group(owner, total):
        ints = given.ints[owner]
        ids = jnp.concatenate([ints[slot : slot + 1] for slot in range(micro)], axis=1)
        weight, log_total = [], []
        for slot in range(micro):
            lengths = ints[2 * micro + slot : 2 * micro + slot + 1]
            noised = ints[micro + slot : micro + slot + 1].astype(jnp.float32)
            weight.append(noised * segments(lengths, slots)[2] / (micro * tokens))
            log_total.append(given.log_total[owner, slot][0:1])
        weight, log_total = (jnp.concatenate(rows, axis=1) for rows in (weight, log_total))
        rows = pl.ds(pl.multiple_of(owner * group_tokens, group_tokens), group_tokens)
        latent = r.latent[rows, :]
        logits = dot_right(r.table[...], latent) * logit_scale
        hit = (row == ids - base).astype(jnp.float32)
        grad_logit = (weight * (jnp.exp(logits - log_total) - hit)).astype(low)
        return (
            total
            + dot(grad_logit, latent) * logit_scale
            + dot(hit.astype(low), r.mixed[rows, :])
        )

    grad_table = lax.fori_loop(
        0, groups, one_group, jnp.zeros((r.table.shape[0], embed), jnp.float32)
    )
    results.table[...] = grad_table[:height]

    arrived(1)
    attention(last)
    normed = r.normed[...].reshape(micro * half, width)
    r.qkv_sum[...] = dot_left(normed, r.grad_packed[...]).reshape(r.qkv_sum.shape)
    r.qkv_send[...] = r.qkv_sum[:, theirs].astype(low)
    swaps[2].start()
    attn = r.attn[...].reshape(micro * half, width)
    r.out_sum[...] = dot_left(r.attended[...], attn).reshape(r.out_sum.shape)
    r.out_send[...] = r.out_sum[theirs].astype(low)
    swaps[3].start()

    swaps[0].wait_recv()
    r.up_leave[...] = (r.up_sum[:, beside] + r.up_recv[...].astype(jnp.float32)).astype(low)
    for step in range(1, along):
        scatter(step, r.up_leave, r.up_arrive, sems.up_send, sems.up_recv).start()

    total = jnp.zeros(given.norm_rows.shape[1:], jnp.float32)
    for source in range(groups):
        total = total + given.norm_rows[source]
    count = given.features.shape[0] * given.features.shape[1]
    r.time[0:embed] = dot_left(
        given.features[...].reshape(count, embed), given.seq_rows[...].reshape(count, width)
    )
    r.time[embed : embed + 8] = total
    rows = embed // groups
    results.time[...] = r.time[pl.ds(pl.multiple_of(group * rows, rows), rows), :]
    own_cols = pl.ds(pl.multiple_of(group * (width // groups), width // groups), width // groups)
    results.norms[...] = r.time[embed : embed + 8, own_cols]

    swaps[1].wait_recv()
    results.down[...] = r.down_sum[beside] + r.down_recv[...].astype(jnp.float32)
    swaps[2].wait_recv()
    r.qkv_leave[...] = (r.qkv_sum[:, beside] + r.qkv_recv[...].astype(jnp.float32)).astype(low)
    for step in range(1, along):
        scatter(step, r.qkv_leave, r.qkv_arrive, sems.qkv_send, sems.qkv_recv).start()
    swaps[3].wait_recv()
    results.out[...] = r.out_sum[beside] + r.out_recv[...].astype(jnp.float32)
    for arrive, leave, recv in (
        (r.up_arrive, r.up_leave, sems.up_recv),
        (r.qkv_arrive, r.qkv_leave, sems.qkv_recv),
    ):
        for source in range(along):

            @pl.when(line == source)
            def _():
                arrive[source] = leave[source]

            @pl.when(line != source)
            def _():
                gathered(source, arrive, recv).wait_recv()

            block = arrive[source].astype(jnp.float32)
            if arrive is r.up_arrive:
                results.up[:, source * quarter : (source + 1) * quarter] = block
            else:
                for kind in range(3):
                    at = kind * width + source * cols
                    results.qkv[:, at : at + cols] = block[:, kind * cols : (kind + 1) * cols]
    for send, board, recv in ends:
        for source in range(along):

            @pl.when(line != source)
            def _():
                gathered(source, board, recv).wait_recv()

    results.end[...] = sum(r.end_line[source].astype(jnp.float32) for source in range(along))
    results.start[...] = sum(r.start_line[source].astype(jnp.float32) for source in range(along))
    for index in range(2):
        pushed(index)
    for swap in swaps:
        swap.wait_send()
    for send, board, recv in ends:
        for step in range(1, along):
            along_line(step, board, send, recv).wait_send()
    for step in range(1, along):
        scatter(step, r.up_leave, r.up_arrive, sems.up_send, sems.up_recv).wait_send()
        scatter(step, r.qkv_leave, r.qkv_arrive, sems.qkv_send, sems.qkv_recv).wait_send()


def run_grads(boards, lates, weights, narrow, given, height, groups, slots):
    f32, low = jnp.float32, jnp.bfloat16
    along, micro, tokens, width = boards[0].shape
    inner = weights[2].shape[1]
    latent, mixed, table = narrow
    embed = table.shape[1]
    total = along * micro * tokens
    quarter, cols, rows = inner // along, width // along, width // groups
    vmem = pl.BlockSpec(memory_space=pltpu.VMEM)
    anywhere = pl.BlockSpec(memory_space=pl.ANY)
    dma = pltpu.SemaphoreType.DMA
    end, start = given.end.shape, given.start.shape
    parts = Parts(
        *(pltpu.VMEM((micro, along, tokens, width), low) for _ in range(4)),
        qkv=pltpu.VMEM((width, 3 * cols), low),
        out=pltpu.VMEM((cols, width), low),
        up=pltpu.VMEM((width, quarter), low),
        down=pltpu.VMEM((quarter, width), low),
        raw=pltpu.VMEM((along * tokens, 3 * cols), f32),
        grad_att=pltpu.VMEM((along * tokens, cols), low),
        attended=pltpu.VMEM((total, cols), low),
        grad_packed=pltpu.VMEM((total, 3 * cols), low),
        up_sum=pltpu.VMEM((along, ACROSS, rows, quarter), f32),
        down_sum=pltpu.VMEM((ACROSS, quarter // ACROSS, width), f32),
        qkv_sum=pltpu.VMEM((along, ACROSS, rows, 3 * cols), f32),
        out_sum=pltpu.VMEM((ACROSS, rows, width), f32),
        up_send=pltpu.VMEM((along, rows, quarter), low),
        up_recv=pltpu.VMEM((along, rows, quarter), low),
        down_send=pltpu.VMEM((quarter // ACROSS, width), low),
        down_recv=pltpu.VMEM((quarter // ACROSS, width), low),
        qkv_send=pltpu.VMEM((along, rows, 3 * cols), low),
        qkv_recv=pltpu.VMEM((along, rows, 3 * cols), low),
        out_send=pltpu.VMEM((rows, width), low),
        out_recv=pltpu.VMEM((rows, width), low),
        up_leave=pltpu.VMEM((along, rows, quarter), low),
        up_arrive=pltpu.VMEM((along, rows, quarter), low),
        qkv_leave=pltpu.VMEM((along, rows, 3 * cols), low),
        qkv_arrive=pltpu.VMEM((along, rows, 3 * cols), low),
        table=pltpu.VMEM(table.shape, low),
        latent=pltpu.VMEM(latent.shape, low),
        mixed=pltpu.VMEM(mixed.shape, low),
        end_recv=pltpu.VMEM(end, low),
        start_recv=pltpu.VMEM(start, low),
        end_line=pltpu.VMEM((along, *end), low),
        start_line=pltpu.VMEM((along, *start), low),
        time=pltpu.VMEM((embed + 8, width), f32),
    )
    flags = Flags(
        load=dma((9 + 4 * micro,)),
        keep=dma((2,)),
        late_send=dma((2,)),
        late_recv=dma((4,)),
        relay=dma((2,)),
        pair_send=dma((6,)),
        pair_recv=dma((6,)),
        up_send=dma((along,)),
        up_recv=dma((along,)),
        qkv_send=dma((along,)),
        qkv_recv=dma((along,)),
        ends_send=dma((2 * along,)),
        end_recv=dma((along,)),
        start_recv=dma((along,)),
    )
    shapes = Results(
        qkv=(rows, 3 * width),
        out=(rows, width),
        up=(rows, inner),
        down=(inner // groups, width),
        table=(height, embed),
        end=end,
        start=start,
        time=(embed // groups, width),
        norms=(8, rows),
    )
    return Results(
        *pl.pallas_call(
            partial(grads_kernel, groups, slots),
            out_shape=tuple(jax.ShapeDtypeStruct(shape, f32) for shape in shapes),
            in_specs=[anywhere] * HBM_INPUTS + [vmem] * len(given),
            out_specs=(vmem,) * len(shapes),
            scratch_shapes=(*parts, *flags),
            compiler_params=pltpu.CompilerParams(
                collective_id=2, has_side_effects=True, vmem_limit_bytes=VMEM_BYTES
            ),
            cost_estimate=pl.CostEstimate(
                flops=10**11, bytes_accessed=10**8, transcendentals=10**7
            ),
            name="grads",
        )(*boards, *lates, *weights, *narrow, *given)
    )


def block_of(array, axis, count, index):
    size = array.shape[axis] // count
    return lax.dynamic_slice_in_dim(array, index * size, size, axis)


def rope_lanes(cosine, sine):
    signed = jnp.concatenate([-sine, sine], axis=-1)
    return (jnp.tile(cosine, (1, 1, 4)), jnp.tile(signed, (1, 1, 2)))


def local_grads(held, w_qkv, w_out, w_up, w_down, rope):
    normed, normed_mlp, branch, attn_branch = held
    cosine, sine, same_seq = rope
    buckets, tokens = same_seq.shape[:2]
    width = normed.shape[1]
    head_size = width // HEADS
    scale = head_size ** (-0.5)
    low = jnp.bfloat16
    wide = partial(jnp.einsum, preferred_element_type=jnp.float32)

    pre_act = wide("td,df->tf", normed_mlp, w_up)
    activated, back_gelu = jax.vjp(gelu_exact, pre_act)
    grad_act = wide("td,fd->tf", branch, w_down)
    grad_pre = back_gelu(grad_act)[0].astype(low)

    packed = wide("td,dc->tc", normed, w_qkv).reshape(buckets, tokens, 3, HEADS, head_size)
    turn = jax.vmap(rotate)
    queries = turn(packed[:, :, 0], cosine, sine).astype(low)
    keys = turn(packed[:, :, 1], cosine, sine).astype(low)
    values = packed[:, :, 2].astype(low)
    scores = jnp.where(
        same_seq[:, None], wide("bthd,bshd->bhts", queries, keys) * scale, mask_fill
    )
    probs = jax.nn.softmax(scores, axis=-1)
    attended = wide("bhts,bshd->bthd", probs.astype(low), values).astype(low)
    grad_att = wide("td,cd->tc", attn_branch, w_out).astype(low).reshape(queries.shape)
    grad_prob = wide("bthd,bshd->bhts", grad_att, values)
    inner = jnp.sum(probs * grad_prob, axis=-1, keepdims=True)
    grad_score = (probs * (grad_prob - inner)).astype(low)
    back = jax.vmap(rotate_back)
    grad_query = back(wide("bhts,bshd->bthd", grad_score, keys) * scale, cosine, sine)
    grad_key = back(wide("bhts,bthd->bshd", grad_score, queries) * scale, cosine, sine)
    grad_value = wide("bhts,bthd->bshd", probs.astype(low), grad_att)
    grads = jnp.stack([grad_query, grad_key, grad_value], axis=2).astype(low)
    return (
        wide("td,tc->dc", normed, grads.reshape(normed.shape[0], -1)),
        wide("tc,td->cd", attended.reshape(normed.shape), attn_branch),
        wide("td,tf->df", normed_mlp, grad_pre),
        wide("tf,td->fd", activated.astype(low), branch),
    )


def table_grads(table, latent_all, mixed_all, own, log_all, weight_all):
    logit_scale = table.shape[1] ** (-0.5)
    hit = own[:, None] == jnp.arange(table.shape[0], dtype=jnp.int32)[None, :]
    logits = jnp.dot(latent_all, table.T, preferred_element_type=jnp.float32) * logit_scale
    grad_logit = jnp.exp(logits - log_all[:, None]) - hit.astype(jnp.float32)
    grad_logit = (weight_all[:, None] * grad_logit).astype(jnp.bfloat16)
    head = jnp.dot(grad_logit.T, latent_all, preferred_element_type=jnp.float32) * logit_scale
    return head + jnp.dot(
        hit.astype(jnp.bfloat16).T, mixed_all, preferred_element_type=jnp.float32
    )


def plain_grads(blocks, lates, weights, narrow, given, rope, make_layout):
    groups, group = lax.axis_size(DP), lax.axis_index(DP)
    _, micro, tokens, width = blocks[NORMED].shape
    latent_all, mixed_all, table = narrow
    embed = table.shape[1]
    slots = given.seq_rows.shape[1] // micro
    ints = given.ints
    line = group // ACROSS
    held = [
        lax.dynamic_index_in_dim(blocks[at], line, 0, keepdims=False)
        for at in (NORMED, MLP, BRANCH, ATTN)
    ]
    for at, late in zip((2, 3), lates):
        held[at] = jnp.concatenate([held[at], late[None]], axis=0)
    sums = local_grads([item.reshape(micro * tokens, width) for item in held], *weights, rope)
    grad_qkv, grad_out, grad_up, grad_down = (
        lax.psum_scatter(
            item.astype(jnp.bfloat16), DP, scatter_dimension=0, tiled=True
        ).astype(jnp.float32)
        for item in sums
    )
    inside = make_layout(
        ints[:, 2 * micro : 3 * micro, :slots].reshape(-1, slots),
        ints[:, 3 * micro : 4 * micro, :slots].reshape(-1, slots),
    )[6]
    noised = ints[:, micro : 2 * micro, :tokens].astype(jnp.float32).reshape(-1)
    first_row = (lax.axis_index(SECTION) * groups + group) * table.shape[0]
    grad_table = table_grads(
        table,
        latent_all,
        mixed_all,
        ints[:, :micro, :tokens].reshape(-1) - first_row,
        given.log_total[:, :, 0].reshape(-1),
        noised * inside.reshape(-1) / (micro * tokens),
    )
    end, start = lax.psum((given.end.astype(jnp.float32), given.start.astype(jnp.float32)), DP)
    features = block_of(given.features.reshape(-1, embed), 1, groups, group)
    grad_time = jnp.dot(
        features.T, given.seq_rows.reshape(-1, width), preferred_element_type=jnp.float32
    )
    norms = block_of(jnp.sum(given.norm_rows, axis=0), 1, groups, group)
    return Results(
        grad_qkv, grad_out, grad_up, grad_down, grad_table, end, start, grad_time, norms
    )


def local(
    token_ids,
    noise,
    noised,
    lengths,
    step_index,
    table,
    in_proj,
    in_bias,
    ln1_gain,
    ln1_bias,
    w_qkv,
    w_out,
    ln2_gain,
    ln2_bias,
    w_up,
    w_down,
    w_time,
    final_gain,
    final_bias,
    out_proj,
):
    sections = lax.axis_size(SECTION)
    groups = lax.axis_size(DP)
    section = lax.axis_index(SECTION)
    group = lax.axis_index(DP)
    micro, tokens = token_ids.shape
    embed, width = in_proj.shape
    head_size = width // HEADS
    total = micro * tokens
    slots = lengths.shape[-1]
    make_layout = jax.vmap(
        partial(
            bucket_layout, tokens=tokens, embed=embed, head_size=head_size, noise_steps=NOISE_STEPS
        )
    )
    layouts = make_layout(lengths[:, 0], step_index[:, 0])

    height = table.shape[0]
    padded = -(-height // LANES) * LANES
    own_rows = jnp.pad(table, ((0, padded - height), (0, 0)))
    lane_fill = ((0, 0), (0, LANES - slots))
    ints = jnp.concatenate(
        [
            token_ids,
            noised,
            jnp.pad(lengths[:, 0], lane_fill),
            jnp.pad(step_index[:, 0], lane_fill),
        ],
        axis=0,
    )
    amount = noised.astype(jnp.float32) * layouts[5]
    shrink = lax.rsqrt(1.0 + amount * amount)

    norms = jnp.concatenate(
        [ln1_gain, ln1_bias, ln2_gain, ln2_bias, final_gain[None], final_bias[None], in_bias[None]],
        axis=0,
    )
    norms = jnp.pad(norms, ((0, 1), (0, 0))).astype(jnp.float32)
    features = layouts[4].astype(jnp.bfloat16)
    per_seq = jnp.einsum(
        "mse,ed->msd",
        features,
        w_time[0],
        preferred_element_type=jnp.float32,
    )
    timed = jnp.einsum("mts,msd->mtd", layouts[0], per_seq, precision=lax.Precision.HIGHEST)
    cosine, sine = rope_lanes(layouts[2], layouts[3])
    mask = jnp.where(layouts[1], 0.0, mask_fill)
    weight = noised.reshape(-1).astype(jnp.float32) * layouts[6].reshape(-1) / total
    column = jnp.arange(ROW_CHUNK, dtype=jnp.int32) % padded
    padding = jnp.broadcast_to(jnp.where(column < height, 0.0, mask_fill), (8, ROW_CHUNK))
    chain = run_chain(
        Sources(own_rows, w_qkv[0], w_out[0], w_up[0], w_down[0]),
        Given(
            ints,
            noise,
            amount.reshape(micro, tokens, 1),
            norms,
            timed,
            cosine,
            sine,
            mask,
            layouts[0].transpose(0, 2, 1),
            features.reshape(micro * slots, embed),
            padding,
            out_proj,
            in_proj,
            weight.reshape(micro, tokens, 1),
            shrink.reshape(micro, tokens, 1),
        ),
        sections,
        groups,
        (height, padded),
    )
    blocks, (end_own, start_own, ints_all, loss, branch, attn_branch) = chain
    loss_block = block_of(loss[:, 4:5], 2, sections, section)
    latent_all = blocks[LATENT].reshape(-1, embed)
    mixed_all = blocks[MIXED_GRAD].reshape(-1, embed)
    log_all = blocks[LOG_TOTAL].reshape(groups, micro, 8, LANES)
    norm_rows = blocks[NORM_ROWS].reshape(groups, 8, width)
    seq_rows = blocks[SEQ_ROWS].reshape(groups, -1, width)
    features_all = blocks[FEATURES].reshape(groups, micro * slots, embed)
    weights = (w_qkv[0], w_out[0], w_up[0], w_down[0])
    lines = groups // ACROSS
    if HEADS % (2 * lines) == 0 and lines * tokens % LANES == 0:
        places = jnp.arange(tokens, dtype=jnp.int32).astype(jnp.float32)
        half_size = head_size // 2
        inverse = rope_base ** (-(jnp.arange(half_size).astype(jnp.float32) * 2.0) / head_size)
        angles = places[:, None] * inverse[None, :]
        turns = jnp.concatenate(rope_lanes(jnp.cos(angles)[None], jnp.sin(angles)[None]), axis=2)[0]
        pieces = []
        for _ in range(3):
            pieces.append(turns.astype(jnp.bfloat16))
            turns = turns - pieces[-1].astype(jnp.float32)
        shares = run_grads(
            [blocks[at] for at in (NORMED, MLP, BRANCH, ATTN)],
            (branch, attn_branch),
            weights,
            (latent_all, mixed_all, own_rows),
            Given2(
                ints_all,
                log_all,
                jnp.concatenate(pieces, axis=1),
                end_own,
                start_own,
                features_all,
                seq_rows,
                norm_rows,
            ),
            height,
            groups,
            slots,
        )
    else:
        shares = plain_grads(
            blocks,
            (branch, attn_branch),
            weights,
            (latent_all, mixed_all, table),
            Given2(
                ints_all, log_all, None, end_own, start_own, features_all, seq_rows, norm_rows
            ),
            (layouts[2], layouts[3], layouts[1]),
            make_layout,
        )
    side = width // sections
    tall = embed // sections
    norm_sums = shares.norms
    start_share, end_share = shares.start, shares.end
    return (
        loss_block,
        shares.table,
        start_share[:tall],
        lax.dynamic_slice_in_dim(start_share[tall], section * side, side),
        norm_sums[0:1],
        norm_sums[1:2],
        shares.qkv[None],
        shares.out[None],
        norm_sums[2:3],
        norm_sums[3:4],
        shares.up[None],
        shares.down[None],
        shares.time[None],
        end_share[side],
        end_share[side + 1],
        end_share[:side],
    )


def solution(mesh):
    placed = (
        P(None, DP),
        P(None, DP, None),
        P(None, DP),
        P(None, DP, None),
        P(None, DP, None),
        P((SECTION, DP), None),
        P(),
        P(),
        P(SECTION, None),
        P(SECTION, None),
        P(SECTION, None, None),
        P(SECTION, None, None),
        P(SECTION, None),
        P(SECTION, None),
        P(SECTION, None, None),
        P(SECTION, None, None),
        P(SECTION, None, None),
        P(),
        P(),
        P(),
    )
    return jax.shard_map(
        local,
        mesh=mesh,
        in_specs=placed,
        out_specs=(
            P(None, DP, SECTION),
            P((SECTION, DP), None),
            P(SECTION, None),
            P(SECTION),
            P(SECTION, DP),
            P(SECTION, DP),
            P(SECTION, DP, None),
            P(SECTION, DP, None),
            P(SECTION, DP),
            P(SECTION, DP),
            P(SECTION, DP, None),
            P(SECTION, DP, None),
            P(SECTION, DP, None),
            P(SECTION),
            P(SECTION),
            P(SECTION, None),
        ),
        check_vma=False,
    )
```

```python
from functools import partial
from typing import Any, NamedTuple

import jax
import jax.numpy as jnp
from jax import lax
from jax.experimental import pallas as pl
from jax.experimental.pallas import tpu as pltpu
from jax.sharding import PartitionSpec as P

HEADS = 16
NOISE_STEPS = 200
SECTION = "section"
DP = "dp"
MESH = pl.DeviceIdType.MESH
VMEM_BYTES = 62 * 1024 * 1024
FF_CHUNK = 512
PACK_CHUNK = 512
ROW_CHUNK = 1024
LANES = 128
ACROSS = 2

norm_eps = 1e-05
mask_fill = -1e30
sigma_low = 1.0
sigma_high = 300.0
rope_base = 10000.0


def layer_norm(values, gain, bias):
    center = values - jnp.mean(values, axis=-1, keepdims=True)
    spread = jnp.mean(center * center, axis=-1, keepdims=True)
    return center * lax.rsqrt(spread + norm_eps) * gain + bias


def gelu_exact(values):
    return jax.nn.gelu(values, approximate=False)


def rotate(vectors, cosine, sine):
    half = vectors.shape[-1] // 2
    first = vectors[..., :half]
    second = vectors[..., half:]
    cos_part = cosine[:, None, :]
    sin_part = sine[:, None, :]
    return jnp.concatenate(
        [first * cos_part - second * sin_part, second * cos_part + first * sin_part], axis=-1
    )


def rotate_back(grads, cosine, sine):
    half = grads.shape[-1] // 2
    first = grads[..., :half]
    second = grads[..., half:]
    cos_part = cosine[:, None, :]
    sin_part = sine[:, None, :]
    return jnp.concatenate(
        [first * cos_part + second * sin_part, second * cos_part - first * sin_part], axis=-1
    )


def bucket_layout(lens, steps, tokens, embed, head_size, noise_steps):
    ends = jnp.cumsum(lens)
    starts = ends - lens
    place = jnp.arange(tokens, dtype=jnp.int32)
    member = (place[:, None] >= starts[None, :]) & (place[:, None] < ends[None, :])
    member_int = member.astype(jnp.int32)
    slots = lens.shape[0]
    inside = jnp.sum(member_int, axis=1)
    segment = (
        jnp.sum(member_int * jnp.arange(slots, dtype=jnp.int32)[None, :], axis=1)
        + (1 - inside) * slots
    )
    offset = jnp.sum(member_int * starts[None, :], axis=1) + (1 - inside) * ends[-1]
    within = (place - offset).astype(jnp.float32)
    membership = member.astype(jnp.float32)
    sigma = sigma_low * (sigma_high / sigma_low) ** (steps.astype(jnp.float32) / (noise_steps - 1))
    level = jnp.sum(membership * sigma[None, :], axis=1)
    half = embed // 2
    rates = 100.0 ** (jnp.arange(half).astype(jnp.float32) / half)
    phase = (jnp.log(sigma) * 0.25)[:, None] * rates[None, :]
    features = jnp.concatenate([jnp.cos(phase), jnp.sin(phase)], axis=1)
    quarter = head_size // 2
    inverse = rope_base ** (-(jnp.arange(quarter).astype(jnp.float32) * 2.0) / head_size)
    angles = within[:, None] * inverse[None, :]
    same_seq = segment[:, None] == segment[None, :]
    return (
        membership,
        same_seq,
        jnp.cos(angles),
        jnp.sin(angles),
        features,
        level,
        inside.astype(jnp.float32),
    )


def embed_input(full_table, token_row, noise_row, noised_row, level):
    rows = full_table[token_row].astype(jnp.float32)
    amount = noised_row.astype(jnp.float32) * level
    shrink = lax.rsqrt(1.0 + amount * amount)
    mixed = (rows + amount[:, None] * noise_row.astype(jnp.float32)) * shrink[:, None]
    return (mixed.astype(jnp.bfloat16), shrink)


def normal(values):
    center = values - jnp.mean(values, axis=-1, keepdims=True)
    spread = jnp.mean(center * center, axis=-1, keepdims=True)
    inverse = lax.rsqrt(spread + norm_eps)
    return (center * inverse, inverse)


def normal_back(grads, gain, unit, inverse):
    scaled = grads * gain
    first = jnp.mean(scaled, axis=-1, keepdims=True)
    second = jnp.mean(scaled * unit, axis=-1, keepdims=True)
    return inverse * (scaled - first - unit * second)


def dot(left, right):
    return lax.dot_general(
        left, right, (((1,), (0,)), ((), ())), preferred_element_type=jnp.float32
    )


def dot_right(left, right):
    return lax.dot_general(
        left, right, (((1,), (1,)), ((), ())), preferred_element_type=jnp.float32
    )


def dot_left(left, right):
    return lax.dot_general(
        left, right, (((0,), (0,)), ((), ())), preferred_element_type=jnp.float32
    )


def halves_swapped(values, head_size, lane):
    half = head_size // 2
    size = values.shape[-1]
    ahead = pltpu.roll(values, size - half, 1)
    behind = pltpu.roll(values, half, 1)
    return jnp.where(lane % head_size < half, ahead, behind)


def apart(pair, lane, head_size):
    zero = jnp.zeros_like(pair)
    return jnp.concatenate(
        [jnp.where(lane < head_size, pair, zero), jnp.where(lane < head_size, zero, pair)], axis=0
    )


NORMED, MLP, BRANCH, ATTN, LATENT, LOG_TOTAL, FEATURES = range(7)
WIDE, PER_SLOT, BLOCKS = 4, 6, 7


class Sources(NamedTuple):
    table: Any
    qkv: Any
    out: Any
    up: Any
    down: Any


class Given(NamedTuple):
    ints: Any
    noise: Any
    amount: Any
    norms: Any
    timed: Any
    cosine: Any
    sine: Any
    mask: Any
    member: Any
    features: Any
    padding: Any
    out_proj: Any
    in_proj: Any
    weight: Any
    shrink: Any


class Kept(NamedTuple):
    table: Any
    qkv: Any
    out: Any
    up: Any
    down: Any
    part: Any
    ints: Any
    rows_parts: Any
    rows: Any
    mixed: Any
    other: Any
    mine: Any
    mine_stats: Any
    arrived: Any
    final: Any
    final_low: Any
    raw: Any
    narrow: Any
    grad_packed: Any
    current: Any
    after: Any
    packed: Any
    probs: Any
    slope: Any
    leaving: Any
    returned: Any
    upstream: Any
    stats: Any
    pulled: Any
    grad_latent: Any
    seq: Any
    mixed_grad: Any
    norm_rows: Any
    seq_rows: Any
    end_rows: Any
    end_parts: Any
    end_own: Any
    start_row: Any
    start_parts: Any
    start_own: Any


class Signals(NamedTuple):
    load: Any
    keep: Any
    out: Any
    line: Any
    beside: Any
    pair: Any
    relay: Any
    ints_send: Any
    ints_recv: Any
    rows_send: Any
    rows_recv: Any
    parts_send: Any
    parts_recv: Any
    table_send: Any
    table_recv: Any
    other_send: Any
    other_recv: Any
    log_send: Any
    log_recv: Any
    on_send: Any
    on_recv: Any
    back_send: Any
    back_recv: Any
    latent_send: Any
    latent_recv: Any
    stats_send: Any
    stats_recv: Any
    pulled_send: Any
    pulled_recv: Any
    end_send: Any
    end_recv: Any
    start_send: Any
    start_recv: Any
    mixed_send: Any
    mixed_recv: Any
    ends: Any


def chain_kernel(sections, groups, heights, *refs):
    refs = iter(refs)
    sources, given = (kind(*(next(refs) for _ in kind._fields)) for kind in (Sources, Given))
    boards = [next(refs) for _ in range(BLOCKS)]
    outs = [next(refs) for _ in range(8)]
    own = [next(refs) for _ in range(BLOCKS)]
    r, sems = (kind(*(next(refs) for _ in kind._fields)) for kind in (Kept, Signals))
    section = lax.axis_index(SECTION)
    group = lax.axis_index(DP)
    last = sections - 1
    along, beside, line = groups // ACROSS, lax.rem(group, ACROSS), group // ACROSS
    partner = line * ACROSS + (1 - beside)
    micro, tokens, width = r.arrived.shape
    inner = r.up.shape[1]
    embed = r.part.shape[2]
    slots = given.member.shape[1]
    height, padded = heights
    head_size = width // HEADS
    scale = head_size ** (-0.5)
    logit_scale = embed ** (-0.5)
    pair = 2 * head_size
    lane = lax.broadcasted_iota(jnp.int32, (tokens, pair), 1)
    low = jnp.bfloat16

    loads = [
        pltpu.make_async_copy(source, target, sems.load.at[index])
        for index, (source, target) in enumerate(
            zip(sources, (r.table, r.qkv, r.out, r.up, r.down))
        )
    ]
    load_table, load_qkv, load_out, load_up, load_down = loads
    for load in (load_table, load_qkv, load_out):
        load.start()

    def section_peer(step):
        return lax.rem(section + step, sections)

    def line_peer(step):
        return lax.rem(line + step, along)

    def group_peer(step):
        return lax.rem(group + step, groups)

    barrier = pltpu.get_barrier_semaphore()
    for step in range(1, sections):
        pl.semaphore_signal(
            barrier, inc=1, device_id={SECTION: section_peer(step)}, device_id_type=MESH
        )
    for step in range(1, groups):
        pl.semaphore_signal(
            barrier, inc=1, device_id={DP: group_peer(step)}, device_id_type=MESH
        )
    for step in range(1, sections):
        pl.semaphore_signal(
            barrier,
            inc=1,
            device_id={SECTION: section_peer(step), DP: partner},
            device_id_type=MESH,
        )
    pl.semaphore_wait(barrier, 2 * sections + groups - 3)

    def sent(source, target, to, send_sem, recv_sem, axis=SECTION):
        return pltpu.make_async_remote_copy(
            src_ref=source,
            dst_ref=target,
            send_sem=send_sem,
            recv_sem=recv_sem,
            device_id={axis: to},
            device_id_type=MESH,
        )

    def place(name, slot):
        board = boards[name]
        if name < PER_SLOT:
            index, mine = name * micro + slot, own[name].at[slot]
        else:
            index, mine = PER_SLOT * micro + name - PER_SLOT, own[name]
        if name < WIDE:
            return index, mine, lambda at: board.at[at, slot]
        if name < PER_SLOT:
            return index, mine, lambda at: board.at[at, beside, slot]
        return index, mine, lambda at: board.at[at, beside]

    relayed = along == 4
    count = PER_SLOT * micro + BLOCKS - PER_SLOT
    early = section < sections // 2
    at_end = (line == 0) | (line == along - 1)

    def slots_of(name):
        if name == ATTN:
            return micro - 1
        return micro if name < PER_SLOT else 1

    def spread(name, slot=0):
        index, mine, at = place(name, slot)
        here = at(line)
        pltpu.make_async_copy(mine, here, sems.keep.at[index]).start()
        for step in range(1, along):
            peer = line_peer(step)
            to = peer * ACROSS + beside
            if name < WIDE and relayed:
                far = (at_end & (jnp.abs(line - peer) == 2)).astype(jnp.int32)

                @pl.when(jnp.abs(line - peer) < 3)
                def _():
                    arrival = sems.line.at[far * count + index]
                    sent(mine, here, to, sems.out.at[index], arrival, DP).start()

            else:
                sent(mine, here, to, sems.out.at[index], sems.line.at[index], DP).start()
        if name >= WIDE:
            sent(mine, here, partner, sems.out.at[index], sems.pair.at[index], DP).start()

    def relay_copy(name, slot):
        index, mine, at = place(name, slot)
        there = at(jnp.where(line == 1, along - 1, 0))
        to = jnp.where(line == 1, 0, along - 1) * ACROSS + beside
        return sent(there, there, to, sems.relay.at[index], sems.line.at[index], DP)

    def relay(name, slot):
        if relayed:
            index, mine, at = place(name, slot)

            @pl.when(jnp.logical_not(at_end))
            def _():
                wait_blocks(at(pl.ds(0, 1)), sems.line.at[count + index])
                relay_copy(name, slot).start()

    def wait_blocks(ref, sem):
        pltpu.make_async_copy(ref, ref, sem).wait()

    def forward(name, slot=0):
        index, mine, at = place(name, slot)
        wait_blocks(at(pl.ds(0, along - 1)), sems.line.at[index])
        for step in range(1, along):
            there = at(line_peer(step))
            sent(there, there, partner, sems.beside.at[index], sems.pair.at[index], DP).start()

    def settle(name, slot=0):
        index, mine, at = place(name, slot)
        pltpu.make_async_copy(mine, at(line), sems.keep.at[index]).wait()
        if name < WIDE and relayed:

            @pl.when(at_end)
            def _():
                wait_blocks(at(pl.ds(0, 2)), sems.out.at[index])
                wait_blocks(at(pl.ds(0, 3)), sems.line.at[index])

            @pl.when(jnp.logical_not(at_end))
            def _():
                wait_blocks(at(pl.ds(0, 3)), sems.out.at[index])
                wait_blocks(at(pl.ds(0, 2)), sems.line.at[index])
                relay_copy(name, slot).wait_send()

        elif name < WIDE:
            wait_blocks(at(pl.ds(0, along - 1)), sems.out.at[index])
            wait_blocks(at(pl.ds(0, along - 1)), sems.line.at[index])
        else:
            wait_blocks(at(pl.ds(0, along)), sems.out.at[index])
            wait_blocks(at(pl.ds(0, along - 1)), sems.beside.at[index])
            wait_blocks(at(pl.ds(0, along)), sems.pair.at[index])

    def passed_on(slot):
        to = jnp.minimum(section + 1, last)
        return sent(
            r.final.at[slot],
            r.arrived.at[slot],
            to,
            sems.on_send.at[slot],
            sems.on_recv.at[slot],
        )

    def passed_back(slot):
        to = jnp.maximum(section - 1, 0)
        return sent(
            r.leaving.at[slot],
            r.returned.at[slot],
            to,
            sems.back_send.at[slot],
            sems.back_recv.at[slot],
        )

    def to_head(source, target, section_to, group_to, send_sem, recv_sem):
        return pltpu.make_async_remote_copy(
            src_ref=source,
            dst_ref=target,
            send_sem=send_sem,
            recv_sem=recv_sem,
            device_id={SECTION: section_to, DP: group_to},
            device_id_type=MESH,
        )

    me = section * ACROSS + beside

    def latent_to(slot, step):
        ref = own[LATENT].at[slot]
        sem = sems.latent_send.at[slot * sections + step]
        return sent(ref, ref, section_peer(step), sem, sems.latent_recv.at[slot])

    def latent_over(slot, step):
        sem = sems.other_send.at[slot * sections + step]
        return to_head(
            own[LATENT].at[slot],
            r.other.at[slot],
            section_peer(step),
            partner,
            sem,
            sems.other_recv.at[slot],
        )

    def shares_to(slot, side):
        to = partner if side else group
        sem = slot * ACROSS + side
        return (
            to_head(
                r.mine.at[side, slot],
                r.pulled.at[me, slot],
                last,
                to,
                sems.pulled_send.at[sem],
                sems.pulled_recv.at[slot * ACROSS * sections + me],
            ),
            to_head(
                r.mine_stats.at[side, slot],
                r.stats.at[me, slot],
                last,
                to,
                sems.stats_send.at[sem],
                sems.stats_recv.at[slot * ACROSS * sections + me],
            ),
        )

    def shares_from(slot, source):
        sem = slot * ACROSS * sections + source
        return tuple(
            to_head(store.at[source, slot], store.at[source, slot], last, partner, send, recv)
            for store, send, recv in (
                (r.pulled, sems.pulled_send.at[slot], sems.pulled_recv.at[sem]),
                (r.stats, sems.stats_send.at[slot], sems.stats_recv.at[sem]),
            )
        )

    def log_to(slot, step):
        ref = own[LOG_TOTAL].at[slot]
        sem = sems.log_send.at[slot * sections + step]
        return sent(ref, ref, section_peer(step), sem, sems.log_recv.at[slot])

    def end_to(step):
        to = section_peer(step)
        return sent(
            r.end_parts.at[to], r.end_own, to, sems.end_send.at[step], sems.end_recv
        )

    def start_to(step):
        to = section_peer(step)
        return sent(
            r.start_parts.at[to], r.start_own, to, sems.start_send.at[step], sems.start_recv
        )

    def mixed_to(slot, step):
        ref = r.mixed_grad.at[slot]
        return sent(
            ref,
            ref,
            section_peer(step),
            sems.mixed_send.at[slot * sections + step],
            sems.mixed_recv.at[slot],
        )

    def ints_to(step):
        ref = r.ints.at[group]
        return sent(
            ref, ref, group_peer(step), sems.ints_send.at[step], sems.ints_recv.at[group], DP
        )

    def ints_from(step):
        source = group_peer(step)
        ref = r.ints.at[source]
        return sent(ref, ref, source, sems.ints_send.at[step], sems.ints_recv.at[source], DP)

    def leaving_rows(peer, stage):
        at = stage * along + peer
        high = r.up.shape[0] // (micro * tokens)
        first = pl.multiple_of(lax.rem(at, high) * (micro * tokens), micro * tokens)
        column = pl.multiple_of(at // high * embed, embed)
        return r.up.at[pl.ds(first, micro * tokens), pl.ds(column, embed)]

    def arriving_rows(peer, stage):
        at = stage * along + peer
        wide = r.down.shape[1] // embed
        first = pl.multiple_of(at // wide * (micro * tokens), micro * tokens)
        column = pl.multiple_of(lax.rem(at, wide) * embed, embed)
        return r.down.at[pl.ds(first, micro * tokens), pl.ds(column, embed)]

    def rows_across(step):
        peer = line_peer(step)
        return sent(
            leaving_rows(peer, 0),
            arriving_rows(peer, 0),
            partner,
            sems.rows_send.at[step],
            sems.rows_recv.at[peer],
            DP,
        )

    def rows_along(step):
        peer = line_peer(step)
        return sent(
            leaving_rows(peer, 1),
            arriving_rows(line, 1),
            peer * ACROSS + beside,
            sems.rows_send.at[along + step],
            sems.rows_recv.at[along + line],
            DP,
        )

    def rows_from(step):
        source = line_peer(step)
        ref = arriving_rows(source, 1)
        sem = along + source
        return sent(ref, ref, partner, sems.rows_send.at[sem], sems.rows_recv.at[sem], DP)

    def parts_to(step):
        ref = r.rows_parts.at[section]
        return sent(
            ref, ref, section_peer(step), sems.parts_send.at[step], sems.parts_recv.at[section]
        )

    def parts_from(step):
        source = section_peer(step)
        ref = r.rows_parts.at[source]
        return sent(ref, ref, source, sems.parts_send.at[step], sems.parts_recv.at[source])

    def table_to(step):
        to = line_peer(step) * ACROSS + beside
        return sent(
            r.table, r.part.at[line], to, sems.table_send.at[step], sems.table_recv.at[line], DP
        )

    def table_settle():
        for step in range(1, along):
            peer = line_peer(step)
            ref = r.part.at[peer]
            sent(
                ref, ref, partner, sems.table_send.at[step], sems.table_recv.at[peer], DP
            ).wait_recv()

    def looked_up(owner):
        ids = r.ints[owner]
        base = (section * groups + group) * height
        column = lax.broadcasted_iota(jnp.int32, (micro * tokens, padded), 1)
        spots = []
        for slot in range(micro):
            wide = jnp.broadcast_to(ids[slot : slot + 1, :tokens], (tokens, tokens))
            spots.append(jnp.transpose(wide.astype(jnp.float32))[:, 0:1])
        at = jnp.concatenate(spots, axis=0).astype(jnp.int32) - base
        at = jnp.where(at < height, at, -1)
        hit = (column == at).astype(jnp.float32).astype(low)
        return dot(hit, r.table[...]).astype(low)

    def front():
        r.ints[group] = given.ints[...]
        for step in range(1, groups):
            ints_to(step).start()
        load_table.wait()
        steps = [*range(1, along), 0]
        for step in range(1, groups):
            ints_from(step).wait_recv()
        for step in steps:
            peer = line_peer(step)
            leaving_rows(peer, 0)[...] = looked_up(peer * ACROSS + (1 - beside))
            rows_across(step).start()
            leaving_rows(peer, 1)[...] = looked_up(peer * ACROSS + beside)
        for step in steps:
            peer = line_peer(step)
            rows_across(step).wait_recv()
            both = leaving_rows(peer, 1)[...].astype(jnp.float32)
            both = both + arriving_rows(peer, 0)[...].astype(jnp.float32)
            if step:
                leaving_rows(peer, 1)[...] = both.astype(low)
                rows_along(step).start()
        total = both
        for step in range(1, along):
            rows_from(step).wait_recv()
            total = total + arriving_rows(line_peer(step), 1)[...].astype(jnp.float32)
        load_down.start()
        r.rows_parts[section] = total.astype(low)
        for step in range(1, sections):
            parts_to(step).start()
        for step in steps:
            rows_across(step).wait_send()
            if step:
                rows_along(step).wait_send()
        load_up.start()
        for step in range(1, along):
            table_to(step).start()
        r.part[line] = r.table[...]
        for step in range(1, sections):
            parts_from(step).wait_recv()
            total = total + r.rows_parts[section_peer(step)].astype(jnp.float32)
        r.rows[...] = total.astype(low).reshape(micro, tokens, embed)

        @pl.when(section == 0)
        def _():
            for slot in range(micro):
                rows = r.rows[slot].astype(jnp.float32)
                mixed = rows + given.amount[slot] * given.noise[slot].astype(jnp.float32)
                mixed = (mixed * given.shrink[slot]).astype(low)
                r.mixed[slot] = mixed
                r.arrived[slot] = dot(mixed, given.in_proj[...]) + given.norms[6:7]

    def layer_on(slot):
        @pl.when(section > 0)
        def _():
            passed_on(slot).wait_recv()

        current = r.arrived[slot] + given.timed[slot]
        r.current[slot] = current
        normed = (normal(current)[0] * given.norms[0:1] + given.norms[1:2]).astype(low)
        own[NORMED][slot] = normed
        if slot == 0:
            load_qkv.wait()
        for at in range(0, 3 * width, PACK_CHUNK):
            r.raw[:, at : at + PACK_CHUNK] = dot(normed, r.qkv[:, at : at + PACK_CHUNK])

        @pl.when(jnp.logical_not(early))
        def _():
            spread(NORMED, slot)

        for at in range(0, width, pair):
            turned = []
            for kind in range(2):
                raw = r.raw[:, kind * width + at : kind * width + at + pair]
                raw = raw * given.cosine[slot] + halves_swapped(raw, head_size, lane) * given.sine[slot]
                raw = raw.astype(low)
                r.packed[slot, :, kind * width + at : kind * width + at + pair] = raw
                turned.append(raw)
            values = r.raw[:, 2 * width + at : 2 * width + at + pair].astype(low)
            r.packed[slot, :, 2 * width + at : 2 * width + at + pair] = values
            scores = dot_right(turned[0], apart(turned[1], lane, head_size)) * scale
            sides = []
            for side in range(2):
                part = scores[:, side * tokens : (side + 1) * tokens] + given.mask[slot]
                raised = jnp.exp(part - jnp.max(part, axis=-1, keepdims=True))
                sides.append(raised / jnp.sum(raised, axis=-1, keepdims=True))
            probs = jnp.concatenate(sides, axis=1)
            r.probs[slot, at // pair] = probs
            r.narrow[:, at : at + pair] = dot(
                probs.astype(low), apart(values, lane, head_size)
            ).astype(low)
        if slot == 0:
            load_out.wait()
        after = current + dot(r.narrow[...], r.out[...])
        r.after[slot] = after
        normed_mlp = (normal(after)[0] * given.norms[2:3] + given.norms[3:4]).astype(low)
        own[MLP][slot] = normed_mlp

        @pl.when(jnp.logical_not(early))
        def _():
            spread(MLP, slot)

        if slot == 0:
            load_up.wait()
            load_down.wait()
        total = after
        for at in range(0, inner, FF_CHUNK):
            pre_act = dot(normed_mlp, r.up[:, at : at + FF_CHUNK])
            below = 0.5 + 0.5 * lax.erf(pre_act * 0.5**0.5)
            bell = jnp.exp(-0.5 * pre_act * pre_act) * (0.5 / jnp.pi) ** 0.5
            r.slope[slot, :, at : at + FF_CHUNK] = below + pre_act * bell
            activated = (pre_act * below).astype(low)
            total = total + dot(activated, r.down[at : at + FF_CHUNK, :])
        r.final[slot] = total

        @pl.when(section < last)
        def _():
            passed_on(slot).start()

        @pl.when(section == last)
        def _():
            final = (normal(total)[0] * given.norms[4:5] + given.norms[5:6]).astype(low)
            r.final_low[slot] = final
            own[LATENT][slot] = dot(final, given.out_proj[...]).astype(low)
            for step in range(sections):
                if step:
                    latent_to(slot, step).start()
                latent_over(slot, step).start()

    def vocabulary(slot):
        @pl.when(section < last)
        def _():
            latent_to(slot, 1).wait_recv()

        latent_over(slot, 1).wait_recv()
        both = jnp.concatenate([own[LATENT][slot], r.other[slot]], axis=0)
        top = jnp.full((ACROSS * tokens, 1), mask_fill, jnp.float32)
        mass = jnp.zeros((ACROSS * tokens, 1), jnp.float32)
        pulled = jnp.zeros((ACROSS * tokens, embed), jnp.float32)
        shards = ROW_CHUNK // padded
        for at in range(0, along, shards):
            rows = r.part[at : at + shards].reshape(ROW_CHUNK, embed)
            logits = dot_right(both, rows) * logit_scale + given.padding[0:1]
            best = jnp.maximum(top, jnp.max(logits, axis=-1, keepdims=True))
            raised = jnp.exp(logits - best)
            fade = jnp.exp(top - best)
            mass = mass * fade + jnp.sum(raised, axis=-1, keepdims=True)
            pulled = pulled * fade + dot(raised.astype(low), rows)
            top = best
        for side in range(ACROSS):
            rows = slice(side * tokens, (side + 1) * tokens)
            r.mine[side, slot] = pulled[rows].astype(low)
            r.mine_stats[side, slot] = jnp.where(lane < LANES // 2, top[rows], mass[rows])
        for copy in shares_to(slot, 1):
            copy.start()

        @pl.when(section < last)
        def _():
            for copy in shares_to(slot, 0):
                copy.start()

    def combine(slot):
        @pl.when(section == last)
        def _():
            sources = [lax.rem(me + step, ACROSS * sections) for step in range(1, ACROSS * sections)]
            for source in sources:
                for copy in shares_from(slot, source):
                    copy.wait_recv()
            stats = [r.mine_stats[0, slot]] + [r.stats[source, slot] for source in sources]
            best = stats[0][:, 0:1]
            for item in stats[1:]:
                best = jnp.maximum(best, item[:, 0:1])
            shares = [jnp.exp(item[:, 0:1] - best) for item in stats]
            total = sum(
                share * item[:, LANES // 2 : LANES // 2 + 1] for share, item in zip(shares, stats)
            )
            pulled = [r.mine[0, slot]] + [r.pulled[source, slot] for source in sources]
            mean = sum(
                share / total * item.astype(jnp.float32) for share, item in zip(shares, pulled)
            )
            row = r.rows[slot].astype(jnp.float32)
            grad_latent = ((mean - row) * (logit_scale * given.weight[slot])).astype(low)
            r.grad_latent[slot] = grad_latent
            grads = dot_right(grad_latent, given.out_proj[...])
            unit, inverse = normal(r.final[slot])
            r.upstream[...] = normal_back(grads, given.norms[4:5], unit, inverse)
            gain = jnp.sum(grads * unit, axis=0, keepdims=True)
            bias = jnp.sum(grads, axis=0, keepdims=True)
            if slot == 0:
                r.end_rows[0:1] = gain
                r.end_rows[1:2] = bias
            else:
                r.end_rows[0:1] += gain
                r.end_rows[1:2] += bias
            log_total = best + jnp.log(total)
            picked = own[LATENT][slot].astype(jnp.float32) * row
            picked = jnp.sum(picked, axis=-1, keepdims=True) * logit_scale
            loss = given.weight[slot] * (log_total - picked)
            turned = jnp.transpose(jnp.where(lane < LANES // 2, log_total, loss))
            own[LOG_TOTAL][slot, 0:4] = turned[0:4]
            own[LOG_TOTAL][slot, 4:8] = turned[LANES // 2 : LANES // 2 + 4]
            for step in range(1, sections):
                log_to(slot, step).start()

        @pl.when(section < last)
        def _():
            passed_back(slot).wait_recv()
            r.upstream[...] = r.returned[slot].astype(jnp.float32)

    def together(rows):
        return jnp.where(lane < head_size, rows[:tokens], rows[tokens:])

    def turned_back(grads, slot):
        return grads * given.cosine[slot] - halves_swapped(grads, head_size, lane) * given.sine[slot]

    def layer_back(slot):
        upstream = r.upstream[...]
        branch = upstream.astype(low)
        own[BRANCH][slot] = branch
        spread(BRANCH, slot)
        grads = jnp.zeros((tokens, width), jnp.float32)
        for at in range(0, inner, FF_CHUNK):
            grad_act = dot_right(branch, r.down[at : at + FF_CHUNK, :])
            grad_pre = (r.slope[slot, :, at : at + FF_CHUNK] * grad_act).astype(low)
            grads = grads + dot_right(grad_pre, r.up[:, at : at + FF_CHUNK])
        unit, inverse = normal(r.after[slot])
        gain_two = jnp.sum(grads * unit, axis=0, keepdims=True)
        bias_two = jnp.sum(grads, axis=0, keepdims=True)
        grad_after = upstream + normal_back(grads, given.norms[2:3], unit, inverse)
        attn_branch = grad_after.astype(low)
        own[ATTN][slot] = attn_branch
        if slot < micro - 1:
            spread(ATTN, slot)
        r.narrow[...] = dot_right(attn_branch, r.out[...]).astype(low)
        for at in range(0, width, pair):
            queries = r.packed[slot, :, at : at + pair]
            keys = r.packed[slot, :, width + at : width + at + pair]
            values = r.packed[slot, :, 2 * width + at : 2 * width + at + pair]
            grad_here = r.narrow[:, at : at + pair]
            probs = r.probs[slot, at // pair]
            grad_prob = dot_right(grad_here, apart(values, lane, head_size))
            sides = []
            for side in range(2):
                here = probs[:, side * tokens : (side + 1) * tokens]
                there = grad_prob[:, side * tokens : (side + 1) * tokens]
                mean = jnp.sum(here * there, axis=-1, keepdims=True)
                sides.append(here * (there - mean))
            grad_score = jnp.concatenate(sides, axis=1).astype(low)
            grad_query = dot(grad_score, apart(keys, lane, head_size)) * scale
            grad_key = together(dot_left(grad_score, queries)) * scale
            grad_value = together(dot_left(probs.astype(low), grad_here))
            for kind, grad in enumerate(
                (turned_back(grad_query, slot), turned_back(grad_key, slot), grad_value)
            ):
                r.grad_packed[:, kind * width + at : kind * width + at + pair] = grad.astype(low)
        grads = jnp.zeros((tokens, width), jnp.float32)
        for at in range(0, 3 * width, PACK_CHUNK):
            grads = grads + dot_right(
                r.grad_packed[:, at : at + PACK_CHUNK], r.qkv[:, at : at + PACK_CHUNK]
            )
        unit, inverse = normal(r.current[slot])
        gain_one = jnp.sum(grads * unit, axis=0, keepdims=True)
        bias_one = jnp.sum(grads, axis=0, keepdims=True)
        grad_current = grad_after + normal_back(grads, given.norms[0:1], unit, inverse)
        leaving = grad_current.astype(low)
        r.leaving[slot] = leaving

        @pl.when(section > 0)
        def _():
            passed_back(slot).start()

        r.seq[slot * slots : (slot + 1) * slots] = lax.dot_general(
            given.member[slot],
            grad_current,
            (((1,), (0,)), ((), ())),
            precision=lax.Precision.HIGHEST,
            preferred_element_type=jnp.float32,
        )
        for index, row in enumerate((gain_one, bias_one, gain_two, bias_two)):
            if slot == 0:
                r.norm_rows[index : index + 1] = row
            else:
                r.norm_rows[index : index + 1] += row

        @pl.when(section == 0)
        def _():
            moved = dot_right(leaving, given.in_proj[...]) * given.shrink[slot]
            r.mixed_grad[slot] = moved.astype(low)
            for step in range(1, sections):
                mixed_to(slot, step).start()
            column = jnp.sum(grad_current, axis=0, keepdims=True)
            if slot == 0:
                r.start_row[...] = column
            else:
                r.start_row[...] += column

    r.norm_rows[...] = jnp.zeros_like(r.norm_rows)
    r.seq[...] = jnp.zeros_like(r.seq)
    r.end_rows[...] = jnp.zeros_like(r.end_rows)
    own[FEATURES][...] = given.features[...]
    front()
    spread(FEATURES)

    layer_on(0)
    for slot in range(1, micro):
        layer_on(slot)

    def spread_all(*names):
        for name in names:
            for slot in range(slots_of(name)):
                spread(name, slot)

    def relay_all(*names):
        for name in names:
            for slot in range(slots_of(name)):
                relay(name, slot)

    @pl.when(early)
    def _():
        spread_all(NORMED, MLP)

    table_settle()
    vocabulary(0)

    @pl.when(section < last)
    def _():
        for slot in range(1, micro):
            vocabulary(slot)

    @pl.when(early)
    def _():
        relay_all(NORMED)

    for slot in range(micro):
        if slot > 0:

            @pl.when(section == last)
            def _():
                vocabulary(slot)

        combine(slot)
        spread(LATENT, slot)

        @pl.when(section < last)
        def _():
            log_to(slot, 1).wait_recv()

        spread(LOG_TOTAL, slot)
        layer_back(slot)
        if slot == 0:

            @pl.when(early)
            def _():
                relay_all(MLP)

    @pl.when(jnp.logical_not(early))
    def _():
        relay_all(NORMED, MLP)

    @pl.when(section == last)
    def _():
        grads = sum(dot_left(r.final_low[slot], r.grad_latent[slot]) for slot in range(micro))
        tall = width // sections
        r.end_parts[...] = jnp.zeros_like(r.end_parts)
        for to in range(sections):
            r.end_parts[to, :tall, :] = grads[to * tall : (to + 1) * tall].astype(low)
            rows = r.end_rows[:, to * tall : (to + 1) * tall]
            r.end_parts[to, tall : tall + 8, :embed] = rows[:, :embed].astype(low)
        for step in range(1, sections):
            end_to(step).start()
        r.end_own[...] = r.end_parts[last]

    @pl.when(section == 0)
    def _():
        grads = sum(dot_left(r.mixed[slot], r.leaving[slot]) for slot in range(micro))
        tall = embed // sections
        r.start_parts[...] = jnp.zeros_like(r.start_parts)
        for to in range(sections):
            r.start_parts[to, :tall, :] = grads[to * tall : (to + 1) * tall].astype(low)
            r.start_parts[to, tall : tall + 8, :] = jnp.broadcast_to(
                r.start_row[...], (8, width)
            ).astype(low)
        for step in range(1, sections):
            start_to(step).start()
        r.start_own[...] = r.start_parts[0]

    r.seq_rows[...] = r.seq[...].astype(low)
    relay_all(BRANCH, ATTN)
    for slot in range(micro):
        forward(LATENT, slot)
        forward(LOG_TOTAL, slot)
    forward(FEATURES)

    @pl.when(section < last)
    def _():
        end_to(1).wait_recv()

    @pl.when(section > 0)
    def _():
        for slot in range(micro):
            mixed_to(slot, 1).wait_recv()
        start_to(1).wait_recv()

    results = (
        r.end_own,
        r.start_own,
        r.ints,
        own[LOG_TOTAL],
        own[ATTN].at[micro - 1],
        r.mixed_grad,
        r.norm_rows,
        r.seq_rows,
    )
    keeps = [
        pltpu.make_async_copy(source, target, sems.ends.at[index])
        for index, (source, target) in enumerate(zip(results, outs))
    ]
    for keep in keeps:
        keep.start()
    for name in range(BLOCKS):
        for slot in range(slots_of(name)):
            settle(name, slot)
    for keep in keeps:
        keep.wait()

    for step in range(1, groups):
        ints_to(step).wait_send()
    for step in range(1, along):
        table_to(step).wait_send()
    for step in range(1, sections):
        parts_to(step).wait_send()
    for slot in range(micro):
        for copy in shares_to(slot, 1):
            copy.wait_send()

        @pl.when(section < last)
        def _():
            passed_on(slot).wait_send()
            for copy in shares_to(slot, 0):
                copy.wait_send()

        @pl.when(section > 0)
        def _():
            passed_back(slot).wait_send()

        @pl.when(section == last)
        def _():
            for step in range(sections):
                if step:
                    latent_to(slot, step).wait_send()
                    log_to(slot, step).wait_send()
                latent_over(slot, step).wait_send()

    @pl.when(section == last)
    def _():
        for step in range(1, sections):
            end_to(step).wait_send()

    @pl.when(section == 0)
    def _():
        for step in range(1, sections):
            for slot in range(micro):
                mixed_to(slot, step).wait_send()
            start_to(step).wait_send()


def run_chain(sources, given, sections, groups, heights):
    f32, low = jnp.float32, jnp.bfloat16
    micro, tokens, width = given.timed.shape
    inner = sources.up.shape[1]
    padded = heights[1]
    embed = given.out_proj.shape[1]
    slots = given.member.shape[1]
    lines = groups // ACROSS
    vmem = pl.BlockSpec(memory_space=pltpu.VMEM)
    anywhere = pl.BlockSpec(memory_space=pl.ANY)
    seq = -(-micro * slots // 16) * 16
    shape = jax.ShapeDtypeStruct
    blocks = (
        shape((micro, tokens, width), low),
        shape((micro, tokens, width), low),
        shape((micro, tokens, width), low),
        shape((micro, tokens, width), low),
        shape((micro, tokens, embed), low),
        shape((micro, 8, LANES), f32),
        shape(given.features.shape, low),
    )
    end = shape((width // sections + 16, embed), low)
    start = shape((embed // sections + 16, width), low)
    dma = pltpu.SemaphoreType.DMA
    count = PER_SLOT * micro + BLOCKS - PER_SLOT
    pairs = micro * sections
    kept = Kept(
        *(pltpu.VMEM(source.shape, low) for source in sources),
        part=pltpu.VMEM((lines, padded, embed), low),
        ints=pltpu.VMEM((groups, *given.ints.shape), jnp.int32),
        rows_parts=pltpu.VMEM((sections, micro * tokens, embed), low),
        rows=pltpu.VMEM((micro, tokens, embed), low),
        mixed=pltpu.VMEM((micro, tokens, embed), low),
        other=pltpu.VMEM((micro, tokens, embed), low),
        mine=pltpu.VMEM((ACROSS, micro, tokens, embed), low),
        mine_stats=pltpu.VMEM((ACROSS, micro, tokens, LANES), f32),
        arrived=pltpu.VMEM((micro, tokens, width), f32),
        final=pltpu.VMEM((micro, tokens, width), f32),
        final_low=pltpu.VMEM((micro, tokens, width), low),
        raw=pltpu.VMEM((tokens, 3 * width), f32),
        narrow=pltpu.VMEM((tokens, width), low),
        grad_packed=pltpu.VMEM((tokens, 3 * width), low),
        current=pltpu.VMEM((micro, tokens, width), f32),
        after=pltpu.VMEM((micro, tokens, width), f32),
        packed=pltpu.VMEM((micro, tokens, 3 * width), low),
        probs=pltpu.VMEM((micro, HEADS // 2, tokens, 2 * tokens), f32),
        slope=pltpu.VMEM((micro, tokens, inner), f32),
        leaving=pltpu.VMEM((micro, tokens, width), low),
        returned=pltpu.VMEM((micro, tokens, width), low),
        upstream=pltpu.VMEM((tokens, width), f32),
        stats=pltpu.VMEM((ACROSS * sections, micro, tokens, LANES), f32),
        pulled=pltpu.VMEM((ACROSS * sections, micro, tokens, embed), low),
        grad_latent=pltpu.VMEM((micro, tokens, embed), low),
        seq=pltpu.VMEM((seq, width), f32),
        mixed_grad=pltpu.VMEM((micro, tokens, embed), low),
        norm_rows=pltpu.VMEM((8, width), f32),
        seq_rows=pltpu.VMEM((seq, width), low),
        end_rows=pltpu.VMEM((8, width), f32),
        end_parts=pltpu.VMEM((sections, *end.shape), low),
        end_own=pltpu.VMEM(end.shape, low),
        start_row=pltpu.VMEM((1, width), f32),
        start_parts=pltpu.VMEM((sections, *start.shape), low),
        start_own=pltpu.VMEM(start.shape, low),
    )
    signals = Signals(
        load=dma((len(sources),)),
        keep=dma((count,)),
        out=dma((count,)),
        line=dma((2 * count,)),
        beside=dma((count,)),
        pair=dma((count,)),
        relay=dma((count,)),
        ints_send=dma((groups,)),
        ints_recv=dma((groups,)),
        rows_send=dma((groups,)),
        rows_recv=dma((groups,)),
        parts_send=dma((sections,)),
        parts_recv=dma((sections,)),
        table_send=dma((lines,)),
        table_recv=dma((lines,)),
        other_send=dma((pairs,)),
        other_recv=dma((micro,)),
        log_send=dma((pairs,)),
        log_recv=dma((micro,)),
        on_send=dma((micro,)),
        on_recv=dma((micro,)),
        back_send=dma((micro,)),
        back_recv=dma((micro,)),
        latent_send=dma((pairs,)),
        latent_recv=dma((micro,)),
        stats_send=dma((micro * ACROSS,)),
        stats_recv=dma((pairs * ACROSS,)),
        pulled_send=dma((micro * ACROSS,)),
        pulled_recv=dma((pairs * ACROSS,)),
        end_send=dma((sections,)),
        end_recv=dma,
        start_send=dma((sections,)),
        start_recv=dma,
        mixed_send=dma((pairs,)),
        mixed_recv=dma((micro,)),
        ends=dma((8,)),
    )
    boards = tuple(
        shape(
            (
                lines,
                *((ACROSS,) if at >= WIDE else ()),
                *((micro - 1, tokens, width) if at == ATTN else block.shape),
            ),
            block.dtype,
        )
        for at, block in enumerate(blocks)
    )
    outs = pl.pallas_call(
        partial(chain_kernel, sections, groups, heights),
        out_shape=(
            *boards,
            end,
            start,
            shape((groups, *given.ints.shape), jnp.int32),
            shape((micro, 8, LANES), f32),
            shape((tokens, width), low),
            shape((micro, tokens, embed), low),
            shape((8, width), f32),
            shape((seq, width), low),
        ),
        in_specs=[anywhere] * len(sources) + [vmem] * len(given),
        out_specs=(anywhere,) * (BLOCKS + 8),
        scratch_shapes=(
            *(pltpu.VMEM(block.shape, block.dtype) for block in blocks),
            *kept,
            *signals,
        ),
        compiler_params=pltpu.CompilerParams(
            collective_id=1, has_side_effects=True, vmem_limit_bytes=VMEM_BYTES
        ),
        cost_estimate=pl.CostEstimate(
            flops=10**11, bytes_accessed=6 * 10**8, transcendentals=10**7
        ),
        name="chain",
    )(*sources, *given)
    return outs[:BLOCKS], outs[BLOCKS:]


class Given2(NamedTuple):
    ints: Any
    log_total: Any
    turns: Any
    end: Any
    start: Any
    features: Any
    mixed: Any
    norm_rows: Any
    seq_rows: Any


class Results(NamedTuple):
    qkv: Any
    out: Any
    up: Any
    down: Any
    table: Any
    end: Any
    start: Any
    time: Any
    norms: Any


class Parts(NamedTuple):
    normed: Any
    mlp: Any
    branch: Any
    attn: Any
    qkv: Any
    out: Any
    up: Any
    down: Any
    raw: Any
    grad_att: Any
    attended: Any
    grad_packed: Any
    up_whole: Any
    up_sum: Any
    down_sum: Any
    qkv_sum: Any
    out_sum: Any
    up_send: Any
    up_recv: Any
    down_send: Any
    down_recv: Any
    qkv_send: Any
    qkv_recv: Any
    out_send: Any
    out_recv: Any
    up_leave: Any
    up_arrive: Any
    qkv_leave: Any
    qkv_arrive: Any
    table: Any
    latent: Any
    mixed: Any
    norm_rows: Any
    seq_rows: Any
    end_recv: Any
    start_recv: Any
    end_line: Any
    start_line: Any
    time: Any


class Flags(NamedTuple):
    load: Any
    keep: Any
    late_send: Any
    late_recv: Any
    relay: Any
    narrow_send: Any
    narrow_line: Any
    narrow_beside: Any
    narrow_pair: Any
    pair_send: Any
    pair_recv: Any
    up_send: Any
    up_recv: Any
    qkv_send: Any
    qkv_recv: Any
    ends_send: Any
    end_recv: Any
    start_recv: Any


HBM_INPUTS = 11


def segments(lengths, slots):
    at = lax.broadcasted_iota(jnp.int32, lengths.shape, 1)
    end = lengths[:, 0:1]
    sequence = jnp.zeros_like(at)
    first = jnp.zeros_like(at)
    for slot in range(slots):
        passed = at >= end
        sequence = sequence + passed.astype(jnp.int32)
        first = jnp.where(passed, end, first)
        if slot < slots - 1:
            end = end + lengths[:, slot + 1 : slot + 2]
    return sequence, at - first, (at < end).astype(jnp.float32)


def grads_kernel(groups, slots, *refs):
    refs = iter(refs)
    hbm = [next(refs) for _ in range(HBM_INPUTS)]
    given, results, r, sems = (
        kind(*(next(refs) for _ in kind._fields)) for kind in (Given2, Results, Parts, Flags)
    )
    boards, attn_late, weights, (latent, table) = hbm[:4], hbm[4], hbm[5:9], hbm[9:]
    group = lax.axis_index(DP)
    along, beside, line = groups // ACROSS, lax.rem(group, ACROSS), group // ACROSS
    partner = line * ACROSS + (1 - beside)
    theirs = 1 - beside
    low = jnp.bfloat16
    micro, _, tokens, width = r.normed.shape
    last = micro - 1
    half = along * tokens
    chunk = r.up.shape[2]
    quarter = ACROSS * chunk
    cols = r.out.shape[0]
    head_size = width // HEADS
    scale = head_size ** (-0.5)
    pair = 2 * head_size
    lane = lax.broadcasted_iota(jnp.int32, (tokens, pair), 1)

    def part_of(size):
        return pl.ds(pl.multiple_of(line * size, size), size)

    moves = []
    for index, side in enumerate((theirs, beside)):
        half_cols = pl.ds(pl.multiple_of(line * quarter + side * chunk, chunk), chunk)
        moves.append((weights[2].at[:, half_cols], r.up.at[index]))
        moves.append((weights[3].at[half_cols, :], r.down.at[index]))
    for slot in range(micro):
        moves.append((boards[1].at[:, slot], r.mlp.at[slot]))
        moves.append((boards[2].at[:, slot], r.branch.at[slot]))
    ready = len(moves)
    moves.append((weights[1].at[part_of(cols), :], r.out))
    for kind in range(3):
        from_col = pl.multiple_of(kind * width + line * cols, cols)
        moves.append((weights[0].at[:, pl.ds(from_col, cols)], r.qkv.at[:, pl.ds(kind * cols, cols)]))
    for slot in range(micro):
        moves.append((boards[0].at[:, slot], r.normed.at[slot]))
    for slot in range(last):
        moves.append((boards[3].at[:, slot], r.attn.at[slot]))
    moves += [(latent, r.latent), (table, r.table)]
    loads = [
        pltpu.make_async_copy(source, target, sems.load.at[index])
        for index, (source, target) in enumerate(moves)
    ]
    for load in loads:
        load.start()

    def line_peer(step):
        return lax.rem(line + step, along)

    barrier = pltpu.get_barrier_semaphore()
    for step in range(1, along):
        to = line_peer(step) * ACROSS + beside
        pl.semaphore_signal(barrier, inc=1, device_id={DP: to}, device_id_type=MESH)
    pl.semaphore_signal(barrier, inc=1, device_id={DP: partner}, device_id_type=MESH)
    pl.semaphore_wait(barrier, along)

    def sent(source, target, to, send_sem, recv_sem):
        return pltpu.make_async_remote_copy(
            src_ref=source,
            dst_ref=target,
            send_sem=send_sem,
            recv_sem=recv_sem,
            device_id={DP: to},
            device_id_type=MESH,
        )

    relayed = along == 4
    at_end = (line == 0) | (line == along - 1)
    late = r.attn.at[last]
    keep = pltpu.make_async_copy(attn_late, late.at[line], sems.keep)
    keep.start()
    for step in range(1, along):
        peer = line_peer(step)
        far = 0
        if relayed:
            far = (at_end & (jnp.abs(line - peer) == 2)).astype(jnp.int32)
        copy = sent(
            attn_late,
            late.at[line],
            peer * ACROSS + beside,
            sems.late_send,
            sems.late_recv.at[far],
        )
        if relayed:
            pl.when(jnp.abs(line - peer) < 3)(copy.start)
        else:
            copy.start()

    def wait_blocks(ref, sem):
        pltpu.make_async_copy(ref, ref, sem).wait()

    def wait_late(ends, middle, sem):
        if relayed:

            @pl.when(at_end)
            def _():
                wait_blocks(late.at[pl.ds(0, ends)], sem)

            @pl.when(jnp.logical_not(at_end))
            def _():
                wait_blocks(late.at[pl.ds(0, middle)], sem)

        else:
            wait_blocks(late.at[pl.ds(0, along - 1)], sem)

    def relay_copy():
        there = late.at[jnp.where(line == 1, along - 1, 0)]
        to = jnp.where(line == 1, 0, along - 1) * ACROSS + beside
        return sent(there, there, to, sems.relay, sems.late_recv.at[0])

    def relay():
        if relayed:

            @pl.when(jnp.logical_not(at_end))
            def _():
                wait_blocks(late.at[pl.ds(0, 1)], sems.late_recv.at[1])
                relay_copy().start()

    narrow = ((given.mixed, r.mixed), (given.norm_rows, r.norm_rows), (given.seq_rows, r.seq_rows))
    for index, (mine, board) in enumerate(narrow):
        board[line, beside] = mine[...]
        send, pair_sem = sems.narrow_send.at[index], sems.narrow_pair.at[index]
        here = board.at[line, beside]
        for step in range(1, along):
            to = line_peer(step) * ACROSS + beside
            sent(mine, here, to, send, sems.narrow_line.at[index]).start()
        sent(mine, here, partner, send, pair_sem).start()

    def narrow_forward():
        for index, (mine, board) in enumerate(narrow):
            wait_blocks(board.at[pl.ds(0, along - 1), beside], sems.narrow_line.at[index])
            for step in range(1, along):
                there = board.at[line_peer(step), beside]
                send, pair_sem = sems.narrow_beside.at[index], sems.narrow_pair.at[index]
                sent(there, there, partner, send, pair_sem).start()

    def narrow_settle():
        for index, (mine, board) in enumerate(narrow):
            wait_blocks(board.at[pl.ds(0, along), beside], sems.narrow_pair.at[index])

    swaps = [
        sent(source, target, partner, sems.pair_send.at[index], sems.pair_recv.at[index])
        for index, (source, target) in enumerate(
            (
                (r.down_send, r.down_recv),
                (r.up_send.at[0], r.up_recv.at[0]),
                (r.up_send.at[1], r.up_recv.at[1]),
                (r.qkv_send, r.qkv_recv),
                (r.out_send, r.out_recv),
                (given.end, r.end_recv),
                (given.start, r.start_recv),
            )
        )
    ]
    swap_down, swap_up, swap_up_too, swap_qkv, swap_out, swap_end, swap_start = swaps
    swap_end.start()
    swap_start.start()

    def along_line(step, board, send, recv):
        ref = board.at[line]
        to = line_peer(step) * ACROSS + beside
        return sent(ref, ref, to, sems.ends_send.at[send * along + step], recv.at[line])

    def scatter(step, leave, arrive, send, recv):
        to = line_peer(step)
        return sent(leave.at[to], arrive.at[line], to * ACROSS + beside, send.at[step], recv.at[line])

    def gathered(source, arrive, recv):
        ref = arrive.at[source]
        return sent(ref, ref, partner, recv.at[source], recv.at[source])

    def feed_forward(index):
        normed_mlp = r.mlp[...].reshape(micro * half, width)
        branch = r.branch[...].reshape(micro * half, width)
        pre_act = dot(normed_mlp, r.up[index])
        below = 0.5 + 0.5 * lax.erf(pre_act * 0.5**0.5)
        bell = jnp.exp(-0.5 * pre_act * pre_act) * (0.5 / jnp.pi) ** 0.5
        activated = (pre_act * below).astype(low)
        grad_act = dot_right(branch, r.down[index])
        grad_pre = ((below + pre_act * bell) * grad_act).astype(low)
        grad_up = dot_left(normed_mlp, grad_pre)
        r.up_whole[...] = grad_up.reshape(r.up_whole.shape)
        return dot_left(activated, branch)

    def turned(values, turns, sign):
        swapped = halves_swapped(values, head_size, lane) * turns[1]
        return values * turns[0] + (swapped if sign > 0 else -swapped)

    def together(rows):
        return jnp.where(lane < head_size, rows[:tokens], rows[tokens:])

    def bucket_turns(slot, owner):
        lengths = given.ints[owner, 2 * micro + slot : 2 * micro + slot + 1, :]
        sequence, inside, _ = segments(lengths, slots)
        both = jnp.broadcast_to(sequence * LANES + inside, (tokens, LANES)).astype(jnp.float32)
        column = jnp.transpose(both).astype(jnp.int32)
        mask = jnp.where(column // LANES == sequence, 0.0, mask_fill)
        hit = (column % LANES == lane).astype(jnp.float32).astype(low)
        found = dot(hit, given.turns[...])
        wide = 2 * pair
        found = found[:, :wide] + found[:, wide : 2 * wide] + found[:, 2 * wide :]
        return (found[:, :pair], found[:, pair:]), mask

    def attention(slot):
        normed = r.normed[slot].reshape(half, width)
        for at in range(0, 3 * cols, cols):
            r.raw[:, at : at + cols] = dot(normed, r.qkv[:, at : at + cols])
        r.grad_att[...] = dot_right(r.attn[slot].reshape(half, width), r.out[...]).astype(low)

        def one_bucket(peer, carry):
            turns, mask = bucket_turns(slot, peer * ACROSS + beside)
            rows = pl.ds(pl.multiple_of(peer * tokens, tokens), tokens)
            to = pl.ds(pl.multiple_of((slot * along + peer) * tokens, tokens), tokens)
            for at in range(0, cols, pair):
                queries = turned(r.raw[rows, at : at + pair], turns, 1).astype(low)
                keys = turned(r.raw[rows, cols + at : cols + at + pair], turns, 1).astype(low)
                values = r.raw[rows, 2 * cols + at : 2 * cols + at + pair].astype(low)
                grad_here = r.grad_att[rows, at : at + pair]
                keys_apart = apart(keys, lane, head_size)
                values_apart = apart(values, lane, head_size)
                scores = dot_right(queries, keys_apart) * scale
                grad_prob = dot_right(grad_here, values_apart)
                probs, grad_score = [], []
                for side in range(2):
                    part = scores[:, side * tokens : (side + 1) * tokens] + mask
                    raised = jnp.exp(part - jnp.max(part, axis=-1, keepdims=True))
                    here = raised / jnp.sum(raised, axis=-1, keepdims=True)
                    there = grad_prob[:, side * tokens : (side + 1) * tokens]
                    mean = jnp.sum(here * there, axis=-1, keepdims=True)
                    probs.append(here.astype(low))
                    grad_score.append((here * (there - mean)).astype(low))
                probs = jnp.concatenate(probs, axis=1)
                grad_score = jnp.concatenate(grad_score, axis=1)
                r.attended[to, at : at + pair] = dot(probs, values_apart).astype(low)
                grad_query = turned(dot(grad_score, keys_apart) * scale, turns, -1)
                grad_key = turned(together(dot_left(grad_score, queries)) * scale, turns, -1)
                grad_value = together(dot_left(probs, grad_here))
                for kind, grad in enumerate((grad_query, grad_key, grad_value)):
                    r.grad_packed[to, kind * cols + at : kind * cols + at + pair] = grad.astype(low)
            return carry

        lax.fori_loop(0, along, one_bucket, 0)

    for load in loads[:ready]:
        load.wait()
    r.down_send[...] = feed_forward(0).astype(low)
    swap_down.start()
    r.up_send[0] = r.up_whole[:, theirs].astype(low)
    swap_up.start()
    r.up_sum[0] = r.up_whole[:, beside]
    narrow_forward()
    r.down_sum[...] = feed_forward(1)
    r.up_send[1] = r.up_whole[:, theirs].astype(low)
    swap_up_too.start()
    r.up_sum[1] = r.up_whole[:, beside]
    for load in loads[ready:]:
        load.wait()
    for slot in range(last):
        attention(slot)
    relay()

    ends = ((0, r.end_line, sems.end_recv), (1, r.start_line, sems.start_recv))
    for swap, mine, other, board in (
        (swap_end, given.end, r.end_recv, r.end_line),
        (swap_start, given.start, r.start_recv, r.start_line),
    ):
        swap.wait_recv()
        board[line] = (mine[...].astype(jnp.float32) + other[...].astype(jnp.float32)).astype(low)
    for send, board, recv in ends:
        for step in range(1, along):
            along_line(step, board, send, recv).start()

    keep.wait()
    wait_late(3, 2, sems.late_recv.at[0])
    attention(last)
    normed = r.normed[...].reshape(micro * half, width)
    r.qkv_sum[...] = dot_left(normed, r.grad_packed[...]).reshape(r.qkv_sum.shape)
    r.qkv_send[...] = r.qkv_sum[:, theirs].astype(low)
    swap_qkv.start()
    attn = r.attn[...].reshape(micro * half, width)
    r.out_sum[...] = dot_left(r.attended[...], attn).reshape(r.out_sum.shape)
    r.out_send[...] = r.out_sum[theirs].astype(low)
    swap_out.start()

    height, embed = results.table.shape
    group_tokens = r.latent.shape[0] // groups
    logit_scale = embed ** (-0.5)
    base = (lax.axis_index(SECTION) * groups + group) * height
    row = lax.broadcasted_iota(jnp.int32, (r.table.shape[0], group_tokens), 0)

    def one_group(owner, total):
        ints = given.ints[owner]
        ids = jnp.concatenate([ints[slot : slot + 1] for slot in range(micro)], axis=1)
        weight, log_total = [], []
        for slot in range(micro):
            lengths = ints[2 * micro + slot : 2 * micro + slot + 1]
            noised = ints[micro + slot : micro + slot + 1].astype(jnp.float32)
            weight.append(noised * segments(lengths, slots)[2] / (micro * tokens))
            log_total.append(given.log_total[owner, slot][0:1])
        weight, log_total = (jnp.concatenate(rows, axis=1) for rows in (weight, log_total))
        rows = pl.ds(pl.multiple_of(owner * group_tokens, group_tokens), group_tokens)
        latent = r.latent[rows, :]
        logits = dot_right(r.table[...], latent) * logit_scale
        hit = (row == ids - base).astype(jnp.float32)
        grad_logit = (weight * (jnp.exp(logits - log_total) - hit)).astype(low)
        return (
            total
            + dot(grad_logit, latent) * logit_scale
            + dot(hit.astype(low), r.mixed[owner // ACROSS, lax.rem(owner, ACROSS)])
        )

    narrow_settle()
    grad_table = lax.fori_loop(
        0, groups, one_group, jnp.zeros((r.table.shape[0], embed), jnp.float32)
    )
    results.table[...] = grad_table[:height]

    swap_up.wait_recv()
    swap_up_too.wait_recv()
    for side in range(ACROSS):
        index = jnp.where(beside == side, 1, 0)
        both = r.up_sum[index] + r.up_recv[1 - index].astype(jnp.float32)
        r.up_leave[:, :, side * chunk : (side + 1) * chunk] = both.astype(low)
    for step in range(1, along):
        scatter(step, r.up_leave, r.up_arrive, sems.up_send, sems.up_recv).start()

    total = jnp.zeros(given.norm_rows.shape, jnp.float32)
    for source in range(groups):
        total = total + r.norm_rows[source // ACROSS, source % ACROSS]
    count = given.features.shape[0] * given.features.shape[1]
    r.time[0:embed] = dot_left(
        given.features[...].reshape(count, embed), r.seq_rows[...].reshape(count, width)
    )
    r.time[embed : embed + 8] = total
    rows = embed // groups
    results.time[...] = r.time[pl.ds(pl.multiple_of(group * rows, rows), rows), :]
    own_cols = pl.ds(pl.multiple_of(group * (width // groups), width // groups), width // groups)
    results.norms[...] = r.time[embed : embed + 8, own_cols]

    swap_down.wait_recv()
    results.down[...] = r.down_sum[...] + r.down_recv[...].astype(jnp.float32)
    swap_qkv.wait_recv()
    r.qkv_leave[...] = (r.qkv_sum[:, beside] + r.qkv_recv[...].astype(jnp.float32)).astype(low)
    for step in range(1, along):
        scatter(step, r.qkv_leave, r.qkv_arrive, sems.qkv_send, sems.qkv_recv).start()
    swap_out.wait_recv()
    results.out[...] = r.out_sum[beside] + r.out_recv[...].astype(jnp.float32)
    for arrive, leave, recv in (
        (r.up_arrive, r.up_leave, sems.up_recv),
        (r.qkv_arrive, r.qkv_leave, sems.qkv_recv),
    ):
        for source in range(along):

            @pl.when(line == source)
            def _():
                arrive[source] = leave[source]

            @pl.when(line != source)
            def _():
                gathered(source, arrive, recv).wait_recv()

            block = arrive[source].astype(jnp.float32)
            if arrive is r.up_arrive:
                results.up[:, source * quarter : (source + 1) * quarter] = block
            else:
                for kind in range(3):
                    at = kind * width + source * cols
                    results.qkv[:, at : at + cols] = block[:, kind * cols : (kind + 1) * cols]
    for send, board, recv in ends:
        for source in range(along):

            @pl.when(line != source)
            def _():
                gathered(source, board, recv).wait_recv()

    results.end[...] = sum(r.end_line[source].astype(jnp.float32) for source in range(along))
    results.start[...] = sum(r.start_line[source].astype(jnp.float32) for source in range(along))
    wait_late(2, 3, sems.late_send)
    if relayed:
        pl.when(jnp.logical_not(at_end))(relay_copy().wait_send)
    for index, (mine, board) in enumerate(narrow):
        wait_blocks(board.at[pl.ds(0, along), beside], sems.narrow_send.at[index])
        wait_blocks(board.at[pl.ds(0, along - 1), beside], sems.narrow_beside.at[index])
    for swap in swaps:
        swap.wait_send()
    for send, board, recv in ends:
        for step in range(1, along):
            along_line(step, board, send, recv).wait_send()
    for step in range(1, along):
        scatter(step, r.up_leave, r.up_arrive, sems.up_send, sems.up_recv).wait_send()
        scatter(step, r.qkv_leave, r.qkv_arrive, sems.qkv_send, sems.qkv_recv).wait_send()


def run_grads(boards, late, weights, latent, table, given, height, groups, slots):
    f32, low = jnp.float32, jnp.bfloat16
    along, micro, tokens, width = boards[0].shape
    inner = weights[2].shape[1]
    embed = table.shape[1]
    total = along * micro * tokens
    quarter, cols, rows = inner // along, width // along, width // groups
    vmem = pl.BlockSpec(memory_space=pltpu.VMEM)
    anywhere = pl.BlockSpec(memory_space=pl.ANY)
    dma = pltpu.SemaphoreType.DMA
    end, start = given.end.shape, given.start.shape
    parts = Parts(
        *(pltpu.VMEM((micro, along, tokens, width), low) for _ in range(4)),
        qkv=pltpu.VMEM((width, 3 * cols), low),
        out=pltpu.VMEM((cols, width), low),
        up=pltpu.VMEM((ACROSS, width, quarter // ACROSS), low),
        down=pltpu.VMEM((ACROSS, quarter // ACROSS, width), low),
        raw=pltpu.VMEM((along * tokens, 3 * cols), f32),
        grad_att=pltpu.VMEM((along * tokens, cols), low),
        attended=pltpu.VMEM((total, cols), low),
        grad_packed=pltpu.VMEM((total, 3 * cols), low),
        up_whole=pltpu.VMEM((along, ACROSS, rows, quarter // ACROSS), f32),
        up_sum=pltpu.VMEM((ACROSS, along, rows, quarter // ACROSS), f32),
        down_sum=pltpu.VMEM((quarter // ACROSS, width), f32),
        qkv_sum=pltpu.VMEM((along, ACROSS, rows, 3 * cols), f32),
        out_sum=pltpu.VMEM((ACROSS, rows, width), f32),
        up_send=pltpu.VMEM((ACROSS, along, rows, quarter // ACROSS), low),
        up_recv=pltpu.VMEM((ACROSS, along, rows, quarter // ACROSS), low),
        down_send=pltpu.VMEM((quarter // ACROSS, width), low),
        down_recv=pltpu.VMEM((quarter // ACROSS, width), low),
        qkv_send=pltpu.VMEM((along, rows, 3 * cols), low),
        qkv_recv=pltpu.VMEM((along, rows, 3 * cols), low),
        out_send=pltpu.VMEM((rows, width), low),
        out_recv=pltpu.VMEM((rows, width), low),
        up_leave=pltpu.VMEM((along, rows, quarter), low),
        up_arrive=pltpu.VMEM((along, rows, quarter), low),
        qkv_leave=pltpu.VMEM((along, rows, 3 * cols), low),
        qkv_arrive=pltpu.VMEM((along, rows, 3 * cols), low),
        table=pltpu.VMEM(table.shape, low),
        latent=pltpu.VMEM(latent.shape, low),
        mixed=pltpu.VMEM((along, ACROSS, *given.mixed.shape), low),
        norm_rows=pltpu.VMEM((along, ACROSS, *given.norm_rows.shape), f32),
        seq_rows=pltpu.VMEM((along, ACROSS, *given.seq_rows.shape), low),
        end_recv=pltpu.VMEM(end, low),
        start_recv=pltpu.VMEM(start, low),
        end_line=pltpu.VMEM((along, *end), low),
        start_line=pltpu.VMEM((along, *start), low),
        time=pltpu.VMEM((embed + 8, width), f32),
    )
    flags = Flags(
        load=dma((9 + 4 * micro,)),
        keep=dma,
        late_send=dma,
        late_recv=dma((2,)),
        relay=dma,
        narrow_send=dma((3,)),
        narrow_line=dma((3,)),
        narrow_beside=dma((3,)),
        narrow_pair=dma((3,)),
        pair_send=dma((7,)),
        pair_recv=dma((7,)),
        up_send=dma((along,)),
        up_recv=dma((along,)),
        qkv_send=dma((along,)),
        qkv_recv=dma((along,)),
        ends_send=dma((2 * along,)),
        end_recv=dma((along,)),
        start_recv=dma((along,)),
    )
    shapes = Results(
        qkv=(rows, 3 * width),
        out=(rows, width),
        up=(rows, inner),
        down=(inner // groups, width),
        table=(height, embed),
        end=end,
        start=start,
        time=(embed // groups, width),
        norms=(8, rows),
    )
    return Results(
        *pl.pallas_call(
            partial(grads_kernel, groups, slots),
            out_shape=tuple(jax.ShapeDtypeStruct(shape, f32) for shape in shapes),
            in_specs=[anywhere] * HBM_INPUTS + [vmem] * len(given),
            out_specs=(vmem,) * len(shapes),
            scratch_shapes=(*parts, *flags),
            compiler_params=pltpu.CompilerParams(
                collective_id=2, has_side_effects=True, vmem_limit_bytes=VMEM_BYTES
            ),
            cost_estimate=pl.CostEstimate(
                flops=10**11, bytes_accessed=10**8, transcendentals=10**7
            ),
            name="grads",
        )(*boards, late, *weights, latent, table, *given)
    )


def block_of(array, axis, count, index):
    size = array.shape[axis] // count
    return lax.dynamic_slice_in_dim(array, index * size, size, axis)


def rope_lanes(cosine, sine):
    signed = jnp.concatenate([-sine, sine], axis=-1)
    return (jnp.tile(cosine, (1, 1, 4)), jnp.tile(signed, (1, 1, 2)))


def local_grads(held, w_qkv, w_out, w_up, w_down, rope):
    normed, normed_mlp, branch, attn_branch = held
    cosine, sine, same_seq = rope
    buckets, tokens = same_seq.shape[:2]
    width = normed.shape[1]
    head_size = width // HEADS
    scale = head_size ** (-0.5)
    low = jnp.bfloat16
    wide = partial(jnp.einsum, preferred_element_type=jnp.float32)

    pre_act = wide("td,df->tf", normed_mlp, w_up)
    activated, back_gelu = jax.vjp(gelu_exact, pre_act)
    grad_act = wide("td,fd->tf", branch, w_down)
    grad_pre = back_gelu(grad_act)[0].astype(low)

    packed = wide("td,dc->tc", normed, w_qkv).reshape(buckets, tokens, 3, HEADS, head_size)
    turn = jax.vmap(rotate)
    queries = turn(packed[:, :, 0], cosine, sine).astype(low)
    keys = turn(packed[:, :, 1], cosine, sine).astype(low)
    values = packed[:, :, 2].astype(low)
    scores = jnp.where(
        same_seq[:, None], wide("bthd,bshd->bhts", queries, keys) * scale, mask_fill
    )
    probs = jax.nn.softmax(scores, axis=-1)
    attended = wide("bhts,bshd->bthd", probs.astype(low), values).astype(low)
    grad_att = wide("td,cd->tc", attn_branch, w_out).astype(low).reshape(queries.shape)
    grad_prob = wide("bthd,bshd->bhts", grad_att, values)
    inner = jnp.sum(probs * grad_prob, axis=-1, keepdims=True)
    grad_score = (probs * (grad_prob - inner)).astype(low)
    back = jax.vmap(rotate_back)
    grad_query = back(wide("bhts,bshd->bthd", grad_score, keys) * scale, cosine, sine)
    grad_key = back(wide("bhts,bthd->bshd", grad_score, queries) * scale, cosine, sine)
    grad_value = wide("bhts,bthd->bshd", probs.astype(low), grad_att)
    grads = jnp.stack([grad_query, grad_key, grad_value], axis=2).astype(low)
    return (
        wide("td,tc->dc", normed, grads.reshape(normed.shape[0], -1)),
        wide("tc,td->cd", attended.reshape(normed.shape), attn_branch),
        wide("td,tf->df", normed_mlp, grad_pre),
        wide("tf,td->fd", activated.astype(low), branch),
    )


def table_grads(table, latent_all, mixed_all, own, log_all, weight_all):
    logit_scale = table.shape[1] ** (-0.5)
    hit = own[:, None] == jnp.arange(table.shape[0], dtype=jnp.int32)[None, :]
    logits = jnp.dot(latent_all, table.T, preferred_element_type=jnp.float32) * logit_scale
    grad_logit = jnp.exp(logits - log_all[:, None]) - hit.astype(jnp.float32)
    grad_logit = (weight_all[:, None] * grad_logit).astype(jnp.bfloat16)
    head = jnp.dot(grad_logit.T, latent_all, preferred_element_type=jnp.float32) * logit_scale
    return head + jnp.dot(
        hit.astype(jnp.bfloat16).T, mixed_all, preferred_element_type=jnp.float32
    )


def plain_grads(blocks, late, weights, latent_all, table, given, rope, make_layout):
    groups, group = lax.axis_size(DP), lax.axis_index(DP)
    _, micro, tokens, width = blocks[NORMED].shape
    embed = table.shape[1]
    slots = given.seq_rows.shape[0] // micro
    mixed_all = lax.all_gather(given.mixed, DP, axis=0, tiled=True)
    seq_rows = lax.all_gather(given.seq_rows, DP, axis=0, tiled=True)
    ints = given.ints
    line = group // ACROSS
    held = [
        lax.dynamic_index_in_dim(blocks[at], line, 0, keepdims=False)
        for at in (NORMED, MLP, BRANCH, ATTN)
    ]
    held[ATTN] = jnp.concatenate([held[ATTN], late[None]], axis=0)
    sums = local_grads([item.reshape(micro * tokens, width) for item in held], *weights, rope)
    grad_qkv, grad_out, grad_up, grad_down = (
        lax.psum_scatter(
            item.astype(jnp.bfloat16), DP, scatter_dimension=0, tiled=True
        ).astype(jnp.float32)
        for item in sums
    )
    inside = make_layout(
        ints[:, 2 * micro : 3 * micro, :slots].reshape(-1, slots),
        ints[:, 3 * micro : 4 * micro, :slots].reshape(-1, slots),
    )[6]
    noised = ints[:, micro : 2 * micro, :tokens].astype(jnp.float32).reshape(-1)
    first_row = (lax.axis_index(SECTION) * groups + group) * table.shape[0]
    grad_table = table_grads(
        table,
        latent_all,
        mixed_all,
        ints[:, :micro, :tokens].reshape(-1) - first_row,
        given.log_total[:, :, 0].reshape(-1),
        noised * inside.reshape(-1) / (micro * tokens),
    )
    end, start = lax.psum((given.end.astype(jnp.float32), given.start.astype(jnp.float32)), DP)
    features = block_of(given.features.reshape(-1, embed), 1, groups, group)
    grad_time = jnp.dot(features.T, seq_rows, preferred_element_type=jnp.float32)
    norms = block_of(lax.psum(given.norm_rows, DP), 1, groups, group)
    return Results(
        grad_qkv, grad_out, grad_up, grad_down, grad_table, end, start, grad_time, norms
    )


def local(
    token_ids,
    noise,
    noised,
    lengths,
    step_index,
    table,
    in_proj,
    in_bias,
    ln1_gain,
    ln1_bias,
    w_qkv,
    w_out,
    ln2_gain,
    ln2_bias,
    w_up,
    w_down,
    w_time,
    final_gain,
    final_bias,
    out_proj,
):
    sections = lax.axis_size(SECTION)
    groups = lax.axis_size(DP)
    section = lax.axis_index(SECTION)
    group = lax.axis_index(DP)
    micro, tokens = token_ids.shape
    embed, width = in_proj.shape
    head_size = width // HEADS
    total = micro * tokens
    slots = lengths.shape[-1]
    make_layout = jax.vmap(
        partial(
            bucket_layout, tokens=tokens, embed=embed, head_size=head_size, noise_steps=NOISE_STEPS
        )
    )
    layouts = make_layout(lengths[:, 0], step_index[:, 0])

    height = table.shape[0]
    padded = -(-height // LANES) * LANES
    own_rows = jnp.pad(table, ((0, padded - height), (0, 0)))
    lane_fill = ((0, 0), (0, LANES - slots))
    ints = jnp.concatenate(
        [
            token_ids,
            noised,
            jnp.pad(lengths[:, 0], lane_fill),
            jnp.pad(step_index[:, 0], lane_fill),
        ],
        axis=0,
    )
    amount = noised.astype(jnp.float32) * layouts[5]
    shrink = lax.rsqrt(1.0 + amount * amount)

    norms = jnp.concatenate(
        [ln1_gain, ln1_bias, ln2_gain, ln2_bias, final_gain[None], final_bias[None], in_bias[None]],
        axis=0,
    )
    norms = jnp.pad(norms, ((0, 1), (0, 0))).astype(jnp.float32)
    features = layouts[4].astype(jnp.bfloat16)
    per_seq = jnp.einsum(
        "mse,ed->msd",
        features,
        w_time[0],
        preferred_element_type=jnp.float32,
    )
    timed = jnp.einsum("mts,msd->mtd", layouts[0], per_seq, precision=lax.Precision.HIGHEST)
    cosine, sine = rope_lanes(layouts[2], layouts[3])
    mask = jnp.where(layouts[1], 0.0, mask_fill)
    weight = noised.reshape(-1).astype(jnp.float32) * layouts[6].reshape(-1) / total
    column = jnp.arange(ROW_CHUNK, dtype=jnp.int32) % padded
    padding = jnp.broadcast_to(jnp.where(column < height, 0.0, mask_fill), (8, ROW_CHUNK))
    chain = run_chain(
        Sources(own_rows, w_qkv[0], w_out[0], w_up[0], w_down[0]),
        Given(
            ints,
            noise,
            amount.reshape(micro, tokens, 1),
            norms,
            timed,
            cosine,
            sine,
            mask,
            layouts[0].transpose(0, 2, 1),
            features.reshape(micro * slots, embed),
            padding,
            out_proj,
            in_proj,
            weight.reshape(micro, tokens, 1),
            shrink.reshape(micro, tokens, 1),
        ),
        sections,
        groups,
        (height, padded),
    )
    blocks, (end_own, start_own, ints_all, loss, attn_branch, mixed_own, norm_own, seq_own) = chain
    loss_block = block_of(loss[:, 4:5], 2, sections, section)
    latent_all = blocks[LATENT].reshape(-1, embed)
    mixed_own = mixed_own.reshape(total, embed)
    log_all = blocks[LOG_TOTAL].reshape(groups, micro, 8, LANES)
    features_all = blocks[FEATURES].reshape(groups, micro * slots, embed)
    weights = (w_qkv[0], w_out[0], w_up[0], w_down[0])
    lines = groups // ACROSS
    if HEADS % (2 * lines) == 0 and lines * tokens % LANES == 0:
        places = jnp.arange(tokens, dtype=jnp.int32).astype(jnp.float32)
        half_size = head_size // 2
        inverse = rope_base ** (-(jnp.arange(half_size).astype(jnp.float32) * 2.0) / head_size)
        angles = places[:, None] * inverse[None, :]
        turns = jnp.concatenate(rope_lanes(jnp.cos(angles)[None], jnp.sin(angles)[None]), axis=2)[0]
        pieces = []
        for _ in range(3):
            pieces.append(turns.astype(jnp.bfloat16))
            turns = turns - pieces[-1].astype(jnp.float32)
        shares = run_grads(
            [blocks[at] for at in (NORMED, MLP, BRANCH, ATTN)],
            attn_branch,
            weights,
            latent_all,
            own_rows,
            Given2(
                ints_all,
                log_all,
                jnp.concatenate(pieces, axis=1),
                end_own,
                start_own,
                features_all,
                mixed_own,
                norm_own,
                seq_own,
            ),
            height,
            groups,
            slots,
        )
    else:
        shares = plain_grads(
            blocks,
            attn_branch,
            weights,
            latent_all,
            table,
            Given2(
                ints_all,
                log_all,
                None,
                end_own,
                start_own,
                features_all,
                mixed_own,
                norm_own,
                seq_own,
            ),
            (layouts[2], layouts[3], layouts[1]),
            make_layout,
        )
    side = width // sections
    tall = embed // sections
    norm_sums = shares.norms
    start_share, end_share = shares.start, shares.end
    return (
        loss_block,
        shares.table,
        start_share[:tall],
        lax.dynamic_slice_in_dim(start_share[tall], section * side, side),
        norm_sums[0:1],
        norm_sums[1:2],
        shares.qkv[None],
        shares.out[None],
        norm_sums[2:3],
        norm_sums[3:4],
        shares.up[None],
        shares.down[None],
        shares.time[None],
        end_share[side],
        end_share[side + 1],
        end_share[:side],
    )


def solution(mesh):
    placed = (
        P(None, DP),
        P(None, DP, None),
        P(None, DP),
        P(None, DP, None),
        P(None, DP, None),
        P((SECTION, DP), None),
        P(),
        P(),
        P(SECTION, None),
        P(SECTION, None),
        P(SECTION, None, None),
        P(SECTION, None, None),
        P(SECTION, None),
        P(SECTION, None),
        P(SECTION, None, None),
        P(SECTION, None, None),
        P(SECTION, None, None),
        P(),
        P(),
        P(),
    )
    return jax.shard_map(
        local,
        mesh=mesh,
        in_specs=placed,
        out_specs=(
            P(None, DP, SECTION),
            P((SECTION, DP), None),
            P(SECTION, None),
            P(SECTION),
            P(SECTION, DP),
            P(SECTION, DP),
            P(SECTION, DP, None),
            P(SECTION, DP, None),
            P(SECTION, DP),
            P(SECTION, DP),
            P(SECTION, DP, None),
            P(SECTION, DP, None),
            P(SECTION, DP, None),
            P(SECTION),
            P(SECTION),
            P(SECTION, None),
        ),
        check_vma=False,
    )
```

```python
from functools import partial
from typing import Any, NamedTuple

import jax
import jax.numpy as jnp
from jax import lax
from jax.experimental import pallas as pl
from jax.experimental.pallas import tpu as pltpu
from jax.sharding import PartitionSpec as P

HEADS = 16
NOISE_STEPS = 200
SECTION = "section"
DP = "dp"
MESH = pl.DeviceIdType.MESH
VMEM_BYTES = 62 * 1024 * 1024
FF_CHUNK = 512
PACK_CHUNK = 512
ROW_CHUNK = 1024
LANES = 128
ACROSS = 2

norm_eps = 1e-05
mask_fill = -1e30
sigma_low = 1.0
sigma_high = 300.0
rope_base = 10000.0


def layer_norm(values, gain, bias):
    center = values - jnp.mean(values, axis=-1, keepdims=True)
    spread = jnp.mean(center * center, axis=-1, keepdims=True)
    return center * lax.rsqrt(spread + norm_eps) * gain + bias


def gelu_exact(values):
    return jax.nn.gelu(values, approximate=False)


def rotate(vectors, cosine, sine):
    half = vectors.shape[-1] // 2
    first = vectors[..., :half]
    second = vectors[..., half:]
    cos_part = cosine[:, None, :]
    sin_part = sine[:, None, :]
    return jnp.concatenate(
        [first * cos_part - second * sin_part, second * cos_part + first * sin_part], axis=-1
    )


def rotate_back(grads, cosine, sine):
    half = grads.shape[-1] // 2
    first = grads[..., :half]
    second = grads[..., half:]
    cos_part = cosine[:, None, :]
    sin_part = sine[:, None, :]
    return jnp.concatenate(
        [first * cos_part + second * sin_part, second * cos_part - first * sin_part], axis=-1
    )


def bucket_layout(lens, steps, tokens, embed, head_size, noise_steps):
    ends = jnp.cumsum(lens)
    starts = ends - lens
    place = jnp.arange(tokens, dtype=jnp.int32)
    member = (place[:, None] >= starts[None, :]) & (place[:, None] < ends[None, :])
    member_int = member.astype(jnp.int32)
    slots = lens.shape[0]
    inside = jnp.sum(member_int, axis=1)
    segment = (
        jnp.sum(member_int * jnp.arange(slots, dtype=jnp.int32)[None, :], axis=1)
        + (1 - inside) * slots
    )
    offset = jnp.sum(member_int * starts[None, :], axis=1) + (1 - inside) * ends[-1]
    within = (place - offset).astype(jnp.float32)
    membership = member.astype(jnp.float32)
    sigma = sigma_low * (sigma_high / sigma_low) ** (steps.astype(jnp.float32) / (noise_steps - 1))
    level = jnp.sum(membership * sigma[None, :], axis=1)
    half = embed // 2
    rates = 100.0 ** (jnp.arange(half).astype(jnp.float32) / half)
    phase = (jnp.log(sigma) * 0.25)[:, None] * rates[None, :]
    features = jnp.concatenate([jnp.cos(phase), jnp.sin(phase)], axis=1)
    quarter = head_size // 2
    inverse = rope_base ** (-(jnp.arange(quarter).astype(jnp.float32) * 2.0) / head_size)
    angles = within[:, None] * inverse[None, :]
    same_seq = segment[:, None] == segment[None, :]
    return (
        membership,
        same_seq,
        jnp.cos(angles),
        jnp.sin(angles),
        features,
        level,
        inside.astype(jnp.float32),
    )


def embed_input(full_table, token_row, noise_row, noised_row, level):
    rows = full_table[token_row].astype(jnp.float32)
    amount = noised_row.astype(jnp.float32) * level
    shrink = lax.rsqrt(1.0 + amount * amount)
    mixed = (rows + amount[:, None] * noise_row.astype(jnp.float32)) * shrink[:, None]
    return (mixed.astype(jnp.bfloat16), shrink)


def normal(values):
    center = values - jnp.mean(values, axis=-1, keepdims=True)
    spread = jnp.mean(center * center, axis=-1, keepdims=True)
    inverse = lax.rsqrt(spread + norm_eps)
    return (center * inverse, inverse)


def normal_back(grads, gain, unit, inverse):
    scaled = grads * gain
    first = jnp.mean(scaled, axis=-1, keepdims=True)
    second = jnp.mean(scaled * unit, axis=-1, keepdims=True)
    return inverse * (scaled - first - unit * second)


def dot(left, right):
    return lax.dot_general(
        left, right, (((1,), (0,)), ((), ())), preferred_element_type=jnp.float32
    )


def dot_right(left, right):
    return lax.dot_general(
        left, right, (((1,), (1,)), ((), ())), preferred_element_type=jnp.float32
    )


def dot_left(left, right):
    return lax.dot_general(
        left, right, (((0,), (0,)), ((), ())), preferred_element_type=jnp.float32
    )


def halves_swapped(values, head_size, lane):
    half = head_size // 2
    size = values.shape[-1]
    ahead = pltpu.roll(values, size - half, 1)
    behind = pltpu.roll(values, half, 1)
    return jnp.where(lane % head_size < half, ahead, behind)


def apart(pair, lane, head_size):
    zero = jnp.zeros_like(pair)
    return jnp.concatenate(
        [jnp.where(lane < head_size, pair, zero), jnp.where(lane < head_size, zero, pair)], axis=0
    )


NORMED, MLP, BRANCH, ATTN, LATENT, LOG_TOTAL, FEATURES = range(7)
WIDE, PER_SLOT, BLOCKS = 4, 6, 7


class Sources(NamedTuple):
    table: Any
    qkv: Any
    out: Any
    up: Any
    down: Any


class Given(NamedTuple):
    ints: Any
    noise: Any
    amount: Any
    norms: Any
    timed: Any
    cosine: Any
    sine: Any
    mask: Any
    member: Any
    features: Any
    padding: Any
    out_proj: Any
    in_proj: Any
    weight: Any
    shrink: Any


class Kept(NamedTuple):
    table: Any
    qkv: Any
    out: Any
    up: Any
    down: Any
    part: Any
    ints: Any
    rows_parts: Any
    rows: Any
    mixed: Any
    other: Any
    mine: Any
    mine_stats: Any
    arrived: Any
    final: Any
    final_low: Any
    raw: Any
    narrow: Any
    grad_packed: Any
    current: Any
    after: Any
    packed: Any
    probs: Any
    slope: Any
    leaving: Any
    returned: Any
    upstream: Any
    stats: Any
    pulled: Any
    grad_latent: Any
    seq: Any
    mixed_grad: Any
    norm_rows: Any
    seq_rows: Any
    end_rows: Any
    end_parts: Any
    end_own: Any
    start_row: Any
    start_parts: Any
    start_own: Any


class Signals(NamedTuple):
    load: Any
    keep: Any
    out: Any
    line: Any
    beside: Any
    pair: Any
    relay: Any
    ints_send: Any
    ints_recv: Any
    rows_send: Any
    rows_recv: Any
    parts_send: Any
    parts_recv: Any
    table_send: Any
    table_recv: Any
    other_send: Any
    other_recv: Any
    log_send: Any
    log_recv: Any
    on_send: Any
    on_recv: Any
    back_send: Any
    back_recv: Any
    latent_send: Any
    latent_recv: Any
    stats_send: Any
    stats_recv: Any
    pulled_send: Any
    pulled_recv: Any
    end_send: Any
    end_recv: Any
    start_send: Any
    start_recv: Any
    mixed_send: Any
    mixed_recv: Any
    ends: Any


def chain_kernel(sections, groups, heights, *refs):
    refs = iter(refs)
    sources, given = (kind(*(next(refs) for _ in kind._fields)) for kind in (Sources, Given))
    boards = [next(refs) for _ in range(BLOCKS)]
    outs = [next(refs) for _ in range(8)]
    own = [next(refs) for _ in range(BLOCKS)]
    r, sems = (kind(*(next(refs) for _ in kind._fields)) for kind in (Kept, Signals))
    section = lax.axis_index(SECTION)
    group = lax.axis_index(DP)
    last = sections - 1
    along, beside, line = groups // ACROSS, lax.rem(group, ACROSS), group // ACROSS
    partner = line * ACROSS + (1 - beside)
    micro, tokens, width = r.arrived.shape
    inner = r.up.shape[1]
    embed = r.part.shape[2]
    slots = given.member.shape[1]
    height, padded = heights
    head_size = width // HEADS
    scale = head_size ** (-0.5)
    logit_scale = embed ** (-0.5)
    pair = 2 * head_size
    lane = lax.broadcasted_iota(jnp.int32, (tokens, pair), 1)
    low = jnp.bfloat16

    loads = [
        pltpu.make_async_copy(source, target, sems.load.at[index])
        for index, (source, target) in enumerate(
            zip(sources, (r.table, r.qkv, r.out, r.up, r.down))
        )
    ]
    load_table, load_qkv, load_out, load_up, load_down = loads
    for load in (load_table, load_qkv, load_out):
        load.start()

    def section_peer(step):
        return lax.rem(section + step, sections)

    def line_peer(step):
        return lax.rem(line + step, along)

    def group_peer(step):
        return lax.rem(group + step, groups)

    barrier = pltpu.get_barrier_semaphore()
    for step in range(1, sections):
        pl.semaphore_signal(
            barrier, inc=1, device_id={SECTION: section_peer(step)}, device_id_type=MESH
        )
    for step in range(1, groups):
        pl.semaphore_signal(
            barrier, inc=1, device_id={DP: group_peer(step)}, device_id_type=MESH
        )
    for step in range(1, sections):
        pl.semaphore_signal(
            barrier,
            inc=1,
            device_id={SECTION: section_peer(step), DP: partner},
            device_id_type=MESH,
        )
    pl.semaphore_wait(barrier, 2 * sections + groups - 3)

    def sent(source, target, to, send_sem, recv_sem, axis=SECTION):
        return pltpu.make_async_remote_copy(
            src_ref=source,
            dst_ref=target,
            send_sem=send_sem,
            recv_sem=recv_sem,
            device_id={axis: to},
            device_id_type=MESH,
        )

    def place(name, slot):
        board = boards[name]
        if name < PER_SLOT:
            index, mine = name * micro + slot, own[name].at[slot]
        else:
            index, mine = PER_SLOT * micro + name - PER_SLOT, own[name]
        if name < WIDE:
            return index, mine, lambda at: board.at[at, slot]
        if name < PER_SLOT:
            return index, mine, lambda at: board.at[at, beside, slot]
        return index, mine, lambda at: board.at[at, beside]

    relayed = along == 4
    count = PER_SLOT * micro + BLOCKS - PER_SLOT
    early = section < sections // 2
    at_end = (line == 0) | (line == along - 1)

    def slots_of(name):
        if name == ATTN:
            return micro - 1
        return micro if name < PER_SLOT else 1

    def spread(name, slot=0):
        index, mine, at = place(name, slot)
        here = at(line)
        pltpu.make_async_copy(mine, here, sems.keep.at[index]).start()
        for step in range(1, along):
            peer = line_peer(step)
            to = peer * ACROSS + beside
            if name < WIDE and relayed:
                far = (at_end & (jnp.abs(line - peer) == 2)).astype(jnp.int32)

                @pl.when(jnp.abs(line - peer) < 3)
                def _():
                    arrival = sems.line.at[far * count + index]
                    sent(mine, here, to, sems.out.at[index], arrival, DP).start()

            else:
                sent(mine, here, to, sems.out.at[index], sems.line.at[index], DP).start()
        if name >= WIDE:
            sent(mine, here, partner, sems.out.at[index], sems.pair.at[index], DP).start()

    def relay_copy(name, slot):
        index, mine, at = place(name, slot)
        there = at(jnp.where(line == 1, along - 1, 0))
        to = jnp.where(line == 1, 0, along - 1) * ACROSS + beside
        return sent(there, there, to, sems.relay.at[index], sems.line.at[index], DP)

    def relay(name, slot):
        if relayed:
            index, mine, at = place(name, slot)

            @pl.when(jnp.logical_not(at_end))
            def _():
                wait_blocks(at(pl.ds(0, 1)), sems.line.at[count + index])
                relay_copy(name, slot).start()

    def wait_blocks(ref, sem):
        pltpu.make_async_copy(ref, ref, sem).wait()

    def forward(name, slot=0):
        index, mine, at = place(name, slot)
        wait_blocks(at(pl.ds(0, along - 1)), sems.line.at[index])
        for step in range(1, along):
            there = at(line_peer(step))
            sent(there, there, partner, sems.beside.at[index], sems.pair.at[index], DP).start()

    def settle(name, slot=0):
        index, mine, at = place(name, slot)
        pltpu.make_async_copy(mine, at(line), sems.keep.at[index]).wait()
        if name < WIDE and relayed:

            @pl.when(at_end)
            def _():
                wait_blocks(at(pl.ds(0, 2)), sems.out.at[index])
                wait_blocks(at(pl.ds(0, 3)), sems.line.at[index])

            @pl.when(jnp.logical_not(at_end))
            def _():
                wait_blocks(at(pl.ds(0, 3)), sems.out.at[index])
                wait_blocks(at(pl.ds(0, 2)), sems.line.at[index])
                relay_copy(name, slot).wait_send()

        elif name < WIDE:
            wait_blocks(at(pl.ds(0, along - 1)), sems.out.at[index])
            wait_blocks(at(pl.ds(0, along - 1)), sems.line.at[index])
        else:
            wait_blocks(at(pl.ds(0, along)), sems.out.at[index])
            wait_blocks(at(pl.ds(0, along - 1)), sems.beside.at[index])
            wait_blocks(at(pl.ds(0, along)), sems.pair.at[index])

    def passed_on(slot):
        to = jnp.minimum(section + 1, last)
        return sent(
            r.final.at[slot],
            r.arrived.at[slot],
            to,
            sems.on_send.at[slot],
            sems.on_recv.at[slot],
        )

    def passed_back(slot):
        to = jnp.maximum(section - 1, 0)
        return sent(
            r.leaving.at[slot],
            r.returned.at[slot],
            to,
            sems.back_send.at[slot],
            sems.back_recv.at[slot],
        )

    def to_head(source, target, section_to, group_to, send_sem, recv_sem):
        return pltpu.make_async_remote_copy(
            src_ref=source,
            dst_ref=target,
            send_sem=send_sem,
            recv_sem=recv_sem,
            device_id={SECTION: section_to, DP: group_to},
            device_id_type=MESH,
        )

    me = section * ACROSS + beside

    def latent_to(slot, step):
        ref = own[LATENT].at[slot]
        sem = sems.latent_send.at[slot * sections + step]
        return sent(ref, ref, section_peer(step), sem, sems.latent_recv.at[slot])

    def latent_over(slot, step):
        sem = sems.other_send.at[slot * sections + step]
        return to_head(
            own[LATENT].at[slot],
            r.other.at[slot],
            section_peer(step),
            partner,
            sem,
            sems.other_recv.at[slot],
        )

    def shares_to(slot, side):
        to = partner if side else group
        sem = slot * ACROSS + side
        return (
            to_head(
                r.mine.at[side, slot],
                r.pulled.at[me, slot],
                last,
                to,
                sems.pulled_send.at[sem],
                sems.pulled_recv.at[slot * ACROSS * sections + me],
            ),
            to_head(
                r.mine_stats.at[side, slot],
                r.stats.at[me, slot],
                last,
                to,
                sems.stats_send.at[sem],
                sems.stats_recv.at[slot * ACROSS * sections + me],
            ),
        )

    def shares_from(slot, source):
        sem = slot * ACROSS * sections + source
        return tuple(
            to_head(store.at[source, slot], store.at[source, slot], last, partner, send, recv)
            for store, send, recv in (
                (r.pulled, sems.pulled_send.at[slot], sems.pulled_recv.at[sem]),
                (r.stats, sems.stats_send.at[slot], sems.stats_recv.at[sem]),
            )
        )

    def log_to(slot, step):
        ref = own[LOG_TOTAL].at[slot]
        sem = sems.log_send.at[slot * sections + step]
        return sent(ref, ref, section_peer(step), sem, sems.log_recv.at[slot])

    def end_to(step):
        to = section_peer(step)
        return sent(
            r.end_parts.at[to], r.end_own, to, sems.end_send.at[step], sems.end_recv
        )

    def start_to(step):
        to = section_peer(step)
        return sent(
            r.start_parts.at[to], r.start_own, to, sems.start_send.at[step], sems.start_recv
        )

    def mixed_to(slot, step):
        ref = r.mixed_grad.at[slot]
        return sent(
            ref,
            ref,
            section_peer(step),
            sems.mixed_send.at[slot * sections + step],
            sems.mixed_recv.at[slot],
        )

    def ints_to(step):
        ref = r.ints.at[group]
        return sent(
            ref, ref, group_peer(step), sems.ints_send.at[step], sems.ints_recv.at[group], DP
        )

    def ints_from(step):
        source = group_peer(step)
        ref = r.ints.at[source]
        return sent(ref, ref, source, sems.ints_send.at[step], sems.ints_recv.at[source], DP)

    def leaving_rows(peer, stage):
        at = stage * along + peer
        high = r.up.shape[0] // (micro * tokens)
        first = pl.multiple_of(lax.rem(at, high) * (micro * tokens), micro * tokens)
        column = pl.multiple_of(at // high * embed, embed)
        return r.up.at[pl.ds(first, micro * tokens), pl.ds(column, embed)]

    def arriving_rows(peer, stage):
        at = stage * along + peer
        wide = r.down.shape[1] // embed
        first = pl.multiple_of(at // wide * (micro * tokens), micro * tokens)
        column = pl.multiple_of(lax.rem(at, wide) * embed, embed)
        return r.down.at[pl.ds(first, micro * tokens), pl.ds(column, embed)]

    def rows_across(step):
        peer = line_peer(step)
        return sent(
            leaving_rows(peer, 0),
            arriving_rows(peer, 0),
            partner,
            sems.rows_send.at[step],
            sems.rows_recv.at[peer],
            DP,
        )

    def rows_along(step):
        peer = line_peer(step)
        return sent(
            leaving_rows(peer, 1),
            arriving_rows(line, 1),
            peer * ACROSS + beside,
            sems.rows_send.at[along + step],
            sems.rows_recv.at[along + line],
            DP,
        )

    def rows_from(step):
        source = line_peer(step)
        ref = arriving_rows(source, 1)
        sem = along + source
        return sent(ref, ref, partner, sems.rows_send.at[sem], sems.rows_recv.at[sem], DP)

    def parts_to(step):
        ref = r.rows_parts.at[section]
        return sent(
            ref, ref, section_peer(step), sems.parts_send.at[step], sems.parts_recv.at[section]
        )

    def parts_from(step):
        source = section_peer(step)
        ref = r.rows_parts.at[source]
        return sent(ref, ref, source, sems.parts_send.at[step], sems.parts_recv.at[source])

    def table_to(step):
        to = line_peer(step) * ACROSS + beside
        return sent(
            r.table, r.part.at[line], to, sems.table_send.at[step], sems.table_recv.at[line], DP
        )

    def table_settle():
        for step in range(1, along):
            peer = line_peer(step)
            ref = r.part.at[peer]
            sent(
                ref, ref, partner, sems.table_send.at[step], sems.table_recv.at[peer], DP
            ).wait_recv()

    def looked_up(owner):
        ids = r.ints[owner]
        base = (section * groups + group) * height
        column = lax.broadcasted_iota(jnp.int32, (micro * tokens, padded), 1)
        spots = []
        for slot in range(micro):
            wide = jnp.broadcast_to(ids[slot : slot + 1, :tokens], (tokens, tokens))
            spots.append(jnp.transpose(wide.astype(jnp.float32))[:, 0:1])
        at = jnp.concatenate(spots, axis=0).astype(jnp.int32) - base
        at = jnp.where(at < height, at, -1)
        hit = (column == at).astype(jnp.float32).astype(low)
        return dot(hit, r.table[...]).astype(low)

    def front():
        r.ints[group] = given.ints[...]
        for step in range(1, groups):
            ints_to(step).start()
        load_table.wait()
        steps = [*range(1, along), 0]
        for step in range(1, groups):
            ints_from(step).wait_recv()
        for step in steps:
            peer = line_peer(step)
            leaving_rows(peer, 0)[...] = looked_up(peer * ACROSS + (1 - beside))
            rows_across(step).start()
            leaving_rows(peer, 1)[...] = looked_up(peer * ACROSS + beside)
        for step in steps:
            peer = line_peer(step)
            rows_across(step).wait_recv()
            both = leaving_rows(peer, 1)[...].astype(jnp.float32)
            both = both + arriving_rows(peer, 0)[...].astype(jnp.float32)
            if step:
                leaving_rows(peer, 1)[...] = both.astype(low)
                rows_along(step).start()
        total = both
        for step in range(1, along):
            rows_from(step).wait_recv()
            total = total + arriving_rows(line_peer(step), 1)[...].astype(jnp.float32)
        load_down.start()
        r.rows_parts[section] = total.astype(low)
        for step in range(1, sections):
            parts_to(step).start()
        for step in steps:
            rows_across(step).wait_send()
            if step:
                rows_along(step).wait_send()
        load_up.start()
        for step in range(1, along):
            table_to(step).start()
        r.part[line] = r.table[...]
        for step in range(1, sections):
            parts_from(step).wait_recv()
            total = total + r.rows_parts[section_peer(step)].astype(jnp.float32)
        r.rows[...] = total.astype(low).reshape(micro, tokens, embed)

        @pl.when(section == 0)
        def _():
            for slot in range(micro):
                rows = r.rows[slot].astype(jnp.float32)
                mixed = rows + given.amount[slot] * given.noise[slot].astype(jnp.float32)
                mixed = (mixed * given.shrink[slot]).astype(low)
                r.mixed[slot] = mixed
                r.arrived[slot] = dot(mixed, given.in_proj[...]) + given.norms[6:7]

    def layer_on(slot):
        @pl.when(section > 0)
        def _():
            passed_on(slot).wait_recv()

        current = r.arrived[slot] + given.timed[slot]
        r.current[slot] = current
        normed = (normal(current)[0] * given.norms[0:1] + given.norms[1:2]).astype(low)
        own[NORMED][slot] = normed
        if slot == 0:
            load_qkv.wait()
        for at in range(0, 3 * width, PACK_CHUNK):
            r.raw[:, at : at + PACK_CHUNK] = dot(normed, r.qkv[:, at : at + PACK_CHUNK])

        @pl.when(jnp.logical_not(early))
        def _():
            spread(NORMED, slot)

        for at in range(0, width, pair):
            turned = []
            for kind in range(2):
                raw = r.raw[:, kind * width + at : kind * width + at + pair]
                raw = raw * given.cosine[slot] + halves_swapped(raw, head_size, lane) * given.sine[slot]
                raw = raw.astype(low)
                r.packed[slot, :, kind * width + at : kind * width + at + pair] = raw
                turned.append(raw)
            values = r.raw[:, 2 * width + at : 2 * width + at + pair].astype(low)
            r.packed[slot, :, 2 * width + at : 2 * width + at + pair] = values
            scores = dot_right(turned[0], apart(turned[1], lane, head_size)) * scale
            sides = []
            for side in range(2):
                part = scores[:, side * tokens : (side + 1) * tokens] + given.mask[slot]
                raised = jnp.exp(part - jnp.max(part, axis=-1, keepdims=True))
                sides.append(raised / jnp.sum(raised, axis=-1, keepdims=True))
            probs = jnp.concatenate(sides, axis=1)
            r.probs[slot, at // pair] = probs
            r.narrow[:, at : at + pair] = dot(
                probs.astype(low), apart(values, lane, head_size)
            ).astype(low)
        if slot == 0:
            load_out.wait()
        after = current + dot(r.narrow[...], r.out[...])
        r.after[slot] = after
        normed_mlp = (normal(after)[0] * given.norms[2:3] + given.norms[3:4]).astype(low)
        own[MLP][slot] = normed_mlp

        @pl.when(jnp.logical_not(early))
        def _():
            spread(MLP, slot)

        if slot == 0:
            load_up.wait()
            load_down.wait()
        total = after
        for at in range(0, inner, FF_CHUNK):
            pre_act = dot(normed_mlp, r.up[:, at : at + FF_CHUNK])
            below = 0.5 + 0.5 * lax.erf(pre_act * 0.5**0.5)
            bell = jnp.exp(-0.5 * pre_act * pre_act) * (0.5 / jnp.pi) ** 0.5
            r.slope[slot, :, at : at + FF_CHUNK] = below + pre_act * bell
            activated = (pre_act * below).astype(low)
            total = total + dot(activated, r.down[at : at + FF_CHUNK, :])
        r.final[slot] = total

        @pl.when(section < last)
        def _():
            passed_on(slot).start()

        @pl.when(section == last)
        def _():
            final = (normal(total)[0] * given.norms[4:5] + given.norms[5:6]).astype(low)
            r.final_low[slot] = final
            own[LATENT][slot] = dot(final, given.out_proj[...]).astype(low)
            for step in range(sections):
                if step:
                    latent_to(slot, step).start()
                latent_over(slot, step).start()

    def vocabulary(slot):
        @pl.when(section < last)
        def _():
            latent_to(slot, 1).wait_recv()

        latent_over(slot, 1).wait_recv()
        both = jnp.concatenate([own[LATENT][slot], r.other[slot]], axis=0)
        top = jnp.full((ACROSS * tokens, 1), mask_fill, jnp.float32)
        mass = jnp.zeros((ACROSS * tokens, 1), jnp.float32)
        pulled = jnp.zeros((ACROSS * tokens, embed), jnp.float32)
        shards = ROW_CHUNK // padded
        for at in range(0, along, shards):
            rows = r.part[at : at + shards].reshape(ROW_CHUNK, embed)
            logits = dot_right(both, rows) * logit_scale + given.padding[0:1]
            best = jnp.maximum(top, jnp.max(logits, axis=-1, keepdims=True))
            raised = jnp.exp(logits - best)
            fade = jnp.exp(top - best)
            mass = mass * fade + jnp.sum(raised, axis=-1, keepdims=True)
            pulled = pulled * fade + dot(raised.astype(low), rows)
            top = best
        for side in range(ACROSS):
            rows = slice(side * tokens, (side + 1) * tokens)
            r.mine[side, slot] = pulled[rows].astype(low)
            r.mine_stats[side, slot] = jnp.where(lane < LANES // 2, top[rows], mass[rows])
        for copy in shares_to(slot, 1):
            copy.start()

        @pl.when(section < last)
        def _():
            for copy in shares_to(slot, 0):
                copy.start()

    def combine(slot):
        @pl.when(section == last)
        def _():
            sources = [lax.rem(me + step, ACROSS * sections) for step in range(1, ACROSS * sections)]
            for source in sources:
                for copy in shares_from(slot, source):
                    copy.wait_recv()
            stats = [r.mine_stats[0, slot]] + [r.stats[source, slot] for source in sources]
            best = stats[0][:, 0:1]
            for item in stats[1:]:
                best = jnp.maximum(best, item[:, 0:1])
            shares = [jnp.exp(item[:, 0:1] - best) for item in stats]
            total = sum(
                share * item[:, LANES // 2 : LANES // 2 + 1] for share, item in zip(shares, stats)
            )
            pulled = [r.mine[0, slot]] + [r.pulled[source, slot] for source in sources]
            mean = sum(
                share / total * item.astype(jnp.float32) for share, item in zip(shares, pulled)
            )
            row = r.rows[slot].astype(jnp.float32)
            grad_latent = ((mean - row) * (logit_scale * given.weight[slot])).astype(low)
            r.grad_latent[slot] = grad_latent
            grads = dot_right(grad_latent, given.out_proj[...])
            unit, inverse = normal(r.final[slot])
            r.upstream[...] = normal_back(grads, given.norms[4:5], unit, inverse)
            gain = jnp.sum(grads * unit, axis=0, keepdims=True)
            bias = jnp.sum(grads, axis=0, keepdims=True)
            if slot == 0:
                r.end_rows[0:1] = gain
                r.end_rows[1:2] = bias
            else:
                r.end_rows[0:1] += gain
                r.end_rows[1:2] += bias
            log_total = best + jnp.log(total)
            picked = own[LATENT][slot].astype(jnp.float32) * row
            picked = jnp.sum(picked, axis=-1, keepdims=True) * logit_scale
            loss = given.weight[slot] * (log_total - picked)
            turned = jnp.transpose(jnp.where(lane < LANES // 2, log_total, loss))
            own[LOG_TOTAL][slot, 0:4] = turned[0:4]
            own[LOG_TOTAL][slot, 4:8] = turned[LANES // 2 : LANES // 2 + 4]
            for step in range(1, sections):
                log_to(slot, step).start()

        @pl.when(section < last)
        def _():
            passed_back(slot).wait_recv()
            r.upstream[...] = r.returned[slot].astype(jnp.float32)

    def together(rows):
        return jnp.where(lane < head_size, rows[:tokens], rows[tokens:])

    def turned_back(grads, slot):
        return grads * given.cosine[slot] - halves_swapped(grads, head_size, lane) * given.sine[slot]

    def layer_back(slot):
        upstream = r.upstream[...]
        branch = upstream.astype(low)
        own[BRANCH][slot] = branch
        spread(BRANCH, slot)
        grads = jnp.zeros((tokens, width), jnp.float32)
        for at in range(0, inner, FF_CHUNK):
            grad_act = dot_right(branch, r.down[at : at + FF_CHUNK, :])
            grad_pre = (r.slope[slot, :, at : at + FF_CHUNK] * grad_act).astype(low)
            grads = grads + dot_right(grad_pre, r.up[:, at : at + FF_CHUNK])
        unit, inverse = normal(r.after[slot])
        gain_two = jnp.sum(grads * unit, axis=0, keepdims=True)
        bias_two = jnp.sum(grads, axis=0, keepdims=True)
        grad_after = upstream + normal_back(grads, given.norms[2:3], unit, inverse)
        attn_branch = grad_after.astype(low)
        own[ATTN][slot] = attn_branch
        if slot < micro - 1:
            spread(ATTN, slot)
        r.narrow[...] = dot_right(attn_branch, r.out[...]).astype(low)
        for at in range(0, width, pair):
            queries = r.packed[slot, :, at : at + pair]
            keys = r.packed[slot, :, width + at : width + at + pair]
            values = r.packed[slot, :, 2 * width + at : 2 * width + at + pair]
            grad_here = r.narrow[:, at : at + pair]
            probs = r.probs[slot, at // pair]
            grad_prob = dot_right(grad_here, apart(values, lane, head_size))
            sides = []
            for side in range(2):
                here = probs[:, side * tokens : (side + 1) * tokens]
                there = grad_prob[:, side * tokens : (side + 1) * tokens]
                mean = jnp.sum(here * there, axis=-1, keepdims=True)
                sides.append(here * (there - mean))
            grad_score = jnp.concatenate(sides, axis=1).astype(low)
            grad_query = dot(grad_score, apart(keys, lane, head_size)) * scale
            grad_key = together(dot_left(grad_score, queries)) * scale
            grad_value = together(dot_left(probs.astype(low), grad_here))
            for kind, grad in enumerate(
                (turned_back(grad_query, slot), turned_back(grad_key, slot), grad_value)
            ):
                r.grad_packed[:, kind * width + at : kind * width + at + pair] = grad.astype(low)
        grads = jnp.zeros((tokens, width), jnp.float32)
        for at in range(0, 3 * width, PACK_CHUNK):
            grads = grads + dot_right(
                r.grad_packed[:, at : at + PACK_CHUNK], r.qkv[:, at : at + PACK_CHUNK]
            )
        unit, inverse = normal(r.current[slot])
        gain_one = jnp.sum(grads * unit, axis=0, keepdims=True)
        bias_one = jnp.sum(grads, axis=0, keepdims=True)
        grad_current = grad_after + normal_back(grads, given.norms[0:1], unit, inverse)
        leaving = grad_current.astype(low)
        r.leaving[slot] = leaving

        @pl.when(section > 0)
        def _():
            passed_back(slot).start()

        r.seq[slot * slots : (slot + 1) * slots] = lax.dot_general(
            given.member[slot],
            grad_current,
            (((1,), (0,)), ((), ())),
            precision=lax.Precision.HIGHEST,
            preferred_element_type=jnp.float32,
        )
        for index, row in enumerate((gain_one, bias_one, gain_two, bias_two)):
            if slot == 0:
                r.norm_rows[index : index + 1] = row
            else:
                r.norm_rows[index : index + 1] += row

        @pl.when(section == 0)
        def _():
            moved = dot_right(leaving, given.in_proj[...]) * given.shrink[slot]
            r.mixed_grad[slot] = moved.astype(low)
            for step in range(1, sections):
                mixed_to(slot, step).start()
            column = jnp.sum(grad_current, axis=0, keepdims=True)
            if slot == 0:
                r.start_row[...] = column
            else:
                r.start_row[...] += column

    r.norm_rows[...] = jnp.zeros_like(r.norm_rows)
    r.seq[...] = jnp.zeros_like(r.seq)
    r.end_rows[...] = jnp.zeros_like(r.end_rows)
    own[FEATURES][...] = given.features[...]
    front()
    spread(FEATURES)

    layer_on(0)
    for slot in range(1, micro):
        layer_on(slot)

    def spread_all(*names):
        for name in names:
            for slot in range(slots_of(name)):
                spread(name, slot)

    def relay_all(*names):
        for name in names:
            for slot in range(slots_of(name)):
                relay(name, slot)

    @pl.when(early)
    def _():
        spread_all(NORMED, MLP)

    table_settle()
    vocabulary(0)

    @pl.when(section < last)
    def _():
        for slot in range(1, micro):
            vocabulary(slot)

    @pl.when(early)
    def _():
        relay_all(NORMED)

    for slot in range(micro):
        if slot > 0:

            @pl.when(section == last)
            def _():
                vocabulary(slot)

        combine(slot)
        spread(LATENT, slot)

        @pl.when(section < last)
        def _():
            log_to(slot, 1).wait_recv()

        spread(LOG_TOTAL, slot)
        layer_back(slot)
        if slot == 0:

            @pl.when(early)
            def _():
                relay_all(MLP)

    @pl.when(jnp.logical_not(early))
    def _():
        relay_all(NORMED, MLP)

    @pl.when(section == last)
    def _():
        grads = sum(dot_left(r.final_low[slot], r.grad_latent[slot]) for slot in range(micro))
        tall = width // sections
        r.end_parts[...] = jnp.zeros_like(r.end_parts)
        for to in range(sections):
            r.end_parts[to, :tall, :] = grads[to * tall : (to + 1) * tall].astype(low)
            rows = r.end_rows[:, to * tall : (to + 1) * tall]
            r.end_parts[to, tall : tall + 8, :embed] = rows[:, :embed].astype(low)
        for step in range(1, sections):
            end_to(step).start()
        r.end_own[...] = r.end_parts[last]

    @pl.when(section == 0)
    def _():
        grads = sum(dot_left(r.mixed[slot], r.leaving[slot]) for slot in range(micro))
        tall = embed // sections
        r.start_parts[...] = jnp.zeros_like(r.start_parts)
        for to in range(sections):
            r.start_parts[to, :tall, :] = grads[to * tall : (to + 1) * tall].astype(low)
            r.start_parts[to, tall : tall + 8, :] = jnp.broadcast_to(
                r.start_row[...], (8, width)
            ).astype(low)
        for step in range(1, sections):
            start_to(step).start()
        r.start_own[...] = r.start_parts[0]

    r.seq_rows[...] = r.seq[...].astype(low)
    relay_all(BRANCH, ATTN)
    for slot in range(micro):
        forward(LATENT, slot)
        forward(LOG_TOTAL, slot)
    forward(FEATURES)

    @pl.when(section < last)
    def _():
        end_to(1).wait_recv()

    @pl.when(section > 0)
    def _():
        for slot in range(micro):
            mixed_to(slot, 1).wait_recv()
        start_to(1).wait_recv()

    results = (
        r.end_own,
        r.start_own,
        r.ints,
        own[LOG_TOTAL],
        own[ATTN].at[micro - 1],
        r.mixed_grad,
        r.norm_rows,
        r.seq_rows,
    )
    keeps = [
        pltpu.make_async_copy(source, target, sems.ends.at[index])
        for index, (source, target) in enumerate(zip(results, outs))
    ]
    for keep in keeps:
        keep.start()
    for name in range(BLOCKS):
        for slot in range(slots_of(name)):
            settle(name, slot)
    for keep in keeps:
        keep.wait()

    for step in range(1, groups):
        ints_to(step).wait_send()
    for step in range(1, along):
        table_to(step).wait_send()
    for step in range(1, sections):
        parts_to(step).wait_send()
    for slot in range(micro):
        for copy in shares_to(slot, 1):
            copy.wait_send()

        @pl.when(section < last)
        def _():
            passed_on(slot).wait_send()
            for copy in shares_to(slot, 0):
                copy.wait_send()

        @pl.when(section > 0)
        def _():
            passed_back(slot).wait_send()

        @pl.when(section == last)
        def _():
            for step in range(sections):
                if step:
                    latent_to(slot, step).wait_send()
                    log_to(slot, step).wait_send()
                latent_over(slot, step).wait_send()

    @pl.when(section == last)
    def _():
        for step in range(1, sections):
            end_to(step).wait_send()

    @pl.when(section == 0)
    def _():
        for step in range(1, sections):
            for slot in range(micro):
                mixed_to(slot, step).wait_send()
            start_to(step).wait_send()


def run_chain(sources, given, sections, groups, heights):
    f32, low = jnp.float32, jnp.bfloat16
    micro, tokens, width = given.timed.shape
    inner = sources.up.shape[1]
    padded = heights[1]
    embed = given.out_proj.shape[1]
    slots = given.member.shape[1]
    lines = groups // ACROSS
    vmem = pl.BlockSpec(memory_space=pltpu.VMEM)
    anywhere = pl.BlockSpec(memory_space=pl.ANY)
    seq = -(-micro * slots // 16) * 16
    shape = jax.ShapeDtypeStruct
    blocks = (
        shape((micro, tokens, width), low),
        shape((micro, tokens, width), low),
        shape((micro, tokens, width), low),
        shape((micro, tokens, width), low),
        shape((micro, tokens, embed), low),
        shape((micro, 8, LANES), f32),
        shape(given.features.shape, low),
    )
    end = shape((width // sections + 16, embed), low)
    start = shape((embed // sections + 16, width), low)
    dma = pltpu.SemaphoreType.DMA
    count = PER_SLOT * micro + BLOCKS - PER_SLOT
    pairs = micro * sections
    kept = Kept(
        *(pltpu.VMEM(source.shape, low) for source in sources),
        part=pltpu.VMEM((lines, padded, embed), low),
        ints=pltpu.VMEM((groups, *given.ints.shape), jnp.int32),
        rows_parts=pltpu.VMEM((sections, micro * tokens, embed), low),
        rows=pltpu.VMEM((micro, tokens, embed), low),
        mixed=pltpu.VMEM((micro, tokens, embed), low),
        other=pltpu.VMEM((micro, tokens, embed), low),
        mine=pltpu.VMEM((ACROSS, micro, tokens, embed), low),
        mine_stats=pltpu.VMEM((ACROSS, micro, tokens, LANES), f32),
        arrived=pltpu.VMEM((micro, tokens, width), f32),
        final=pltpu.VMEM((micro, tokens, width), f32),
        final_low=pltpu.VMEM((micro, tokens, width), low),
        raw=pltpu.VMEM((tokens, 3 * width), f32),
        narrow=pltpu.VMEM((tokens, width), low),
        grad_packed=pltpu.VMEM((tokens, 3 * width), low),
        current=pltpu.VMEM((micro, tokens, width), f32),
        after=pltpu.VMEM((micro, tokens, width), f32),
        packed=pltpu.VMEM((micro, tokens, 3 * width), low),
        probs=pltpu.VMEM((micro, HEADS // 2, tokens, 2 * tokens), f32),
        slope=pltpu.VMEM((micro, tokens, inner), f32),
        leaving=pltpu.VMEM((micro, tokens, width), low),
        returned=pltpu.VMEM((micro, tokens, width), low),
        upstream=pltpu.VMEM((tokens, width), f32),
        stats=pltpu.VMEM((ACROSS * sections, micro, tokens, LANES), f32),
        pulled=pltpu.VMEM((ACROSS * sections, micro, tokens, embed), low),
        grad_latent=pltpu.VMEM((micro, tokens, embed), low),
        seq=pltpu.VMEM((seq, width), f32),
        mixed_grad=pltpu.VMEM((micro, tokens, embed), low),
        norm_rows=pltpu.VMEM((8, width), f32),
        seq_rows=pltpu.VMEM((seq, width), low),
        end_rows=pltpu.VMEM((8, width), f32),
        end_parts=pltpu.VMEM((sections, *end.shape), low),
        end_own=pltpu.VMEM(end.shape, low),
        start_row=pltpu.VMEM((1, width), f32),
        start_parts=pltpu.VMEM((sections, *start.shape), low),
        start_own=pltpu.VMEM(start.shape, low),
    )
    signals = Signals(
        load=dma((len(sources),)),
        keep=dma((count,)),
        out=dma((count,)),
        line=dma((2 * count,)),
        beside=dma((count,)),
        pair=dma((count,)),
        relay=dma((count,)),
        ints_send=dma((groups,)),
        ints_recv=dma((groups,)),
        rows_send=dma((groups,)),
        rows_recv=dma((groups,)),
        parts_send=dma((sections,)),
        parts_recv=dma((sections,)),
        table_send=dma((lines,)),
        table_recv=dma((lines,)),
        other_send=dma((pairs,)),
        other_recv=dma((micro,)),
        log_send=dma((pairs,)),
        log_recv=dma((micro,)),
        on_send=dma((micro,)),
        on_recv=dma((micro,)),
        back_send=dma((micro,)),
        back_recv=dma((micro,)),
        latent_send=dma((pairs,)),
        latent_recv=dma((micro,)),
        stats_send=dma((micro * ACROSS,)),
        stats_recv=dma((pairs * ACROSS,)),
        pulled_send=dma((micro * ACROSS,)),
        pulled_recv=dma((pairs * ACROSS,)),
        end_send=dma((sections,)),
        end_recv=dma,
        start_send=dma((sections,)),
        start_recv=dma,
        mixed_send=dma((pairs,)),
        mixed_recv=dma((micro,)),
        ends=dma((8,)),
    )
    boards = tuple(
        shape(
            (
                lines,
                *((ACROSS,) if at >= WIDE else ()),
                *((micro - 1, tokens, width) if at == ATTN else block.shape),
            ),
            block.dtype,
        )
        for at, block in enumerate(blocks)
    )
    outs = pl.pallas_call(
        partial(chain_kernel, sections, groups, heights),
        out_shape=(
            *boards,
            end,
            start,
            shape((groups, *given.ints.shape), jnp.int32),
            shape((micro, 8, LANES), f32),
            shape((tokens, width), low),
            shape((micro, tokens, embed), low),
            shape((8, width), f32),
            shape((seq, width), low),
        ),
        in_specs=[anywhere] * len(sources) + [vmem] * len(given),
        out_specs=(anywhere,) * (BLOCKS + 8),
        scratch_shapes=(
            *(pltpu.VMEM(block.shape, block.dtype) for block in blocks),
            *kept,
            *signals,
        ),
        compiler_params=pltpu.CompilerParams(
            collective_id=1, has_side_effects=True, vmem_limit_bytes=VMEM_BYTES
        ),
        cost_estimate=pl.CostEstimate(
            flops=10**11, bytes_accessed=6 * 10**8, transcendentals=10**7
        ),
        name="chain",
    )(*sources, *given)
    return outs[:BLOCKS], outs[BLOCKS:]


class Given2(NamedTuple):
    ints: Any
    log_total: Any
    turns: Any
    end: Any
    start: Any
    features: Any
    mixed: Any
    norm_rows: Any
    seq_rows: Any


class Results(NamedTuple):
    qkv: Any
    out: Any
    up: Any
    down: Any
    table: Any
    proj_in: Any
    bias_in: Any
    proj_out: Any
    gain_end: Any
    bias_end: Any
    time: Any
    gain_one: Any
    bias_one: Any
    gain_two: Any
    bias_two: Any


class Parts(NamedTuple):
    normed: Any
    mlp: Any
    branch: Any
    attn: Any
    qkv: Any
    out: Any
    up: Any
    down: Any
    raw: Any
    grad_att: Any
    attended: Any
    grad_packed: Any
    up_whole: Any
    up_sum: Any
    down_sum: Any
    qkv_sum: Any
    out_sum: Any
    up_send: Any
    up_recv: Any
    down_send: Any
    down_recv: Any
    qkv_send: Any
    qkv_recv: Any
    out_send: Any
    out_recv: Any
    up_leave: Any
    up_arrive: Any
    qkv_leave: Any
    qkv_arrive: Any
    table: Any
    latent: Any
    mixed: Any
    norm_rows: Any
    seq_rows: Any
    end_recv: Any
    start_recv: Any
    end_line: Any
    start_line: Any
    time: Any


class Flags(NamedTuple):
    load: Any
    keep: Any
    late_send: Any
    late_recv: Any
    relay: Any
    narrow_send: Any
    narrow_line: Any
    narrow_beside: Any
    narrow_pair: Any
    pair_send: Any
    pair_recv: Any
    up_send: Any
    up_recv: Any
    qkv_send: Any
    qkv_recv: Any
    ends_send: Any
    end_recv: Any
    start_recv: Any


HBM_INPUTS = 11


def segments(lengths, slots):
    at = lax.broadcasted_iota(jnp.int32, lengths.shape, 1)
    end = lengths[:, 0:1]
    sequence = jnp.zeros_like(at)
    first = jnp.zeros_like(at)
    for slot in range(slots):
        passed = at >= end
        sequence = sequence + passed.astype(jnp.int32)
        first = jnp.where(passed, end, first)
        if slot < slots - 1:
            end = end + lengths[:, slot + 1 : slot + 2]
    return sequence, at - first, (at < end).astype(jnp.float32)


def grads_kernel(groups, slots, *refs):
    refs = iter(refs)
    hbm = [next(refs) for _ in range(HBM_INPUTS)]
    given, results, r, sems = (
        kind(*(next(refs) for _ in kind._fields)) for kind in (Given2, Results, Parts, Flags)
    )
    boards, attn_late, weights, (latent, table) = hbm[:4], hbm[4], hbm[5:9], hbm[9:]
    group = lax.axis_index(DP)
    along, beside, line = groups // ACROSS, lax.rem(group, ACROSS), group // ACROSS
    partner = line * ACROSS + (1 - beside)
    theirs = 1 - beside
    low = jnp.bfloat16
    micro, _, tokens, width = r.normed.shape
    last = micro - 1
    half = along * tokens
    chunk = r.up.shape[2]
    quarter = ACROSS * chunk
    cols = r.out.shape[0]
    head_size = width // HEADS
    scale = head_size ** (-0.5)
    pair = 2 * head_size
    lane = lax.broadcasted_iota(jnp.int32, (tokens, pair), 1)

    def part_of(size):
        return pl.ds(pl.multiple_of(line * size, size), size)

    moves = []
    for index, side in enumerate((theirs, beside)):
        half_cols = pl.ds(pl.multiple_of(line * quarter + side * chunk, chunk), chunk)
        moves.append((weights[2].at[:, half_cols], r.up.at[index]))
        moves.append((weights[3].at[half_cols, :], r.down.at[index]))
    for slot in range(micro):
        moves.append((boards[1].at[:, slot], r.mlp.at[slot]))
        moves.append((boards[2].at[:, slot], r.branch.at[slot]))
    ready = len(moves)
    moves.append((weights[1].at[part_of(cols), :], r.out))
    for kind in range(3):
        from_col = pl.multiple_of(kind * width + line * cols, cols)
        moves.append((weights[0].at[:, pl.ds(from_col, cols)], r.qkv.at[:, pl.ds(kind * cols, cols)]))
    for slot in range(micro):
        moves.append((boards[0].at[:, slot], r.normed.at[slot]))
    for slot in range(last):
        moves.append((boards[3].at[:, slot], r.attn.at[slot]))
    moves += [(latent, r.latent), (table, r.table)]
    loads = [
        pltpu.make_async_copy(source, target, sems.load.at[index])
        for index, (source, target) in enumerate(moves)
    ]
    for load in loads:
        load.start()

    def line_peer(step):
        return lax.rem(line + step, along)

    barrier = pltpu.get_barrier_semaphore()
    for step in range(1, along):
        to = line_peer(step) * ACROSS + beside
        pl.semaphore_signal(barrier, inc=1, device_id={DP: to}, device_id_type=MESH)
    pl.semaphore_signal(barrier, inc=1, device_id={DP: partner}, device_id_type=MESH)
    pl.semaphore_wait(barrier, along)

    def sent(source, target, to, send_sem, recv_sem):
        return pltpu.make_async_remote_copy(
            src_ref=source,
            dst_ref=target,
            send_sem=send_sem,
            recv_sem=recv_sem,
            device_id={DP: to},
            device_id_type=MESH,
        )

    relayed = along == 4
    at_end = (line == 0) | (line == along - 1)
    late = r.attn.at[last]
    keep = pltpu.make_async_copy(attn_late, late.at[line], sems.keep)
    keep.start()
    for step in range(1, along):
        peer = line_peer(step)
        far = 0
        if relayed:
            far = (at_end & (jnp.abs(line - peer) == 2)).astype(jnp.int32)
        copy = sent(
            attn_late,
            late.at[line],
            peer * ACROSS + beside,
            sems.late_send,
            sems.late_recv.at[far],
        )
        if relayed:
            pl.when(jnp.abs(line - peer) < 3)(copy.start)
        else:
            copy.start()

    def wait_blocks(ref, sem):
        pltpu.make_async_copy(ref, ref, sem).wait()

    def wait_late(ends, middle, sem):
        if relayed:

            @pl.when(at_end)
            def _():
                wait_blocks(late.at[pl.ds(0, ends)], sem)

            @pl.when(jnp.logical_not(at_end))
            def _():
                wait_blocks(late.at[pl.ds(0, middle)], sem)

        else:
            wait_blocks(late.at[pl.ds(0, along - 1)], sem)

    def relay_copy():
        there = late.at[jnp.where(line == 1, along - 1, 0)]
        to = jnp.where(line == 1, 0, along - 1) * ACROSS + beside
        return sent(there, there, to, sems.relay, sems.late_recv.at[0])

    def relay():
        if relayed:

            @pl.when(jnp.logical_not(at_end))
            def _():
                wait_blocks(late.at[pl.ds(0, 1)], sems.late_recv.at[1])
                relay_copy().start()

    narrow = ((given.mixed, r.mixed), (given.norm_rows, r.norm_rows), (given.seq_rows, r.seq_rows))
    for index, (mine, board) in enumerate(narrow):
        board[line, beside] = mine[...]
        send, pair_sem = sems.narrow_send.at[index], sems.narrow_pair.at[index]
        here = board.at[line, beside]
        for step in range(1, along):
            to = line_peer(step) * ACROSS + beside
            sent(mine, here, to, send, sems.narrow_line.at[index]).start()
        sent(mine, here, partner, send, pair_sem).start()

    def narrow_forward():
        for index, (mine, board) in enumerate(narrow):
            wait_blocks(board.at[pl.ds(0, along - 1), beside], sems.narrow_line.at[index])
            for step in range(1, along):
                there = board.at[line_peer(step), beside]
                send, pair_sem = sems.narrow_beside.at[index], sems.narrow_pair.at[index]
                sent(there, there, partner, send, pair_sem).start()

    def narrow_settle():
        for index, (mine, board) in enumerate(narrow):
            wait_blocks(board.at[pl.ds(0, along), beside], sems.narrow_pair.at[index])

    swaps = [
        sent(source, target, partner, sems.pair_send.at[index], sems.pair_recv.at[index])
        for index, (source, target) in enumerate(
            (
                (r.down_send, r.down_recv),
                (r.up_send.at[0], r.up_recv.at[0]),
                (r.up_send.at[1], r.up_recv.at[1]),
                (r.qkv_send, r.qkv_recv),
                (r.out_send, r.out_recv),
                (given.end, r.end_recv),
                (given.start, r.start_recv),
            )
        )
    ]
    swap_down, swap_up, swap_up_too, swap_qkv, swap_out, swap_end, swap_start = swaps
    swap_end.start()
    swap_start.start()

    def along_line(step, board, send, recv):
        ref = board.at[line]
        to = line_peer(step) * ACROSS + beside
        return sent(ref, ref, to, sems.ends_send.at[send * along + step], recv.at[line])

    def scatter(step, leave, arrive, send, recv):
        to = line_peer(step)
        return sent(leave.at[to], arrive.at[line], to * ACROSS + beside, send.at[step], recv.at[line])

    def gathered(source, arrive, recv):
        ref = arrive.at[source]
        return sent(ref, ref, partner, recv.at[source], recv.at[source])

    def feed_forward(index):
        normed_mlp = r.mlp[...].reshape(micro * half, width)
        branch = r.branch[...].reshape(micro * half, width)
        pre_act = dot(normed_mlp, r.up[index])
        below = 0.5 + 0.5 * lax.erf(pre_act * 0.5**0.5)
        bell = jnp.exp(-0.5 * pre_act * pre_act) * (0.5 / jnp.pi) ** 0.5
        activated = (pre_act * below).astype(low)
        grad_act = dot_right(branch, r.down[index])
        grad_pre = ((below + pre_act * bell) * grad_act).astype(low)
        grad_up = dot_left(normed_mlp, grad_pre)
        r.up_whole[...] = grad_up.reshape(r.up_whole.shape)
        return dot_left(activated, branch)

    def turned(values, turns, sign):
        swapped = halves_swapped(values, head_size, lane) * turns[1]
        return values * turns[0] + (swapped if sign > 0 else -swapped)

    def together(rows):
        return jnp.where(lane < head_size, rows[:tokens], rows[tokens:])

    def bucket_turns(slot, owner):
        lengths = given.ints[owner, 2 * micro + slot : 2 * micro + slot + 1, :]
        sequence, inside, _ = segments(lengths, slots)
        both = jnp.broadcast_to(sequence * LANES + inside, (tokens, LANES)).astype(jnp.float32)
        column = jnp.transpose(both).astype(jnp.int32)
        mask = jnp.where(column // LANES == sequence, 0.0, mask_fill)
        hit = (column % LANES == lane).astype(jnp.float32).astype(low)
        found = dot(hit, given.turns[...])
        wide = 2 * pair
        found = found[:, :wide] + found[:, wide : 2 * wide] + found[:, 2 * wide :]
        return (found[:, :pair], found[:, pair:]), mask

    def attention(slot):
        normed = r.normed[slot].reshape(half, width)
        for at in range(0, 3 * cols, cols):
            r.raw[:, at : at + cols] = dot(normed, r.qkv[:, at : at + cols])
        r.grad_att[...] = dot_right(r.attn[slot].reshape(half, width), r.out[...]).astype(low)

        def one_bucket(peer, carry):
            turns, mask = bucket_turns(slot, peer * ACROSS + beside)
            rows = pl.ds(pl.multiple_of(peer * tokens, tokens), tokens)
            to = pl.ds(pl.multiple_of((slot * along + peer) * tokens, tokens), tokens)
            for at in range(0, cols, pair):
                queries = turned(r.raw[rows, at : at + pair], turns, 1).astype(low)
                keys = turned(r.raw[rows, cols + at : cols + at + pair], turns, 1).astype(low)
                values = r.raw[rows, 2 * cols + at : 2 * cols + at + pair].astype(low)
                grad_here = r.grad_att[rows, at : at + pair]
                keys_apart = apart(keys, lane, head_size)
                values_apart = apart(values, lane, head_size)
                scores = dot_right(queries, keys_apart) * scale
                grad_prob = dot_right(grad_here, values_apart)
                probs, grad_score = [], []
                for side in range(2):
                    part = scores[:, side * tokens : (side + 1) * tokens] + mask
                    raised = jnp.exp(part - jnp.max(part, axis=-1, keepdims=True))
                    here = raised / jnp.sum(raised, axis=-1, keepdims=True)
                    there = grad_prob[:, side * tokens : (side + 1) * tokens]
                    mean = jnp.sum(here * there, axis=-1, keepdims=True)
                    probs.append(here.astype(low))
                    grad_score.append((here * (there - mean)).astype(low))
                probs = jnp.concatenate(probs, axis=1)
                grad_score = jnp.concatenate(grad_score, axis=1)
                r.attended[to, at : at + pair] = dot(probs, values_apart).astype(low)
                grad_query = turned(dot(grad_score, keys_apart) * scale, turns, -1)
                grad_key = turned(together(dot_left(grad_score, queries)) * scale, turns, -1)
                grad_value = together(dot_left(probs, grad_here))
                for kind, grad in enumerate((grad_query, grad_key, grad_value)):
                    r.grad_packed[to, kind * cols + at : kind * cols + at + pair] = grad.astype(low)
            return carry

        lax.fori_loop(0, along, one_bucket, 0)

    for load in loads[:ready]:
        load.wait()
    r.down_send[...] = feed_forward(0).astype(low)
    swap_down.start()
    r.up_send[0] = r.up_whole[:, theirs].astype(low)
    swap_up.start()
    r.up_sum[0] = r.up_whole[:, beside]
    narrow_forward()
    r.down_sum[...] = feed_forward(1)
    r.up_send[1] = r.up_whole[:, theirs].astype(low)
    swap_up_too.start()
    r.up_sum[1] = r.up_whole[:, beside]
    for load in loads[ready:]:
        load.wait()
    for slot in range(last):
        attention(slot)
    relay()

    ends = ((0, r.end_line, sems.end_recv), (1, r.start_line, sems.start_recv))
    for swap, mine, other, board in (
        (swap_end, given.end, r.end_recv, r.end_line),
        (swap_start, given.start, r.start_recv, r.start_line),
    ):
        swap.wait_recv()
        board[line] = (mine[...].astype(jnp.float32) + other[...].astype(jnp.float32)).astype(low)
    for send, board, recv in ends:
        for step in range(1, along):
            along_line(step, board, send, recv).start()

    keep.wait()
    wait_late(3, 2, sems.late_recv.at[0])
    attention(last)
    normed = r.normed[...].reshape(micro * half, width)
    r.qkv_sum[...] = dot_left(normed, r.grad_packed[...]).reshape(r.qkv_sum.shape)
    r.qkv_send[...] = r.qkv_sum[:, theirs].astype(low)
    swap_qkv.start()
    attn = r.attn[...].reshape(micro * half, width)
    r.out_sum[...] = dot_left(r.attended[...], attn).reshape(r.out_sum.shape)
    r.out_send[...] = r.out_sum[theirs].astype(low)
    swap_out.start()

    height, embed = results.table.shape
    group_tokens = r.latent.shape[0] // groups
    logit_scale = embed ** (-0.5)
    base = (lax.axis_index(SECTION) * groups + group) * height
    row = lax.broadcasted_iota(jnp.int32, (r.table.shape[0], group_tokens), 0)

    def one_group(owner, total):
        ints = given.ints[owner]
        ids = jnp.concatenate([ints[slot : slot + 1] for slot in range(micro)], axis=1)
        weight, log_total = [], []
        for slot in range(micro):
            lengths = ints[2 * micro + slot : 2 * micro + slot + 1]
            noised = ints[micro + slot : micro + slot + 1].astype(jnp.float32)
            weight.append(noised * segments(lengths, slots)[2] / (micro * tokens))
            log_total.append(given.log_total[owner, slot][0:1])
        weight, log_total = (jnp.concatenate(rows, axis=1) for rows in (weight, log_total))
        rows = pl.ds(pl.multiple_of(owner * group_tokens, group_tokens), group_tokens)
        latent = r.latent[rows, :]
        logits = dot_right(r.table[...], latent) * logit_scale
        hit = (row == ids - base).astype(jnp.float32)
        grad_logit = (weight * (jnp.exp(logits - log_total) - hit)).astype(low)
        return (
            total
            + dot(grad_logit, latent) * logit_scale
            + dot(hit.astype(low), r.mixed[owner // ACROSS, lax.rem(owner, ACROSS)])
        )

    narrow_settle()
    grad_table = lax.fori_loop(
        0, groups, one_group, jnp.zeros((r.table.shape[0], embed), jnp.float32)
    )
    results.table[...] = grad_table[:height]

    swap_up.wait_recv()
    swap_up_too.wait_recv()
    for side in range(ACROSS):
        index = jnp.where(beside == side, 1, 0)
        both = r.up_sum[index] + r.up_recv[1 - index].astype(jnp.float32)
        r.up_leave[:, :, side * chunk : (side + 1) * chunk] = both.astype(low)
    for step in range(1, along):
        scatter(step, r.up_leave, r.up_arrive, sems.up_send, sems.up_recv).start()

    total = jnp.zeros(given.norm_rows.shape, jnp.float32)
    for source in range(groups):
        total = total + r.norm_rows[source // ACROSS, source % ACROSS]
    count = given.features.shape[0] * given.features.shape[1]
    r.time[0:embed] = dot_left(
        given.features[...].reshape(count, embed), r.seq_rows[...].reshape(count, width)
    )
    r.time[embed : embed + 8] = total
    rows = embed // groups
    results.time[...] = r.time[pl.ds(pl.multiple_of(group * rows, rows), rows), :]
    own_cols = pl.ds(pl.multiple_of(group * (width // groups), width // groups), width // groups)
    for index, norm in enumerate(
        (results.gain_one, results.bias_one, results.gain_two, results.bias_two)
    ):
        norm[...] = r.time[embed + index : embed + index + 1, own_cols]

    swap_down.wait_recv()
    results.down[...] = r.down_sum[...] + r.down_recv[...].astype(jnp.float32)
    swap_qkv.wait_recv()
    r.qkv_leave[...] = (r.qkv_sum[:, beside] + r.qkv_recv[...].astype(jnp.float32)).astype(low)
    for step in range(1, along):
        scatter(step, r.qkv_leave, r.qkv_arrive, sems.qkv_send, sems.qkv_recv).start()
    swap_out.wait_recv()
    results.out[...] = r.out_sum[beside] + r.out_recv[...].astype(jnp.float32)
    for arrive, leave, recv in (
        (r.up_arrive, r.up_leave, sems.up_recv),
        (r.qkv_arrive, r.qkv_leave, sems.qkv_recv),
    ):
        for source in range(along):

            @pl.when(line == source)
            def _():
                arrive[source] = leave[source]

            @pl.when(line != source)
            def _():
                gathered(source, arrive, recv).wait_recv()

            block = arrive[source].astype(jnp.float32)
            if arrive is r.up_arrive:
                results.up[:, source * quarter : (source + 1) * quarter] = block
            else:
                for kind in range(3):
                    at = kind * width + source * cols
                    results.qkv[:, at : at + cols] = block[:, kind * cols : (kind + 1) * cols]
    for send, board, recv in ends:
        for source in range(along):

            @pl.when(line != source)
            def _():
                gathered(source, board, recv).wait_recv()

    side, tall = given.end.shape[0] - 16, given.start.shape[0] - 16
    total = sum(r.end_line[source].astype(jnp.float32) for source in range(along))
    results.proj_out[...] = total[:side]
    results.gain_end[...] = total[side : side + 1]
    results.bias_end[...] = total[side + 1 : side + 2]
    total = sum(r.start_line[source].astype(jnp.float32) for source in range(along))
    results.proj_in[...] = total[:tall]
    r.time[embed : embed + 8] = total[tall : tall + 8]
    mine = pl.ds(pl.multiple_of(lax.axis_index(SECTION) * side, side), side)
    results.bias_in[...] = r.time[embed : embed + 1, mine]
    wait_late(2, 3, sems.late_send)
    if relayed:
        pl.when(jnp.logical_not(at_end))(relay_copy().wait_send)
    for index, (mine, board) in enumerate(narrow):
        wait_blocks(board.at[pl.ds(0, along), beside], sems.narrow_send.at[index])
        wait_blocks(board.at[pl.ds(0, along - 1), beside], sems.narrow_beside.at[index])
    for swap in swaps:
        swap.wait_send()
    for send, board, recv in ends:
        for step in range(1, along):
            along_line(step, board, send, recv).wait_send()
    for step in range(1, along):
        scatter(step, r.up_leave, r.up_arrive, sems.up_send, sems.up_recv).wait_send()
        scatter(step, r.qkv_leave, r.qkv_arrive, sems.qkv_send, sems.qkv_recv).wait_send()


def run_grads(boards, late, weights, latent, table, given, height, groups, slots):
    f32, low = jnp.float32, jnp.bfloat16
    along, micro, tokens, width = boards[0].shape
    inner = weights[2].shape[1]
    embed = table.shape[1]
    total = along * micro * tokens
    quarter, cols, rows = inner // along, width // along, width // groups
    vmem = pl.BlockSpec(memory_space=pltpu.VMEM)
    anywhere = pl.BlockSpec(memory_space=pl.ANY)
    dma = pltpu.SemaphoreType.DMA
    end, start = given.end.shape, given.start.shape
    parts = Parts(
        *(pltpu.VMEM((micro, along, tokens, width), low) for _ in range(4)),
        qkv=pltpu.VMEM((width, 3 * cols), low),
        out=pltpu.VMEM((cols, width), low),
        up=pltpu.VMEM((ACROSS, width, quarter // ACROSS), low),
        down=pltpu.VMEM((ACROSS, quarter // ACROSS, width), low),
        raw=pltpu.VMEM((along * tokens, 3 * cols), f32),
        grad_att=pltpu.VMEM((along * tokens, cols), low),
        attended=pltpu.VMEM((total, cols), low),
        grad_packed=pltpu.VMEM((total, 3 * cols), low),
        up_whole=pltpu.VMEM((along, ACROSS, rows, quarter // ACROSS), f32),
        up_sum=pltpu.VMEM((ACROSS, along, rows, quarter // ACROSS), f32),
        down_sum=pltpu.VMEM((quarter // ACROSS, width), f32),
        qkv_sum=pltpu.VMEM((along, ACROSS, rows, 3 * cols), f32),
        out_sum=pltpu.VMEM((ACROSS, rows, width), f32),
        up_send=pltpu.VMEM((ACROSS, along, rows, quarter // ACROSS), low),
        up_recv=pltpu.VMEM((ACROSS, along, rows, quarter // ACROSS), low),
        down_send=pltpu.VMEM((quarter // ACROSS, width), low),
        down_recv=pltpu.VMEM((quarter // ACROSS, width), low),
        qkv_send=pltpu.VMEM((along, rows, 3 * cols), low),
        qkv_recv=pltpu.VMEM((along, rows, 3 * cols), low),
        out_send=pltpu.VMEM((rows, width), low),
        out_recv=pltpu.VMEM((rows, width), low),
        up_leave=pltpu.VMEM((along, rows, quarter), low),
        up_arrive=pltpu.VMEM((along, rows, quarter), low),
        qkv_leave=pltpu.VMEM((along, rows, 3 * cols), low),
        qkv_arrive=pltpu.VMEM((along, rows, 3 * cols), low),
        table=pltpu.VMEM(table.shape, low),
        latent=pltpu.VMEM(latent.shape, low),
        mixed=pltpu.VMEM((along, ACROSS, *given.mixed.shape), low),
        norm_rows=pltpu.VMEM((along, ACROSS, *given.norm_rows.shape), f32),
        seq_rows=pltpu.VMEM((along, ACROSS, *given.seq_rows.shape), low),
        end_recv=pltpu.VMEM(end, low),
        start_recv=pltpu.VMEM(start, low),
        end_line=pltpu.VMEM((along, *end), low),
        start_line=pltpu.VMEM((along, *start), low),
        time=pltpu.VMEM((embed + 8, width), f32),
    )
    flags = Flags(
        load=dma((9 + 4 * micro,)),
        keep=dma,
        late_send=dma,
        late_recv=dma((2,)),
        relay=dma,
        narrow_send=dma((3,)),
        narrow_line=dma((3,)),
        narrow_beside=dma((3,)),
        narrow_pair=dma((3,)),
        pair_send=dma((7,)),
        pair_recv=dma((7,)),
        up_send=dma((along,)),
        up_recv=dma((along,)),
        qkv_send=dma((along,)),
        qkv_recv=dma((along,)),
        ends_send=dma((2 * along,)),
        end_recv=dma((along,)),
        start_recv=dma((along,)),
    )
    shapes = Results(
        qkv=(rows, 3 * width),
        out=(rows, width),
        up=(rows, inner),
        down=(inner // groups, width),
        table=(height, embed),
        proj_in=(start[0] - 16, width),
        bias_in=(1, end[0] - 16),
        proj_out=(end[0] - 16, embed),
        gain_end=(1, end[0] - 16),
        bias_end=(1, end[0] - 16),
        time=(embed // groups, width),
        gain_one=(1, rows),
        bias_one=(1, rows),
        gain_two=(1, rows),
        bias_two=(1, rows),
    )
    return Results(
        *pl.pallas_call(
            partial(grads_kernel, groups, slots),
            out_shape=tuple(jax.ShapeDtypeStruct(shape, f32) for shape in shapes),
            in_specs=[anywhere] * HBM_INPUTS + [vmem] * len(given),
            out_specs=(vmem,) * len(shapes),
            scratch_shapes=(*parts, *flags),
            compiler_params=pltpu.CompilerParams(
                collective_id=2, has_side_effects=True, vmem_limit_bytes=VMEM_BYTES
            ),
            cost_estimate=pl.CostEstimate(
                flops=10**11, bytes_accessed=10**8, transcendentals=10**7
            ),
            name="grads",
        )(*boards, late, *weights, latent, table, *given)
    )


def block_of(array, axis, count, index):
    size = array.shape[axis] // count
    return lax.dynamic_slice_in_dim(array, index * size, size, axis)


def rope_lanes(cosine, sine):
    signed = jnp.concatenate([-sine, sine], axis=-1)
    return (jnp.tile(cosine, (1, 1, 4)), jnp.tile(signed, (1, 1, 2)))


def local_grads(held, w_qkv, w_out, w_up, w_down, rope):
    normed, normed_mlp, branch, attn_branch = held
    cosine, sine, same_seq = rope
    buckets, tokens = same_seq.shape[:2]
    width = normed.shape[1]
    head_size = width // HEADS
    scale = head_size ** (-0.5)
    low = jnp.bfloat16
    wide = partial(jnp.einsum, preferred_element_type=jnp.float32)

    pre_act = wide("td,df->tf", normed_mlp, w_up)
    activated, back_gelu = jax.vjp(gelu_exact, pre_act)
    grad_act = wide("td,fd->tf", branch, w_down)
    grad_pre = back_gelu(grad_act)[0].astype(low)

    packed = wide("td,dc->tc", normed, w_qkv).reshape(buckets, tokens, 3, HEADS, head_size)
    turn = jax.vmap(rotate)
    queries = turn(packed[:, :, 0], cosine, sine).astype(low)
    keys = turn(packed[:, :, 1], cosine, sine).astype(low)
    values = packed[:, :, 2].astype(low)
    scores = jnp.where(
        same_seq[:, None], wide("bthd,bshd->bhts", queries, keys) * scale, mask_fill
    )
    probs = jax.nn.softmax(scores, axis=-1)
    attended = wide("bhts,bshd->bthd", probs.astype(low), values).astype(low)
    grad_att = wide("td,cd->tc", attn_branch, w_out).astype(low).reshape(queries.shape)
    grad_prob = wide("bthd,bshd->bhts", grad_att, values)
    inner = jnp.sum(probs * grad_prob, axis=-1, keepdims=True)
    grad_score = (probs * (grad_prob - inner)).astype(low)
    back = jax.vmap(rotate_back)
    grad_query = back(wide("bhts,bshd->bthd", grad_score, keys) * scale, cosine, sine)
    grad_key = back(wide("bhts,bthd->bshd", grad_score, queries) * scale, cosine, sine)
    grad_value = wide("bhts,bthd->bshd", probs.astype(low), grad_att)
    grads = jnp.stack([grad_query, grad_key, grad_value], axis=2).astype(low)
    return (
        wide("td,tc->dc", normed, grads.reshape(normed.shape[0], -1)),
        wide("tc,td->cd", attended.reshape(normed.shape), attn_branch),
        wide("td,tf->df", normed_mlp, grad_pre),
        wide("tf,td->fd", activated.astype(low), branch),
    )


def table_grads(table, latent_all, mixed_all, own, log_all, weight_all):
    logit_scale = table.shape[1] ** (-0.5)
    hit = own[:, None] == jnp.arange(table.shape[0], dtype=jnp.int32)[None, :]
    logits = jnp.dot(latent_all, table.T, preferred_element_type=jnp.float32) * logit_scale
    grad_logit = jnp.exp(logits - log_all[:, None]) - hit.astype(jnp.float32)
    grad_logit = (weight_all[:, None] * grad_logit).astype(jnp.bfloat16)
    head = jnp.dot(grad_logit.T, latent_all, preferred_element_type=jnp.float32) * logit_scale
    return head + jnp.dot(
        hit.astype(jnp.bfloat16).T, mixed_all, preferred_element_type=jnp.float32
    )


def plain_grads(blocks, late, weights, latent_all, table, given, rope, make_layout):
    groups, group = lax.axis_size(DP), lax.axis_index(DP)
    _, micro, tokens, width = blocks[NORMED].shape
    embed = table.shape[1]
    slots = given.seq_rows.shape[0] // micro
    mixed_all = lax.all_gather(given.mixed, DP, axis=0, tiled=True)
    seq_rows = lax.all_gather(given.seq_rows, DP, axis=0, tiled=True)
    ints = given.ints
    line = group // ACROSS
    held = [
        lax.dynamic_index_in_dim(blocks[at], line, 0, keepdims=False)
        for at in (NORMED, MLP, BRANCH, ATTN)
    ]
    held[ATTN] = jnp.concatenate([held[ATTN], late[None]], axis=0)
    sums = local_grads([item.reshape(micro * tokens, width) for item in held], *weights, rope)
    grad_qkv, grad_out, grad_up, grad_down = (
        lax.psum_scatter(
            item.astype(jnp.bfloat16), DP, scatter_dimension=0, tiled=True
        ).astype(jnp.float32)
        for item in sums
    )
    inside = make_layout(
        ints[:, 2 * micro : 3 * micro, :slots].reshape(-1, slots),
        ints[:, 3 * micro : 4 * micro, :slots].reshape(-1, slots),
    )[6]
    noised = ints[:, micro : 2 * micro, :tokens].astype(jnp.float32).reshape(-1)
    first_row = (lax.axis_index(SECTION) * groups + group) * table.shape[0]
    grad_table = table_grads(
        table,
        latent_all,
        mixed_all,
        ints[:, :micro, :tokens].reshape(-1) - first_row,
        given.log_total[:, :, 0].reshape(-1),
        noised * inside.reshape(-1) / (micro * tokens),
    )
    end, start = lax.psum((given.end.astype(jnp.float32), given.start.astype(jnp.float32)), DP)
    features = block_of(given.features.reshape(-1, embed), 1, groups, group)
    grad_time = jnp.dot(features.T, seq_rows, preferred_element_type=jnp.float32)
    norms = block_of(lax.psum(given.norm_rows, DP), 1, groups, group)
    side, tall = end.shape[0] - 16, start.shape[0] - 16
    bias_in = lax.dynamic_slice_in_dim(start[tall:], lax.axis_index(SECTION) * side, side, 1)
    return Results(
        grad_qkv,
        grad_out,
        grad_up,
        grad_down,
        grad_table,
        start[:tall],
        bias_in[:1],
        end[:side],
        end[side : side + 1],
        end[side + 1 : side + 2],
        grad_time,
        *(norms[row : row + 1] for row in range(4)),
    )


def local(
    token_ids,
    noise,
    noised,
    lengths,
    step_index,
    table,
    in_proj,
    in_bias,
    ln1_gain,
    ln1_bias,
    w_qkv,
    w_out,
    ln2_gain,
    ln2_bias,
    w_up,
    w_down,
    w_time,
    final_gain,
    final_bias,
    out_proj,
):
    sections = lax.axis_size(SECTION)
    groups = lax.axis_size(DP)
    section = lax.axis_index(SECTION)
    group = lax.axis_index(DP)
    micro, tokens = token_ids.shape
    embed, width = in_proj.shape
    head_size = width // HEADS
    total = micro * tokens
    slots = lengths.shape[-1]
    make_layout = jax.vmap(
        partial(
            bucket_layout, tokens=tokens, embed=embed, head_size=head_size, noise_steps=NOISE_STEPS
        )
    )
    layouts = make_layout(lengths[:, 0], step_index[:, 0])

    height = table.shape[0]
    padded = -(-height // LANES) * LANES
    own_rows = jnp.pad(table, ((0, padded - height), (0, 0)))
    lane_fill = ((0, 0), (0, LANES - slots))
    ints = jnp.concatenate(
        [
            token_ids,
            noised,
            jnp.pad(lengths[:, 0], lane_fill),
            jnp.pad(step_index[:, 0], lane_fill),
        ],
        axis=0,
    )
    amount = noised.astype(jnp.float32) * layouts[5]
    shrink = lax.rsqrt(1.0 + amount * amount)

    norms = jnp.concatenate(
        [ln1_gain, ln1_bias, ln2_gain, ln2_bias, final_gain[None], final_bias[None], in_bias[None]],
        axis=0,
    )
    norms = jnp.pad(norms, ((0, 1), (0, 0))).astype(jnp.float32)
    features = layouts[4].astype(jnp.bfloat16)
    per_seq = jnp.einsum(
        "mse,ed->msd",
        features,
        w_time[0],
        preferred_element_type=jnp.float32,
    )
    timed = jnp.einsum("mts,msd->mtd", layouts[0], per_seq, precision=lax.Precision.HIGHEST)
    cosine, sine = rope_lanes(layouts[2], layouts[3])
    mask = jnp.where(layouts[1], 0.0, mask_fill)
    weight = noised.reshape(-1).astype(jnp.float32) * layouts[6].reshape(-1) / total
    column = jnp.arange(ROW_CHUNK, dtype=jnp.int32) % padded
    padding = jnp.broadcast_to(jnp.where(column < height, 0.0, mask_fill), (8, ROW_CHUNK))
    chain = run_chain(
        Sources(own_rows, w_qkv[0], w_out[0], w_up[0], w_down[0]),
        Given(
            ints,
            noise,
            amount.reshape(micro, tokens, 1),
            norms,
            timed,
            cosine,
            sine,
            mask,
            layouts[0].transpose(0, 2, 1),
            features.reshape(micro * slots, embed),
            padding,
            out_proj,
            in_proj,
            weight.reshape(micro, tokens, 1),
            shrink.reshape(micro, tokens, 1),
        ),
        sections,
        groups,
        (height, padded),
    )
    blocks, (end_own, start_own, ints_all, loss, attn_branch, mixed_own, norm_own, seq_own) = chain
    loss_block = block_of(loss[:, 4:5], 2, sections, section)
    latent_all = blocks[LATENT].reshape(-1, embed)
    mixed_own = mixed_own.reshape(total, embed)
    log_all = blocks[LOG_TOTAL].reshape(groups, micro, 8, LANES)
    features_all = blocks[FEATURES].reshape(groups, micro * slots, embed)
    weights = (w_qkv[0], w_out[0], w_up[0], w_down[0])
    lines = groups // ACROSS
    if HEADS % (2 * lines) == 0 and lines * tokens % LANES == 0:
        places = jnp.arange(tokens, dtype=jnp.int32).astype(jnp.float32)
        half_size = head_size // 2
        inverse = rope_base ** (-(jnp.arange(half_size).astype(jnp.float32) * 2.0) / head_size)
        angles = places[:, None] * inverse[None, :]
        turns = jnp.concatenate(rope_lanes(jnp.cos(angles)[None], jnp.sin(angles)[None]), axis=2)[0]
        pieces = []
        for _ in range(3):
            pieces.append(turns.astype(jnp.bfloat16))
            turns = turns - pieces[-1].astype(jnp.float32)
        shares = run_grads(
            [blocks[at] for at in (NORMED, MLP, BRANCH, ATTN)],
            attn_branch,
            weights,
            latent_all,
            own_rows,
            Given2(
                ints_all,
                log_all,
                jnp.concatenate(pieces, axis=1),
                end_own,
                start_own,
                features_all,
                mixed_own,
                norm_own,
                seq_own,
            ),
            height,
            groups,
            slots,
        )
    else:
        shares = plain_grads(
            blocks,
            attn_branch,
            weights,
            latent_all,
            table,
            Given2(
                ints_all,
                log_all,
                None,
                end_own,
                start_own,
                features_all,
                mixed_own,
                norm_own,
                seq_own,
            ),
            (layouts[2], layouts[3], layouts[1]),
            make_layout,
        )
    return (
        loss_block,
        shares.table,
        shares.proj_in,
        shares.bias_in[0],
        shares.gain_one,
        shares.bias_one,
        shares.qkv[None],
        shares.out[None],
        shares.gain_two,
        shares.bias_two,
        shares.up[None],
        shares.down[None],
        shares.time[None],
        shares.gain_end[0],
        shares.bias_end[0],
        shares.proj_out,
    )


def solution(mesh):
    placed = (
        P(None, DP),
        P(None, DP, None),
        P(None, DP),
        P(None, DP, None),
        P(None, DP, None),
        P((SECTION, DP), None),
        P(),
        P(),
        P(SECTION, None),
        P(SECTION, None),
        P(SECTION, None, None),
        P(SECTION, None, None),
        P(SECTION, None),
        P(SECTION, None),
        P(SECTION, None, None),
        P(SECTION, None, None),
        P(SECTION, None, None),
        P(),
        P(),
        P(),
    )
    return jax.shard_map(
        local,
        mesh=mesh,
        in_specs=placed,
        out_specs=(
            P(None, DP, SECTION),
            P((SECTION, DP), None),
            P(SECTION, None),
            P(SECTION),
            P(SECTION, DP),
            P(SECTION, DP),
            P(SECTION, DP, None),
            P(SECTION, DP, None),
            P(SECTION, DP),
            P(SECTION, DP),
            P(SECTION, DP, None),
            P(SECTION, DP, None),
            P(SECTION, DP, None),
            P(SECTION),
            P(SECTION),
            P(SECTION, None),
        ),
        check_vma=False,
    )
```
